128 devices in a mesh: strike: 8 (over y, core), normal: 16 (over z, x).
Axes of the slice: x: 4, y: 4, z: 4, core: 2. Of those that a mesh axis runs over, the one named last changes fastest.
Arguments:
- displacement: float32 [3, 64, 256, 512], P(None, 'strike', 'normal'), may hold values from -4 to 4
- body_force: float32 [3, 64, 256, 512], P(None, 'strike', 'normal'), may hold values from -6 to 6
- stiffness: float32 [64, 256, 512], P('strike', 'normal'), may hold values from 0.5 to 4
- aperture_base: float32 [64, 512], P('strike', 'normal'), may hold values from 0.5 to 1.5
- contact_open: int32 [64, 512], P('strike', 'normal'), may hold values 0 or 1
- pressure_init: float32 [64, 512], P('strike', 'normal'), may hold values from -4 to 4
- injection: float32 [64, 512], P('strike', 'normal'), may hold values from -6 to 6
Outputs:
- displacement_out: float32 [3, 64, 256, 512], P(None, 'strike', 'normal')
- pressure_out: float32 [64, 512], P('strike', 'normal')
The draws below stay inside these ranges and needn't reach their ends.
All inputs are finite; a program needn't handle non-finite values. No bound on the sum of `contact_open` on one device may be relied on, other than what follows from the above.
Results may differ from the reference program's by a relative error of at most 0.00002.
Values sent between devices are 32-bit elements; how exact they have to be, the bound alone decides.
A program may use at most 64 MiB of HBM per device.

```python
import math
import jax
import jax.numpy as jnp

DIP = 512
ITERS = 2
SW_E = 4
SW_L = 6
NX = 64
NY = 256


def touch_ends(drawn, rng, smallest, top_value):
    shape = drawn.shape
    index_at = [jax.random.randint(jax.random.fold_in(rng, axis), (), 0, shape[axis]) for axis in range(len(shape))]
    drawn = drawn.at[tuple(index_at)].set(smallest)
    longest = shape.index(max(shape))
    index_at[longest] = (index_at[longest] + 1) % shape[longest]
    return drawn.at[tuple(index_at)].set(top_value)


def levels(rng, extent, pieces, least, high):
    def one(position, blocks):
        draws = jax.random.uniform(jax.random.fold_in(jax.random.fold_in(rng, 6), position), (blocks,), jnp.float32, least / len(pieces), high / len(pieces))
        return jnp.repeat(jnp.exp(draws), extent[position] // blocks).reshape((-1,) + (1,) * (len(extent) - position - 1))

    factor_of = one(*pieces[0])
    for cut in pieces[1:]:
        factor_of = factor_of * one(*cut)
    return factor_of


def centred(key, shape, spread, limit, cuts=(), dtype=jnp.bfloat16):
    loudness = levels(key, shape, cuts, -0.22, 0.18) if cuts else 1.0
    result = jax.random.normal(key, shape, jnp.float32) * spread * loudness
    return jnp.minimum(jnp.maximum(result, -limit), limit).astype(dtype)


def setup_inputs(seed: int = 0) -> dict:
    key_of = jax.random.split(jax.random.key(seed), 8)
    displacement = centred(key_of[0], (3, NX, NY, DIP), 0.5, 4.0, ((1, 8), (2, 16)), jnp.float32)
    body_force = centred(key_of[1], (3, NX, NY, DIP), 1.0, 6.0, ((1, 8), (2, 16)), jnp.float32)
    stiffness = jnp.clip(jnp.exp(math.log(4.0) - 2.0794415 * jax.random.uniform(key_of[2], (NX, NY, DIP), jnp.float32) ** levels(key_of[2], (NX, NY, DIP), ((0, 8), (1, 16)), -0.2, 0.2)), 0.5, 4.0)
    aperture_base = jnp.clip(jnp.exp(math.log(1.5) - 1.0986123 * jax.random.uniform(key_of[3], (NX, DIP), jnp.float32) ** levels(key_of[3], (NX, DIP), ((0, 8), (1, 16)), -0.2, 0.2)), 0.5, 1.5)
    contact_open = touch_ends((jax.random.randint(key_of[4], (NX, DIP), 0, 4) < 3).astype(jnp.int32), jax.random.fold_in(key_of[4], 1), 0, 1)
    pressure_init = centred(key_of[5], (NX, DIP), 0.5, 4.0, ((0, 8), (1, 16)), jnp.float32)
    injection = centred(key_of[6], (NX, DIP), 1.0, 6.0, ((0, 8), (1, 16)), jnp.float32)
    return {"displacement": displacement, "body_force": body_force, "stiffness": stiffness, "aperture_base": aperture_base, "contact_open": contact_open, "pressure_init": pressure_init, "injection": injection}


WEIGHT_TABLE = ((2.0, 1.0, 1.0), (1.0, 2.0, 1.0), (1.0, 1.0, 2.0))
OMEGA = 0.8
TRACTION = 0.5
STORAGE = 0.5


def sweep(u, stiffness, force):
    out = []
    for comp in range(3):
        wx, wy, wz = WEIGHT_TABLE[comp]
        cell = u[comp]
        padded = jnp.pad(cell, 1)
        lap_x = 2.0 * cell - padded[2:, 1:-1, 1:-1] - padded[:-2, 1:-1, 1:-1]
        lap_y = 2.0 * cell - padded[1:-1, 2:, 1:-1] - padded[1:-1, :-2, 1:-1]
        lap_z = 2.0 * cell - padded[1:-1, 1:-1, 2:] - padded[1:-1, 1:-1, :-2]
        applied = stiffness * (wx * lap_x + wy * lap_y + wz * lap_z)
        out.append(cell + OMEGA * (force[comp] - applied) / (8.0 * stiffness))
    return jnp.stack(out)


def relax(pressure, conduct, base):
    p_pad = jnp.pad(pressure, 1)
    k_pad = jnp.pad(conduct, 1)
    numer = jnp.zeros_like(pressure)
    denom = jnp.zeros_like(pressure)
    for sx, sy in ((2, 1), (0, 1), (1, 2), (1, 0)):
        k_near = k_pad[sx:sx + pressure.shape[0], sy:sy + pressure.shape[1]]
        p_near = p_pad[sx:sx + pressure.shape[0], sy:sy + pressure.shape[1]]
        face = 0.5 * (conduct + k_near)
        numer = numer + face * p_near
        denom = denom + face
    return (base + numer) / (STORAGE + denom)


def reference(displacement, body_force, stiffness, aperture_base, contact_open, pressure_init, injection):
    u = displacement
    pressure = pressure_init
    half = NY // 2
    for step in range(ITERS):
        force = body_force.at[1, :, half, :].add(TRACTION * pressure)
        force = force.at[1, :, half - 1, :].add(-(TRACTION * pressure))
        for sweep_count in range(SW_E):
            u = sweep(u, stiffness, force)
        opening = u[1, :, half, :] - u[1, :, half - 1, :]
        width = aperture_base + jax.nn.softplus(opening)
        conduct = contact_open.astype(jnp.float32) * (width * width * width) / 12.0
        base = STORAGE * pressure - opening + injection
        for sweep_count in range(SW_L):
            pressure = relax(pressure, conduct, base)
    return u, pressure
```

```python
import jax
import jax.numpy as jnp
from jax import lax
from jax.experimental import pallas as pl
from jax.experimental.pallas import tpu as pltpu
from jax.sharding import PartitionSpec as P

MESH = pl.DeviceIdType.MESH
F32 = jnp.float32
NS, NN = 8, 16
HS, HN, DIP = 8, 16, 512
SW = 4
SW_L = 6
O = 5
LANES = 128
NJ = DIP // LANES
WAYS = (-1, 1)


def lane_pair(x, lane):
    left, right = [], []
    rl = [pltpu.roll(v, 1, 1) for v in x]
    rr = [pltpu.roll(v, LANES - 1, 1) for v in x]
    for j in range(NJ):
        left.append(jnp.where(lane == 0, rl[j - 1] if j else 0.0, rl[j]))
        right.append(jnp.where(lane == LANES - 1, rr[j + 1] if j < NJ - 1 else 0.0, rr[j]))
    return left, right


def cols(j):
    return slice(j * LANES, (j + 1) * LANES)


def lane_sums(x, first, last):
    width = x.shape[1]
    return (jnp.where(first, 0.0, pltpu.roll(x, 1, 1)), jnp.where(last, 0.0, pltpu.roll(x, width - 1, 1)))


def rows_sums(x):
    count = x.shape[0]
    return pltpu.roll(x, 1, 0), pltpu.roll(x, count - 1, 0)


def kernel(
    u_in, f_in, st_in, ap_in, ct_in, p_in, inj_in,
    u_out, p_out,
    xb, gb, st, outb, rs, rn, sn, rc, sc, pk, gath, plw, qw, r4, r8, row, tt, tx, corr, p1w, p2t, e4s, e4r,
    in_sem, out_sem, s_snd, s_rcv, n_snd, n_rcv, c_snd, c_rcv, g_snd, g_rcv,
    q_snd, q_rcv, w_snd, w_rcv, r4_snd, r4_rcv, r8_snd, r8_rcv, e4_snd, e4_rcv,
):
    s = lax.axis_index("strike")
    n = lax.axis_index("normal")
    is_a = n == NN // 2 - 1
    is_b = n == NN // 2
    is_i = jnp.logical_or(is_a, is_b)
    side = jnp.where(n >= NN // 2, 1, 0)
    has_s = {-1: s > 0, 1: s < NS - 1}
    has_n = {-1: n > 0, 1: n < NN - 1}
    lane = lax.broadcasted_iota(jnp.int32, (8, LANES), 1)
    sub = lax.broadcasted_iota(jnp.int32, (8, LANES), 0)
    sub5 = lax.broadcasted_iota(jnp.int32, (8, DIP), 0)

    order = (1, 0, 2)
    loads = {"st": pltpu.make_async_copy(st_in, st, in_sem.at[6])}
    for c in range(3):
        loads["u", c] = pltpu.make_async_copy(
            u_in.at[c], xb.at[0, c, 0, pl.ds(O, HS), pl.ds(0, HN)], in_sem.at[c]
        )
        loads["f", c] = pltpu.make_async_copy(f_in.at[c], gb.at[c, pl.ds(O, HS)], in_sem.at[3 + c])
    loads["st"].start()
    for c in order:
        loads["f", c].start()
        loads["u", c].start()

    barrier = pltpu.get_barrier_semaphore()
    count = jnp.int32(0)

    def greet(cond, target):
        @pl.when(cond)
        def _():
            pl.semaphore_signal(barrier, inc=1, device_id=target, device_id_type=MESH)

        return jnp.where(cond, 1, 0)

    for a in WAYS:
        count += greet(has_s[a], (s + a, n))
        count += greet(has_n[a], (s, n + a))
        for b in WAYS:
            count += greet(jnp.logical_and(has_s[a], has_n[b]), (s + a, n + b))
    for mid in (NN // 2 - 1, NN // 2):
        count += greet(n != mid, (s, mid))
    for other in range(NN):
        count += greet(jnp.logical_and(is_i, n != other), (s, other))

    def in_range(j):
        return jnp.logical_and(s + (j - 2) >= 0, s + (j - 2) <= NS - 1)

    for j in range(5):
        ok = jnp.logical_and(is_i, in_range(j))
        if j != 2:
            count += greet(ok, (s + (j - 2), n))
        count += greet(ok, (s + (j - 2), NN - 1 - n))

    zrow = jnp.zeros((24, DIP), F32)

    def clear(i, carry):
        for c in range(3):
            for rd in range(2):
                lo = i
                for pp in range(2):
                    xb[rd, c, pp, jnp.where(lo < 4, lo + 1 - pp, lo + 9 + pp)] = zrow
            gb[c, jnp.where(i < 4, i + 1, i + 9)] = jnp.zeros((HN, DIP), F32)
        for c in range(3):
            for rd in range(2):
                xb[rd, c, 0, O + i, pl.ds(16, 8), :] = jnp.zeros((8, DIP), F32)
        return carry

    lax.fori_loop(0, 8, clear, 0)

    for a, w in ((-1, 0), (1, 1)):
        @pl.when(jnp.logical_not(has_s[a]))
        def _():
            rs[:, :, w] = jnp.zeros((2, 3, 4, HN, DIP), F32)

        @pl.when(jnp.logical_not(has_n[a]))
        def _():
            rn[:, :, w] = jnp.zeros((2, 3, 4, 8, DIP), F32)

        for b, v in ((-1, 0), (1, 1)):
            @pl.when(jnp.logical_not(jnp.logical_and(has_s[a], has_n[b])))
            def _():
                rc[:, :, w, v] = jnp.zeros((2, 3, 8, DIP), F32)

    @pl.when(is_i)
    def _():
        tx[...] = jnp.zeros_like(tx)
        for j in range(5):
            @pl.when(jnp.logical_not(in_range(j)))
            def _():
                plw[j] = jnp.zeros((4, 8, DIP), F32)
                qw[:, j] = jnp.zeros((2, 8, DIP), F32)
                r4[:, j] = jnp.zeros((2, 8, DIP), F32)
                if 1 <= j <= 3:
                    r8[:, j - 1] = jnp.zeros((2, 8, DIP), F32)

    pk[...] = jnp.concatenate(
        [p_in[...], ap_in[...], ct_in[...].astype(F32), inj_in[...]], axis=1
    )

    pl.semaphore_wait(barrier, count)

    gathers = []
    for k, mid in enumerate((NN // 2 - 1, NN // 2)):
        gathers.append(
            (
                n != mid,
                pltpu.make_async_remote_copy(
                    src_ref=pk, dst_ref=gath.at[n], send_sem=g_snd.at[k], recv_sem=g_rcv,
                    device_id=(s, mid), device_id_type=MESH,
                ),
            )
        )
    for cond, copy in gathers:
        pl.when(cond)(copy.start)

    loads["st"].wait()

    def recip(i, carry):
        st[i] = 0.1 / st[i]
        return carry

    lax.fori_loop(0, HS, recip, 0)

    @pl.when(is_a)
    def _():
        for i in range(HS):
            qw[0, 2, i : i + 1, :] = 0.5 * st[i, HN - 1 : HN, :]

    @pl.when(is_b)
    def _():
        for i in range(HS):
            qw[0, 2, i : i + 1, :] = 0.5 * st[i, 0:1, :]

    def row_copies(buf, snd, rcv, first, last, src):
        out = []
        for rel in range(2):
            for j in range(first, last):
                if rel == 0 and j == 2:
                    continue
                target_n = n if rel == 0 else NN - 1 - n
                snd_copy = pltpu.make_async_remote_copy(
                    src_ref=src, dst_ref=buf.at[rel, 4 - j - first], send_sem=snd.at[rel, j - first],
                    recv_sem=rcv.at[rel, 4 - j - first], device_id=(s + (j - 2), target_n), device_id_type=MESH,
                )
                rcv_copy = pltpu.make_async_remote_copy(
                    src_ref=src, dst_ref=buf.at[rel, j - first], send_sem=snd.at[rel, j - first],
                    recv_sem=rcv.at[rel, j - first], device_id=(s + (j - 2), target_n), device_id_type=MESH,
                )
                out.append((in_range(j), snd_copy, rcv_copy))
        return out

    q_copies = row_copies(qw, q_snd, q_rcv, 0, 5, qw.at[0, 2])
    r4_copies = row_copies(r4, r4_snd, r4_rcv, 0, 5, r4.at[0, 2])
    r8_copies = row_copies(r8, r8_snd, r8_rcv, 1, 4, r8.at[0, 1])
    w_copies = []
    for j in (0, 1, 3, 4):
        w_copies.append(
            (
                in_range(j),
                pltpu.make_async_remote_copy(
                    src_ref=plw.at[2], dst_ref=plw.at[4 - j], send_sem=w_snd.at[j], recv_sem=w_rcv.at[4 - j],
                    device_id=(s + (j - 2), n), device_id_type=MESH,
                ),
                pltpu.make_async_remote_copy(
                    src_ref=plw.at[2], dst_ref=plw.at[j], send_sem=w_snd.at[j], recv_sem=w_rcv.at[j],
                    device_id=(s + (j - 2), n), device_id_type=MESH,
                ),
            )
        )

    def send_rows(copies):
        for cond, snd, _ in copies:
            pl.when(cond)(snd.start)

    def get_rows(copies):
        for cond, _, rcv in copies:
            pl.when(cond)(rcv.wait_recv)

    def end_rows(copies):
        for cond, snd, _ in copies:
            pl.when(cond)(snd.wait_send)

    @pl.when(is_i)
    def _():
        send_rows(q_copies)

    keep_hi = jnp.logical_or(has_n[1], sub >= 4)
    keep_lo = jnp.logical_or(has_n[-1], sub < 4)
    keep = jnp.logical_and(keep_hi, keep_lo)

    def sweeps(rd, c):
        ax, ay, az = [0.2 if c == k else 0.1 for k in range(3)]

        def sweep(k, carry):
            src = lax.rem(k - 1, 2)
            dst = lax.rem(k, 2)
            lo = jnp.where(has_s[-1], O - k, O)
            hi = jnp.where(has_s[1], O + HS + k, O + HS)

            def one(i, inner):
                x = [[xb[rd, c, src, i, t * 8 : t * 8 + 8, cols(j)] for j in range(NJ)] for t in range(3)]
                up = [[pltpu.roll(v, 1, 0) for v in r] for r in x]
                dn = [[pltpu.roll(v, 7, 0) for v in r] for r in x]
                for t in range(3):
                    left, right = lane_pair(x[t], lane)
                    for j in range(NJ):
                        xm = xb[rd, c, src, i - 1, t * 8 : t * 8 + 8, cols(j)]
                        xp = xb[rd, c, src, i + 1, t * 8 : t * 8 + 8, cols(j)]
                        sy = jnp.where(sub == 0, up[(t + 2) % 3][j], up[t][j]) + jnp.where(
                            sub == 7, dn[(t + 1) % 3][j], dn[t][j]
                        )
                        sx = xm + xp
                        sz = left[j] + right[j]
                        if c == 0:
                            val = 0.2 * (x[t][j] + sx) + 0.1 * (sy + sz)
                        elif c == 1:
                            val = 0.2 * (x[t][j] + sy) + 0.1 * (sx + sz)
                        else:
                            val = 0.2 * (x[t][j] + sz) + 0.1 * (sx + sy)
                        if t < 2:
                            val = val + gb[c, i, t * 8 : t * 8 + 8, cols(j)]
                        else:
                            val = jnp.where(keep, val, 0.0)
                        xb[rd, c, dst, i, t * 8 : t * 8 + 8, cols(j)] = val
                return inner

            lax.fori_loop(lo, hi, one, 0)
            return carry

        lax.fori_loop(1, SW + 1, sweep, 0)

    def messages(rd, c):
        out = []
        for a, w in ((-1, 0), (1, 1)):
            first = 1 if a < 0 else O + HS
            out.append(
                (
                    has_s[a],
                    pltpu.make_async_remote_copy(
                        src_ref=xb.at[rd, c, 0, pl.ds(first, 4), pl.ds(0, HN)], dst_ref=rs.at[rd, c, 1 - w],
                        send_sem=s_snd.at[rd, c, w], recv_sem=s_rcv.at[rd, c, 1 - w],
                        device_id=(s + a, n), device_id_type=MESH,
                    ),
                    pltpu.make_async_remote_copy(
                        src_ref=rs.at[rd, c, w], dst_ref=rs.at[rd, c, w],
                        send_sem=s_snd.at[rd, c, w], recv_sem=s_rcv.at[rd, c, w],
                        device_id=(s + a, n), device_id_type=MESH,
                    ),
                )
            )
        for b, v in ((-1, 0), (1, 1)):
            out.append(
                (
                    has_n[b],
                    pltpu.make_async_remote_copy(
                        src_ref=sn.at[rd, c, v], dst_ref=rn.at[rd, c, 1 - v],
                        send_sem=n_snd.at[rd, c, v], recv_sem=n_rcv.at[rd, c, 1 - v],
                        device_id=(s, n + b), device_id_type=MESH,
                    ),
                    pltpu.make_async_remote_copy(
                        src_ref=sn.at[rd, c, v], dst_ref=rn.at[rd, c, v],
                        send_sem=n_snd.at[rd, c, v], recv_sem=n_rcv.at[rd, c, v],
                        device_id=(s, n + b), device_id_type=MESH,
                    ),
                )
            )
        for a, w in ((-1, 0), (1, 1)):
            for b, v in ((-1, 0), (1, 1)):
                out.append(
                    (
                        jnp.logical_and(has_s[a], has_n[b]),
                        pltpu.make_async_remote_copy(
                            src_ref=sc.at[rd, c, w, v], dst_ref=rc.at[rd, c, 1 - w, 1 - v],
                            send_sem=c_snd.at[rd, c, w, v], recv_sem=c_rcv.at[rd, c, 1 - w, 1 - v],
                            device_id=(s + a, n + b), device_id_type=MESH,
                        ),
                        pltpu.make_async_remote_copy(
                            src_ref=sc.at[rd, c, w, v], dst_ref=rc.at[rd, c, w, v],
                            send_sem=c_snd.at[rd, c, w, v], recv_sem=c_rcv.at[rd, c, w, v],
                            device_id=(s + a, n + b), device_id_type=MESH,
                        ),
                    )
                )
        return out

    msgs = {(rd, c): messages(rd, c) for rd in range(2) for c in range(3)}
    r4sub = sub5 < 4

    def ghost(rd, c, i):
        return xb[rd, c, 0, i, 16:24, :]

    def send(rd, c):
        group = msgs[rd, c]
        for cond, snd, _ in group[:2]:
            pl.when(cond)(snd.start)
        for w in range(2):
            g = [ghost(rd, c, O - d if w == 0 else O + HS - 1 + d) for d in (1, 2, 3)]
            sc[rd, c, w, 1] = jnp.where(
                r4sub, g[0], jnp.where(sub5 < 6, pltpu.roll(g[1], 4, 0), pltpu.roll(g[2], 6, 0))
            )
            sc[rd, c, w, 0] = jnp.where(
                r4sub, jnp.where(sub5 >= 2, pltpu.roll(g[1], 4, 0), pltpu.roll(g[2], 2, 0)), g[0]
            )
        for cond, snd, _ in group[4:]:
            pl.when(cond)(snd.start)
        for t in range(4):
            first, second = ghost(rd, c, O + t), ghost(rd, c, O + t + 4)
            sn[rd, c, 1, t] = jnp.where(r4sub, first, pltpu.roll(second, 4, 0))
            sn[rd, c, 0, t] = jnp.where(r4sub, pltpu.roll(first, 4, 0), second)
        for cond, snd, _ in group[2:4]:
            pl.when(cond)(snd.start)

    def merge(rd, c, store):
        for cond, _, rcv in msgs[rd, c]:
            pl.when(cond)(rcv.wait_recv)
        for i in range(HS):
            t = i % 4
            low = xb[rd, c, 0, O + i, 0:8, :]
            high = xb[rd, c, 0, O + i, 8:16, :]
            way = 0 if i < 4 else 1
            low = low + rs[rd, c, way, t, 0:8, :]
            high = high + rs[rd, c, way, t, 8:16, :]
            from_lo, from_hi = rn[rd, c, 0, t], rn[rd, c, 1, t]
            if i < 4:
                from_hi = pltpu.roll(from_hi, 4, 0)
            else:
                from_lo = pltpu.roll(from_lo, 4, 0)
            low = low + jnp.where(r4sub, from_lo, 0.0)
            high = high + jnp.where(r4sub, 0.0, from_hi)
            d = i + 1 if i < 4 else HS - i
            if d <= 3:
                corner_lo, corner_hi = rc[rd, c, way, 0], rc[rd, c, way, 1]
                if d == 1:
                    low = low + jnp.where(r4sub, corner_lo, 0.0)
                    high = high + jnp.where(r4sub, 0.0, corner_hi)
                elif d == 2:
                    low = low + jnp.where(sub5 < 2, pltpu.roll(corner_lo, 4, 0), 0.0)
                    high = high + jnp.where(sub5 >= 6, pltpu.roll(corner_hi, 4, 0), 0.0)
                else:
                    low = low + jnp.where(sub5 < 2, pltpu.roll(corner_lo, 2, 0), 0.0)
                    high = high + jnp.where(sub5 >= 6, pltpu.roll(corner_hi, 6, 0), 0.0)
            store(i, low, high)

    def traction(p_of, q_of):
        for r in range(-3, HS + 3):
            p_row = p_of(r)
            own = p_row * q_of(0, r)
            far = p_row * q_of(1, r)
            below = jnp.where(is_b, far, own)
            above = jnp.where(is_b, own, far)
            tt[r + 3] = jnp.where(sub5 == 3, -below, jnp.where(sub5 == 4, above, 0.0))

        def tile_sweep(src, dst, lo, hi, shift):
            def one(i, carry):
                x = [src[i, :, cols(j)] for j in range(NJ)]
                left, right = lane_pair(x, lane)
                for j in range(NJ):
                    sy = pltpu.roll(x[j], 1, 0) + pltpu.roll(x[j], 7, 0)
                    sx = src[i - 1, :, cols(j)] + src[i + 1, :, cols(j)]
                    dst[i - shift, :, cols(j)] = (
                        0.2 * (x[j] + sy) + 0.1 * (sx + left[j] + right[j]) + tt[i, :, cols(j)]
                    )
                return carry

            lax.fori_loop(jnp.where(has_s[-1], lo, 3), jnp.where(has_s[1], hi, 11), one, 0)

        tile_sweep(tt, tx.at[0], 1, 13, 0)
        tile_sweep(tx.at[0], tx.at[1], 2, 12, 0)
        tile_sweep(tx.at[1], corr, 3, 11, 3)

    def win_row(ref, r):
        j, i = divmod(r + 16, 8)
        return ref(j)[i : i + 1, :]

    def lubricate(opening, p, ap, ct, inj, first_row):
        rows = opening.shape[0]
        lanes = lax.broadcasted_iota(jnp.int32, (rows, DIP), 1)
        first, last = lanes == 0, lanes == DIP - 1
        strike = lax.broadcasted_iota(jnp.int32, (rows, DIP), 0) + (s * HS + first_row)
        valid = jnp.logical_and(strike >= 0, strike < NS * HS)
        soft = jnp.maximum(opening, 0.0) + jnp.log1p(jnp.exp(-jnp.abs(opening)))
        width = ap + soft
        k = ct * (width * width * width) / 12.0
        base = 0.5 * p - opening + inj
        k_up, k_dn = rows_sums(k)
        k_l, k_r = lane_sums(k, first, last)
        f_up, f_dn, f_l, f_r = [0.5 * (k + v) for v in (k_up, k_dn, k_l, k_r)]
        rden = jnp.where(valid, 1.0 / (0.5 + (f_up + f_dn + f_l + f_r)), 0.0)
        base = base * rden
        f_up, f_dn = f_up * rden, f_dn * rden
        f_l = jnp.where(first, 0.0, f_l * rden)
        f_r = jnp.where(last, 0.0, f_r * rden)
        for _ in range(SW_L):
            p_up, p_dn = rows_sums(p)
            p = base + f_up * p_up + f_dn * p_dn + f_l * pltpu.roll(p, 1, 1) + f_r * pltpu.roll(p, DIP - 1, 1)
        return p

    sign = jnp.where(is_b, 1.0, -1.0)

    for c in order:
        loads["f", c].wait()

        def scale(i, carry, c=c):
            gb[c, O + i] = gb[c, O + i] * st[i]
            return carry

        lax.fori_loop(0, HS, scale, 0)
        loads["u", c].wait()
        sweeps(0, c)
        send(0, c)

    @pl.when(is_i)
    def _():
        gath[n] = pk[...]
        pltpu.make_async_copy(gath.at[pl.ds(0, NN - 1)], gath.at[pl.ds(0, NN - 1)], g_rcv).wait()
        for big in range(NJ):
            tiles = [gath[big * 4 + m] for m in range(4)]
            for kind in range(4):
                val = None
                for m in range(4):
                    shift = (m - kind) % 4 * 32
                    piece = pltpu.roll(tiles[m], shift, 1) if shift else tiles[m]
                    val = piece if val is None else jnp.where(lane >= 32 * m, piece, val)
                plw[2, kind, :, cols(big)] = val
        send_rows(w_copies)
        get_rows(q_copies)
        get_rows(w_copies)
        traction(
            lambda r: win_row(lambda j: plw[j, 0], r), lambda rel, r: win_row(lambda j: qw[rel, j], r)
        )

    def to_second(c):
        def store(i, low, high):
            xb[1, c, 0, O + i, 0:8, :] = low
            xb[1, c, 0, O + i, 8:16, :] = high

        return store

    def to_out(c):
        def store(i, low, high):
            outb[c, i, 0:8, :] = low
            outb[c, i, 8:16, :] = high

        return store

    def own_tile(get, put):
        @pl.when(is_a)
        def _():
            for i in range(HS):
                put(i, 8, get(i, 8) + jnp.where(r4sub, 0.0, pltpu.roll(corr[i], 4, 0)))

        @pl.when(is_b)
        def _():
            for i in range(HS):
                put(i, 0, get(i, 0) + jnp.where(r4sub, pltpu.roll(corr[i], 4, 0), 0.0))

    def put_rows(get, put):
        @pl.when(is_a)
        def _():
            for i in range(HS):
                put(i, get(i, HN - 1))

        @pl.when(is_b)
        def _():
            for i in range(HS):
                put(i, get(i, 0))

    def put_second(i, r, v):
        xb[1, 1, 0, O + i, r : r + 8, :] = v

    def put_out(i, r, v):
        outb[1, i, r : r + 8, :] = v

    def put_r4(i, v):
        r4[0, 2, i : i + 1, :] = v

    def put_r8(i, v):
        r8[0, 1, i : i + 1, :] = v

    for c in order:
        merge(0, c, to_second(c))
        if c == 1:
            own_tile(lambda i, r: xb[1, 1, 0, O + i, r : r + 8, :], put_second)
            put_rows(lambda i, r: xb[1, 1, 0, O + i, r : r + 1, :], put_r4)
            pl.when(is_i)(lambda: send_rows(r4_copies))
        sweeps(1, c)
        send(1, c)

    def flat(x):
        return x.reshape(x.shape[0] * 8, DIP)

    @pl.when(is_i)
    def _():
        get_rows(r4_copies)
        opening = sign * (flat(r4[0]) - flat(r4[1]))
        p1 = lubricate(opening, *[flat(plw[:, kind]) for kind in range(4)], -16)
        p1w[...] = p1.reshape(5, 8, DIP)
        traction(
            lambda r: win_row(lambda j: p1w[j], r), lambda rel, r: win_row(lambda j: qw[rel, j], r)
        )

    copies_out = [pltpu.make_async_copy(outb.at[c], u_out.at[c], out_sem.at[c]) for c in range(3)]
    for c in order:
        merge(1, c, to_out(c))
        if c == 1:
            put_rows(lambda i, r: outb[1, i, r : r + 1, :], put_r8)
            pl.when(is_i)(lambda: send_rows(r8_copies))
            own_tile(lambda i, r: outb[1, i, r : r + 8, :], put_out)
        copies_out[c].start()

    e4_copies = []
    for i in range(NN // 2):
        e4_copies.append(
            (
                jnp.logical_and(is_i, n != side * 8 + i),
                pltpu.make_async_remote_copy(
                    src_ref=e4s.at[i], dst_ref=e4r, send_sem=e4_snd.at[i], recv_sem=e4_rcv,
                    device_id=(s, side * 8 + i), device_id_type=MESH,
                ),
            )
        )

    @pl.when(is_i)
    def _():
        lanes = lax.broadcasted_iota(jnp.int32, (40, DIP), 1)
        first, last = lanes == 0, lanes == DIP - 1
        strike = lax.broadcasted_iota(jnp.int32, (40, DIP), 0) + (s * HS - 16)
        valid = jnp.logical_and(strike >= 0, strike < NS * HS)

        def across(x):
            up, dn = rows_sums(x)
            left, right = lane_sums(x, first, last)
            return 0.1 * ((up + dn) + (left + right))

        force = flat(p1w[...]) * (flat(qw[0]) + flat(qw[1]))
        d0 = jnp.where(valid, across(force) + force, 0.0)
        d1 = 0.2 * force
        e0 = jnp.where(valid, 0.2 * d1 + across(d0) + force, 0.0)
        e1 = jnp.where(valid, 0.2 * d1 + across(d1) + 0.2 * d0, 0.0)
        extra = (0.2 * e1 + across(e0) + force)[8:32]
        get_rows(r8_copies)
        opening = sign * (flat(r8[0]) - flat(r8[1])) + extra
        p2 = lubricate(
            opening, flat(p1w[1:4]), flat(plw[1:4, 1]), flat(plw[1:4, 2]), flat(plw[1:4, 3]), -8
        )
        for j in range(NJ):
            p2t[j] = p2[8:16, cols(j)]
        for i in range(NN // 2):
            shift = -(i % 4) * 32 % LANES
            tile = p2t[side * 2 + i // 4]
            e4s[i] = pltpu.roll(tile, shift, 1) if shift else tile
        for cond, copy in e4_copies:
            pl.when(cond)(copy.start)
        e4r[...] = e4s[jnp.where(is_b, 0, 7)]

    @pl.when(jnp.logical_not(is_i))
    def _():
        pltpu.make_async_remote_copy(
            src_ref=e4s.at[0], dst_ref=e4r, send_sem=e4_snd.at[0], recv_sem=e4_rcv,
            device_id=(s, NN - 1 - n), device_id_type=MESH,
        ).wait_recv()

    p_out[...] = e4r[:, 0:32]

    for copy in copies_out:
        copy.wait()
    for group in msgs.values():
        for cond, snd, _ in group:
            pl.when(cond)(snd.wait_send)
    for cond, copy in gathers:
        pl.when(cond)(copy.wait_send)
    for cond, copy in e4_copies:
        pl.when(cond)(copy.wait_send)

    @pl.when(is_i)
    def _():
        for copies in (q_copies, w_copies, r4_copies, r8_copies):
            end_rows(copies)


def body(displacement, body_force, stiffness, aperture_base, contact_open, pressure_init, injection):
    vm = pl.BlockSpec(memory_space=pltpu.VMEM)
    hbm = pl.BlockSpec(memory_space=pl.ANY)
    dma = pltpu.SemaphoreType.DMA

    def buf(*shape):
        return pltpu.VMEM(shape, F32)

    scratch = [
        buf(2, 3, 2, 18, 24, DIP),
        buf(3, 18, HN, DIP),
        buf(HS, HN, DIP),
        buf(3, HS, HN, DIP),
        buf(2, 3, 2, 4, HN, DIP),
        buf(2, 3, 2, 4, 8, DIP),
        buf(2, 3, 2, 4, 8, DIP),
        buf(2, 3, 2, 2, 8, DIP),
        buf(2, 3, 2, 2, 8, DIP),
        buf(8, LANES),
        buf(NN, 8, LANES),
        buf(5, 4, 8, DIP),
        buf(2, 5, 8, DIP),
        buf(2, 5, 8, DIP),
        buf(2, 3, 8, DIP),
        buf(8, DIP),
        buf(14, 8, DIP),
        buf(2, 14, 8, DIP),
        buf(HS, 8, DIP),
        buf(5, 8, DIP),
        buf(NJ, 8, LANES),
        buf(NN // 2, 8, LANES),
        buf(8, LANES),
        dma((7,)), dma((3,)),
        dma((2, 3, 2)), dma((2, 3, 2)), dma((2, 3, 2)), dma((2, 3, 2)),
        dma((2, 3, 2, 2)), dma((2, 3, 2, 2)),
        dma((2,)), dma,
        dma((2, 5)), dma((2, 5)), dma((5,)), dma((5,)), dma((2, 5)), dma((2, 5)), dma((2, 3)), dma((2, 3)),
        dma((NN // 2,)), dma,
    ]
    return pl.pallas_call(
        kernel,
        out_shape=(
            jax.ShapeDtypeStruct((3, HS, HN, DIP), F32),
            jax.ShapeDtypeStruct((8, 32), F32),
        ),
        in_specs=[hbm, hbm, hbm, vm, vm, vm, vm],
        out_specs=(hbm, vm),
        scratch_shapes=scratch,
        compiler_params=pltpu.CompilerParams(
            collective_id=0, has_side_effects=True, vmem_limit_bytes=48 * 2**20
        ),
        cost_estimate=pl.CostEstimate(flops=60_000_000, bytes_accessed=2_700_000, transcendentals=40_000),
    )(displacement, body_force, stiffness, aperture_base, contact_open, pressure_init, injection)


def solution(mesh):
    in_specs = (
        P(None, "strike", "normal", None),
        P(None, "strike", "normal", None),
        P("strike", "normal", None),
        P("strike", "normal"),
        P("strike", "normal"),
        P("strike", "normal"),
        P("strike", "normal"),
    )
    out_specs = (P(None, "strike", "normal", None), P("strike", "normal"))
    return jax.shard_map(body, mesh=mesh, in_specs=in_specs, out_specs=out_specs, check_vma=False)
```

```python
import jax
import jax.numpy as jnp
from jax import lax
from jax.experimental import pallas as pl
from jax.experimental.pallas import tpu as pltpu
from jax.sharding import PartitionSpec as P

MESH = pl.DeviceIdType.MESH
F32 = jnp.float32
NS, NN = 8, 16
HS, HN, DIP = 8, 16, 512
SW = 4
SW_L = 6
O = 5
LANES = 128
NJ = DIP // LANES
WAYS = (-1, 1)


def lane_pair(x, lane):
    left, right = [], []
    rl = [pltpu.roll(v, 1, 1) for v in x]
    rr = [pltpu.roll(v, LANES - 1, 1) for v in x]
    for j in range(NJ):
        left.append(jnp.where(lane == 0, rl[j - 1] if j else 0.0, rl[j]))
        right.append(jnp.where(lane == LANES - 1, rr[j + 1] if j < NJ - 1 else 0.0, rr[j]))
    return left, right


def cols(j):
    return slice(j * LANES, (j + 1) * LANES)


def lane_sums(x, first, last):
    width = x.shape[1]
    return (jnp.where(first, 0.0, pltpu.roll(x, 1, 1)), jnp.where(last, 0.0, pltpu.roll(x, width - 1, 1)))


def rows_sums(x):
    count = x.shape[0]
    return pltpu.roll(x, 1, 0), pltpu.roll(x, count - 1, 0)


def kernel(
    u_in, f_in, st_in, ap_hbm, ct_hbm, p_hbm, inj_hbm,
    u_out, p_out,
    xb, gb, st, outb, rs, rn, sn, rc, sc, pk, gath, plw, qw, r4, r8, small, ct_v, tt, tx, corr, p1w, p2t, e4s, e4r,
    in_sem, out_sem, s_snd, s_rcv, n_snd, n_rcv, c_snd, c_rcv, g_snd, g_rcv,
    q_snd, q_rcv, w_snd, w_rcv, r4_snd, r4_rcv, r8_snd, r8_rcv, e4_snd, e4_rcv,
):
    s = lax.axis_index("strike")
    n = lax.axis_index("normal")
    is_a = n == NN // 2 - 1
    is_b = n == NN // 2
    is_i = jnp.logical_or(is_a, is_b)
    side = jnp.where(n >= NN // 2, 1, 0)
    has_s = {-1: s > 0, 1: s < NS - 1}
    has_n = {-1: n > 0, 1: n < NN - 1}
    lane = lax.broadcasted_iota(jnp.int32, (8, LANES), 1)
    sub = lax.broadcasted_iota(jnp.int32, (8, LANES), 0)
    sub5 = lax.broadcasted_iota(jnp.int32, (8, DIP), 0)

    order = (1, 0, 2)
    loads = {"st": pltpu.make_async_copy(st_in, st, in_sem.at[6])}
    for c in range(3):
        loads["u", c] = pltpu.make_async_copy(
            u_in.at[c], xb.at[0, c, 0, pl.ds(O, HS), pl.ds(0, HN)], in_sem.at[c]
        )
        loads["f", c] = pltpu.make_async_copy(f_in.at[c], gb.at[c, pl.ds(O, HS)], in_sem.at[3 + c])
    for k, ref in enumerate((p_hbm, ap_hbm, inj_hbm)):
        loads["small", k] = pltpu.make_async_copy(ref, small.at[k], in_sem.at[7 + k])
        loads["small", k].start()
    loads["ct"] = pltpu.make_async_copy(ct_hbm, ct_v, in_sem.at[10])
    loads["ct"].start()
    loads["st"].start()
    for c in order:
        loads["f", c].start()
        loads["u", c].start()

    barrier = pltpu.get_barrier_semaphore()
    count = jnp.int32(0)

    def greet(cond, target):
        @pl.when(cond)
        def _():
            pl.semaphore_signal(barrier, inc=1, device_id=target, device_id_type=MESH)

        return jnp.where(cond, 1, 0)

    for a in WAYS:
        count += greet(has_s[a], (s + a, n))
        count += greet(has_n[a], (s, n + a))
        for b in WAYS:
            count += greet(jnp.logical_and(has_s[a], has_n[b]), (s + a, n + b))
    for mid in (NN // 2 - 1, NN // 2):
        count += greet(n != mid, (s, mid))
    for other in range(NN):
        count += greet(jnp.logical_and(is_i, n != other), (s, other))

    def in_range(j):
        return jnp.logical_and(s + (j - 2) >= 0, s + (j - 2) <= NS - 1)

    for j in range(5):
        ok = jnp.logical_and(is_i, in_range(j))
        if j != 2:
            count += greet(ok, (s + (j - 2), n))
        count += greet(ok, (s + (j - 2), NN - 1 - n))

    zrow = jnp.zeros((24, DIP), F32)

    def clear(i, carry):
        for c in range(3):
            for rd in range(2):
                lo = i
                for pp in range(2):
                    xb[rd, c, pp, jnp.where(lo < 4, lo + 1 - pp, lo + 9 + pp)] = zrow
            gb[c, jnp.where(i < 4, i + 1, i + 9)] = jnp.zeros((HN, DIP), F32)
        for c in range(3):
            for rd in range(2):
                xb[rd, c, 0, O + i, pl.ds(16, 8), :] = jnp.zeros((8, DIP), F32)
        return carry

    lax.fori_loop(0, 8, clear, 0)

    for a, w in ((-1, 0), (1, 1)):
        @pl.when(jnp.logical_not(has_s[a]))
        def _():
            rs[:, :, w] = jnp.zeros((2, 3, 4, HN, DIP), F32)

        @pl.when(jnp.logical_not(has_n[a]))
        def _():
            rn[:, :, w] = jnp.zeros((2, 3, 4, 8, DIP), F32)

        for b, v in ((-1, 0), (1, 1)):
            @pl.when(jnp.logical_not(jnp.logical_and(has_s[a], has_n[b])))
            def _():
                rc[:, :, w, v] = jnp.zeros((2, 3, 8, DIP), F32)

    @pl.when(is_i)
    def _():
        tx[...] = jnp.zeros_like(tx)
        for j in range(5):
            @pl.when(jnp.logical_not(in_range(j)))
            def _():
                plw[j] = jnp.zeros((4, 8, DIP), F32)
                qw[:, j] = jnp.zeros((2, 8, DIP), F32)
                r4[:, j] = jnp.zeros((2, 8, DIP), F32)
                if 1 <= j <= 3:
                    r8[:, j - 1] = jnp.zeros((2, 8, DIP), F32)

    for k in range(3):
        loads["small", k].wait()
    loads["ct"].wait()
    pk[...] = jnp.concatenate([small[0], small[1], ct_v[...].astype(F32), small[2]], axis=1)

    pl.semaphore_wait(barrier, count)

    gathers = []
    for k, mid in enumerate((NN // 2 - 1, NN // 2)):
        gathers.append(
            (
                n != mid,
                pltpu.make_async_remote_copy(
                    src_ref=pk, dst_ref=gath.at[n], send_sem=g_snd.at[k], recv_sem=g_rcv,
                    device_id=(s, mid), device_id_type=MESH,
                ),
            )
        )
    for cond, copy in gathers:
        pl.when(cond)(copy.start)

    loads["st"].wait()

    def recip(i, carry):
        st[i] = 0.1 / st[i]
        return carry

    lax.fori_loop(0, HS, recip, 0)

    @pl.when(is_a)
    def _():
        for i in range(HS):
            qw[0, 2, i : i + 1, :] = 0.5 * st[i, HN - 1 : HN, :]

    @pl.when(is_b)
    def _():
        for i in range(HS):
            qw[0, 2, i : i + 1, :] = 0.5 * st[i, 0:1, :]

    def row_copies(buf, snd, rcv, first, last, src):
        out = []
        for rel in range(2):
            for j in range(first, last):
                if rel == 0 and j == 2:
                    continue
                target_n = n if rel == 0 else NN - 1 - n
                snd_copy = pltpu.make_async_remote_copy(
                    src_ref=src, dst_ref=buf.at[rel, 4 - j - first], send_sem=snd.at[rel, j - first],
                    recv_sem=rcv.at[rel, 4 - j - first], device_id=(s + (j - 2), target_n), device_id_type=MESH,
                )
                rcv_copy = pltpu.make_async_remote_copy(
                    src_ref=src, dst_ref=buf.at[rel, j - first], send_sem=snd.at[rel, j - first],
                    recv_sem=rcv.at[rel, j - first], device_id=(s + (j - 2), target_n), device_id_type=MESH,
                )
                out.append((in_range(j), snd_copy, rcv_copy))
        return out

    q_copies = row_copies(qw, q_snd, q_rcv, 0, 5, qw.at[0, 2])
    r4_copies = row_copies(r4, r4_snd, r4_rcv, 0, 5, r4.at[0, 2])
    r8_copies = row_copies(r8, r8_snd, r8_rcv, 1, 4, r8.at[0, 1])
    w_copies = []
    for j in (0, 1, 3, 4):
        w_copies.append(
            (
                in_range(j),
                pltpu.make_async_remote_copy(
                    src_ref=plw.at[2], dst_ref=plw.at[4 - j], send_sem=w_snd.at[j], recv_sem=w_rcv.at[4 - j],
                    device_id=(s + (j - 2), n), device_id_type=MESH,
                ),
                pltpu.make_async_remote_copy(
                    src_ref=plw.at[2], dst_ref=plw.at[j], send_sem=w_snd.at[j], recv_sem=w_rcv.at[j],
                    device_id=(s + (j - 2), n), device_id_type=MESH,
                ),
            )
        )

    def send_rows(copies):
        for cond, snd, _ in copies:
            pl.when(cond)(snd.start)

    def get_rows(copies):
        for cond, _, rcv in copies:
            pl.when(cond)(rcv.wait_recv)

    def end_rows(copies):
        for cond, snd, _ in copies:
            pl.when(cond)(snd.wait_send)

    @pl.when(is_i)
    def _():
        send_rows(q_copies)

    keep_hi = jnp.logical_or(has_n[1], sub >= 4)
    keep_lo = jnp.logical_or(has_n[-1], sub < 4)
    keep = jnp.logical_and(keep_hi, keep_lo)

    def sweeps(rd, c):
        def sweep(k, carry):
            src = lax.rem(k - 1, 2)
            dst = lax.rem(k, 2)

            def get(i):
                return [[xb[rd, c, src, i, t * 8 : t * 8 + 8, cols(j)] for j in range(NJ)] for t in range(3)]

            def pair(m, inner):
                base = O - k + 2 * m
                rows = [get(base - 1 + r) for r in range(2 + 2)]
                vals = {}
                for r in range(2):
                    i = base + r
                    xm, x, xp = rows[r : r + 3]
                    ok = jnp.logical_and(
                        jnp.logical_or(has_s[-1], i >= O), jnp.logical_or(has_s[1], i < O + HS)
                    )
                    one, two = jnp.where(ok, 0.1, 0.0), jnp.where(ok, 0.2, 0.0)
                    up = [[pltpu.roll(v, 1, 0) for v in q] for q in x]
                    dn = [[pltpu.roll(v, 7, 0) for v in q] for q in x]
                    for t in range(3):
                        left, right = lane_pair(x[t], lane)
                        for j in range(NJ):
                            sy = jnp.where(sub == 0, up[(t + 2) % 3][j], up[t][j]) + jnp.where(
                                sub == 7, dn[(t + 1) % 3][j], dn[t][j]
                            )
                            sx = xm[t][j] + xp[t][j]
                            sz = left[j] + right[j]
                            if c == 0:
                                val = two * (x[t][j] + sx) + one * (sy + sz)
                            elif c == 1:
                                val = two * (x[t][j] + sy) + one * (sx + sz)
                            else:
                                val = two * (x[t][j] + sz) + one * (sx + sy)
                            if t < 2:
                                val = val + gb[c, i, t * 8 : t * 8 + 8, cols(j)]
                            else:
                                val = jnp.where(keep, val, 0.0)
                            vals[r, t, j] = val
                for (r, t, j), val in vals.items():
                    xb[rd, c, dst, base + r, t * 8 : t * 8 + 8, cols(j)] = val
                return inner

            lax.fori_loop(0, HS // 2 + k, pair, 0)
            return carry

        lax.fori_loop(1, SW + 1, sweep, 0)

    def messages(rd, c):
        out = []
        for a, w in ((-1, 0), (1, 1)):
            first = 1 if a < 0 else O + HS
            out.append(
                (
                    has_s[a],
                    pltpu.make_async_remote_copy(
                        src_ref=xb.at[rd, c, 0, pl.ds(first, 4), pl.ds(0, HN)], dst_ref=rs.at[rd, c, 1 - w],
                        send_sem=s_snd.at[rd, c, w], recv_sem=s_rcv.at[rd, c, 1 - w],
                        device_id=(s + a, n), device_id_type=MESH,
                    ),
                    pltpu.make_async_remote_copy(
                        src_ref=rs.at[rd, c, w], dst_ref=rs.at[rd, c, w],
                        send_sem=s_snd.at[rd, c, w], recv_sem=s_rcv.at[rd, c, w],
                        device_id=(s + a, n), device_id_type=MESH,
                    ),
                )
            )
        for b, v in ((-1, 0), (1, 1)):
            out.append(
                (
                    has_n[b],
                    pltpu.make_async_remote_copy(
                        src_ref=sn.at[rd, c, v], dst_ref=rn.at[rd, c, 1 - v],
                        send_sem=n_snd.at[rd, c, v], recv_sem=n_rcv.at[rd, c, 1 - v],
                        device_id=(s, n + b), device_id_type=MESH,
                    ),
                    pltpu.make_async_remote_copy(
                        src_ref=sn.at[rd, c, v], dst_ref=rn.at[rd, c, v],
                        send_sem=n_snd.at[rd, c, v], recv_sem=n_rcv.at[rd, c, v],
                        device_id=(s, n + b), device_id_type=MESH,
                    ),
                )
            )
        for a, w in ((-1, 0), (1, 1)):
            for b, v in ((-1, 0), (1, 1)):
                out.append(
                    (
                        jnp.logical_and(has_s[a], has_n[b]),
                        pltpu.make_async_remote_copy(
                            src_ref=sc.at[rd, c, w, v], dst_ref=rc.at[rd, c, 1 - w, 1 - v],
                            send_sem=c_snd.at[rd, c, w, v], recv_sem=c_rcv.at[rd, c, 1 - w, 1 - v],
                            device_id=(s + a, n + b), device_id_type=MESH,
                        ),
                        pltpu.make_async_remote_copy(
                            src_ref=sc.at[rd, c, w, v], dst_ref=rc.at[rd, c, w, v],
                            send_sem=c_snd.at[rd, c, w, v], recv_sem=c_rcv.at[rd, c, w, v],
                            device_id=(s + a, n + b), device_id_type=MESH,
                        ),
                    )
                )
        return out

    msgs = {(rd, c): messages(rd, c) for rd in range(2) for c in range(3)}
    r4sub = sub5 < 4

    def ghost(rd, c, i):
        return xb[rd, c, 0, i, 16:24, :]

    def send(rd, c):
        group = msgs[rd, c]
        for cond, snd, _ in group[:2]:
            pl.when(cond)(snd.start)
        for w in range(2):
            g = [ghost(rd, c, O - d if w == 0 else O + HS - 1 + d) for d in (1, 2, 3)]
            sc[rd, c, w, 1] = jnp.where(
                r4sub, g[0], jnp.where(sub5 < 6, pltpu.roll(g[1], 4, 0), pltpu.roll(g[2], 6, 0))
            )
            sc[rd, c, w, 0] = jnp.where(
                r4sub, jnp.where(sub5 >= 2, pltpu.roll(g[1], 4, 0), pltpu.roll(g[2], 2, 0)), g[0]
            )
        for cond, snd, _ in group[4:]:
            pl.when(cond)(snd.start)
        for t in range(4):
            first, second = ghost(rd, c, O + t), ghost(rd, c, O + t + 4)
            sn[rd, c, 1, t] = jnp.where(r4sub, first, pltpu.roll(second, 4, 0))
            sn[rd, c, 0, t] = jnp.where(r4sub, pltpu.roll(first, 4, 0), second)
        for cond, snd, _ in group[2:4]:
            pl.when(cond)(snd.start)

    def merge(rd, c, store):
        for cond, _, rcv in msgs[rd, c]:
            pl.when(cond)(rcv.wait_recv)
        for i in range(HS):
            t = i % 4
            low = xb[rd, c, 0, O + i, 0:8, :]
            high = xb[rd, c, 0, O + i, 8:16, :]
            way = 0 if i < 4 else 1
            low = low + rs[rd, c, way, t, 0:8, :]
            high = high + rs[rd, c, way, t, 8:16, :]
            from_lo, from_hi = rn[rd, c, 0, t], rn[rd, c, 1, t]
            if i < 4:
                from_hi = pltpu.roll(from_hi, 4, 0)
            else:
                from_lo = pltpu.roll(from_lo, 4, 0)
            low = low + jnp.where(r4sub, from_lo, 0.0)
            high = high + jnp.where(r4sub, 0.0, from_hi)
            d = i + 1 if i < 4 else HS - i
            if d <= 3:
                corner_lo, corner_hi = rc[rd, c, way, 0], rc[rd, c, way, 1]
                if d == 1:
                    low = low + jnp.where(r4sub, corner_lo, 0.0)
                    high = high + jnp.where(r4sub, 0.0, corner_hi)
                elif d == 2:
                    low = low + jnp.where(sub5 < 2, pltpu.roll(corner_lo, 4, 0), 0.0)
                    high = high + jnp.where(sub5 >= 6, pltpu.roll(corner_hi, 4, 0), 0.0)
                else:
                    low = low + jnp.where(sub5 < 2, pltpu.roll(corner_lo, 2, 0), 0.0)
                    high = high + jnp.where(sub5 >= 6, pltpu.roll(corner_hi, 6, 0), 0.0)
            store(i, low, high)

    def traction(p_of, q_of):
        for r in range(-3, HS + 3):
            p_row = p_of(r)
            own = p_row * q_of(0, r)
            far = p_row * q_of(1, r)
            below = jnp.where(is_b, far, own)
            above = jnp.where(is_b, own, far)
            tt[r + 3] = jnp.where(sub5 == 3, -below, jnp.where(sub5 == 4, above, 0.0))

        def tile_sweep(src, dst, lo, hi, shift):
            def one(i, carry):
                x = [src[i, :, cols(j)] for j in range(NJ)]
                left, right = lane_pair(x, lane)
                for j in range(NJ):
                    sy = pltpu.roll(x[j], 1, 0) + pltpu.roll(x[j], 7, 0)
                    sx = src[i - 1, :, cols(j)] + src[i + 1, :, cols(j)]
                    dst[i - shift, :, cols(j)] = (
                        0.2 * (x[j] + sy) + 0.1 * (sx + left[j] + right[j]) + tt[i, :, cols(j)]
                    )
                return carry

            lax.fori_loop(jnp.where(has_s[-1], lo, 3), jnp.where(has_s[1], hi, 11), one, 0)

        tile_sweep(tt, tx.at[0], 1, 13, 0)
        tile_sweep(tx.at[0], tx.at[1], 2, 12, 0)
        tile_sweep(tx.at[1], corr, 3, 11, 3)

    def win_row(ref, r):
        j, i = divmod(r + 16, 8)
        return ref(j)[i : i + 1, :]

    def lubricate(opening, p, ap, ct, inj, first_row):
        rows = opening.shape[0]
        lanes = lax.broadcasted_iota(jnp.int32, (rows, DIP), 1)
        first, last = lanes == 0, lanes == DIP - 1
        strike = lax.broadcasted_iota(jnp.int32, (rows, DIP), 0) + (s * HS + first_row)
        valid = jnp.logical_and(strike >= 0, strike < NS * HS)
        soft = jnp.maximum(opening, 0.0) + jnp.log1p(jnp.exp(-jnp.abs(opening)))
        width = ap + soft
        k = ct * (width * width * width) / 12.0
        base = 0.5 * p - opening + inj
        k_up, k_dn = rows_sums(k)
        k_l, k_r = lane_sums(k, first, last)
        f_up, f_dn, f_l, f_r = [0.5 * (k + v) for v in (k_up, k_dn, k_l, k_r)]
        rden = jnp.where(valid, 1.0 / (0.5 + (f_up + f_dn + f_l + f_r)), 0.0)
        base = base * rden
        f_up, f_dn = f_up * rden, f_dn * rden
        f_l = jnp.where(first, 0.0, f_l * rden)
        f_r = jnp.where(last, 0.0, f_r * rden)
        for _ in range(SW_L):
            p_up, p_dn = rows_sums(p)
            p = base + f_up * p_up + f_dn * p_dn + f_l * pltpu.roll(p, 1, 1) + f_r * pltpu.roll(p, DIP - 1, 1)
        return p

    sign = jnp.where(is_b, 1.0, -1.0)

    for c in order:
        loads["f", c].wait()

        def scale(i, carry, c=c):
            gb[c, O + i] = gb[c, O + i] * st[i]
            return carry

        lax.fori_loop(0, HS, scale, 0)
        loads["u", c].wait()
        sweeps(0, c)
        send(0, c)

    @pl.when(is_i)
    def _():
        gath[n] = pk[...]
        pltpu.make_async_copy(gath.at[pl.ds(0, NN - 1)], gath.at[pl.ds(0, NN - 1)], g_rcv).wait()
        for big in range(NJ):
            tiles = [gath[big * 4 + m] for m in range(4)]
            for kind in range(4):
                val = None
                for m in range(4):
                    shift = (m - kind) % 4 * 32
                    piece = pltpu.roll(tiles[m], shift, 1) if shift else tiles[m]
                    val = piece if val is None else jnp.where(lane >= 32 * m, piece, val)
                plw[2, kind, :, cols(big)] = val
        send_rows(w_copies)
        get_rows(q_copies)
        get_rows(w_copies)
        traction(
            lambda r: win_row(lambda j: plw[j, 0], r), lambda rel, r: win_row(lambda j: qw[rel, j], r)
        )

    def to_second(c):
        def store(i, low, high):
            xb[1, c, 0, O + i, 0:8, :] = low
            xb[1, c, 0, O + i, 8:16, :] = high

        return store

    def to_out(c):
        def store(i, low, high):
            outb[c, i, 0:8, :] = low
            outb[c, i, 8:16, :] = high

        return store

    def own_tile(get, put):
        @pl.when(is_a)
        def _():
            for i in range(HS):
                put(i, 8, get(i, 8) + jnp.where(r4sub, 0.0, pltpu.roll(corr[i], 4, 0)))

        @pl.when(is_b)
        def _():
            for i in range(HS):
                put(i, 0, get(i, 0) + jnp.where(r4sub, pltpu.roll(corr[i], 4, 0), 0.0))

    def put_rows(get, put):
        @pl.when(is_a)
        def _():
            for i in range(HS):
                put(i, get(i, HN - 1))

        @pl.when(is_b)
        def _():
            for i in range(HS):
                put(i, get(i, 0))

    def put_second(i, r, v):
        xb[1, 1, 0, O + i, r : r + 8, :] = v

    def put_out(i, r, v):
        outb[1, i, r : r + 8, :] = v

    def put_r4(i, v):
        r4[0, 2, i : i + 1, :] = v

    def put_r8(i, v):
        r8[0, 1, i : i + 1, :] = v

    for c in order:
        merge(0, c, to_second(c))
        if c == 1:
            own_tile(lambda i, r: xb[1, 1, 0, O + i, r : r + 8, :], put_second)
            put_rows(lambda i, r: xb[1, 1, 0, O + i, r : r + 1, :], put_r4)
            pl.when(is_i)(lambda: send_rows(r4_copies))
        sweeps(1, c)
        send(1, c)

    def flat(x):
        return x.reshape(x.shape[0] * 8, DIP)

    @pl.when(is_i)
    def _():
        get_rows(r4_copies)
        opening = sign * (flat(r4[0]) - flat(r4[1]))
        p1 = lubricate(opening, *[flat(plw[:, kind]) for kind in range(4)], -16)
        p1w[...] = p1.reshape(5, 8, DIP)
        traction(
            lambda r: win_row(lambda j: p1w[j], r), lambda rel, r: win_row(lambda j: qw[rel, j], r)
        )

    copies_out = [pltpu.make_async_copy(outb.at[c], u_out.at[c], out_sem.at[c]) for c in range(3)]
    for c in order:
        merge(1, c, to_out(c))
        if c == 1:
            put_rows(lambda i, r: outb[1, i, r : r + 1, :], put_r8)
            pl.when(is_i)(lambda: send_rows(r8_copies))
            own_tile(lambda i, r: outb[1, i, r : r + 8, :], put_out)
        copies_out[c].start()

    e4_copies = []
    for i in range(NN // 2):
        e4_copies.append(
            (
                jnp.logical_and(is_i, n != side * 8 + i),
                pltpu.make_async_remote_copy(
                    src_ref=e4s.at[i], dst_ref=e4r, send_sem=e4_snd.at[i], recv_sem=e4_rcv,
                    device_id=(s, side * 8 + i), device_id_type=MESH,
                ),
            )
        )

    @pl.when(is_i)
    def _():
        lanes = lax.broadcasted_iota(jnp.int32, (40, DIP), 1)
        first, last = lanes == 0, lanes == DIP - 1
        strike = lax.broadcasted_iota(jnp.int32, (40, DIP), 0) + (s * HS - 16)
        valid = jnp.logical_and(strike >= 0, strike < NS * HS)

        def across(x):
            up, dn = rows_sums(x)
            left, right = lane_sums(x, first, last)
            return 0.1 * ((up + dn) + (left + right))

        force = flat(p1w[...]) * (flat(qw[0]) + flat(qw[1]))
        d0 = jnp.where(valid, across(force) + force, 0.0)
        d1 = 0.2 * force
        e0 = jnp.where(valid, 0.2 * d1 + across(d0) + force, 0.0)
        e1 = jnp.where(valid, 0.2 * d1 + across(d1) + 0.2 * d0, 0.0)
        extra = (0.2 * e1 + across(e0) + force)[8:32]
        get_rows(r8_copies)
        opening = sign * (flat(r8[0]) - flat(r8[1])) + extra
        p2 = lubricate(
            opening, flat(p1w[1:4]), flat(plw[1:4, 1]), flat(plw[1:4, 2]), flat(plw[1:4, 3]), -8
        )
        for j in range(NJ):
            p2t[j] = p2[8:16, cols(j)]
        for i in range(NN // 2):
            shift = -(i % 4) * 32 % LANES
            tile = p2t[side * 2 + i // 4]
            e4s[i] = pltpu.roll(tile, shift, 1) if shift else tile
        for cond, copy in e4_copies:
            pl.when(cond)(copy.start)
        e4r[...] = e4s[jnp.where(is_b, 0, 7)]

    @pl.when(jnp.logical_not(is_i))
    def _():
        pltpu.make_async_remote_copy(
            src_ref=e4s.at[0], dst_ref=e4r, send_sem=e4_snd.at[0], recv_sem=e4_rcv,
            device_id=(s, NN - 1 - n), device_id_type=MESH,
        ).wait_recv()

    p_out[...] = e4r[:, 0:32]

    for copy in copies_out:
        copy.wait()
    for group in msgs.values():
        for cond, snd, _ in group:
            pl.when(cond)(snd.wait_send)
    for cond, copy in gathers:
        pl.when(cond)(copy.wait_send)
    for cond, copy in e4_copies:
        pl.when(cond)(copy.wait_send)

    @pl.when(is_i)
    def _():
        for copies in (q_copies, w_copies, r4_copies, r8_copies):
            end_rows(copies)


def body(displacement, body_force, stiffness, aperture_base, contact_open, pressure_init, injection):
    vm = pl.BlockSpec(memory_space=pltpu.VMEM)
    hbm = pl.BlockSpec(memory_space=pl.ANY)
    dma = pltpu.SemaphoreType.DMA

    def buf(*shape):
        return pltpu.VMEM(shape, F32)

    scratch = [
        buf(2, 3, 2, 18, 24, DIP),
        buf(3, 18, HN, DIP),
        buf(HS, HN, DIP),
        buf(3, HS, HN, DIP),
        buf(2, 3, 2, 4, HN, DIP),
        buf(2, 3, 2, 4, 8, DIP),
        buf(2, 3, 2, 4, 8, DIP),
        buf(2, 3, 2, 2, 8, DIP),
        buf(2, 3, 2, 2, 8, DIP),
        buf(8, LANES),
        buf(NN, 8, LANES),
        buf(5, 4, 8, DIP),
        buf(2, 5, 8, DIP),
        buf(2, 5, 8, DIP),
        buf(2, 3, 8, DIP),
        buf(3, 8, 32),
        pltpu.VMEM((8, 32), jnp.int32),
        buf(14, 8, DIP),
        buf(2, 14, 8, DIP),
        buf(HS, 8, DIP),
        buf(5, 8, DIP),
        buf(NJ, 8, LANES),
        buf(NN // 2, 8, LANES),
        buf(8, LANES),
        dma((11,)), dma((3,)),
        dma((2, 3, 2)), dma((2, 3, 2)), dma((2, 3, 2)), dma((2, 3, 2)),
        dma((2, 3, 2, 2)), dma((2, 3, 2, 2)),
        dma((2,)), dma,
        dma((2, 5)), dma((2, 5)), dma((5,)), dma((5,)), dma((2, 5)), dma((2, 5)), dma((2, 3)), dma((2, 3)),
        dma((NN // 2,)), dma,
    ]
    return pl.pallas_call(
        kernel,
        out_shape=(
            jax.ShapeDtypeStruct((3, HS, HN, DIP), F32),
            jax.ShapeDtypeStruct((8, 32), F32),
        ),
        in_specs=[hbm] * 7,
        out_specs=(hbm, vm),
        scratch_shapes=scratch,
        compiler_params=pltpu.CompilerParams(
            collective_id=0, has_side_effects=True, vmem_limit_bytes=60 * 2**20
        ),
        cost_estimate=pl.CostEstimate(flops=60_000_000, bytes_accessed=2_700_000, transcendentals=40_000),
    )(displacement, body_force, stiffness, aperture_base, contact_open, pressure_init, injection)


def solution(mesh):
    in_specs = (
        P(None, "strike", "normal", None),
        P(None, "strike", "normal", None),
        P("strike", "normal", None),
        P("strike", "normal"),
        P("strike", "normal"),
        P("strike", "normal"),
        P("strike", "normal"),
    )
    out_specs = (P(None, "strike", "normal", None), P("strike", "normal"))
    return jax.shard_map(body, mesh=mesh, in_specs=in_specs, out_specs=out_specs, check_vma=False)
```

```python
import jax
import jax.numpy as jnp
from jax import lax
from jax.experimental import pallas as pl
from jax.experimental.pallas import tpu as pltpu
from jax.sharding import PartitionSpec as P

MESH = pl.DeviceIdType.MESH
F32 = jnp.float32
NS, NN = 8, 16
HS, HN, DIP = 8, 16, 512
SW = 4
SW_L = 6
O = 5
LANES = 128
NJ = DIP // LANES
WAYS = (-1, 1)


def lane_pair(x, lane):
    left = [jnp.where(lane == 0, 0.0, pltpu.roll(x[-1], 1, 1))] + x[:-1]
    right = x[1:] + [jnp.where(lane == LANES - 1, 0.0, pltpu.roll(x[0], LANES - 1, 1))]
    return left, right


def cols(j):
    return slice(j * LANES, (j + 1) * LANES)


def lane_shifts(x):
    cut = DIP - LANES
    left = jnp.concatenate([pltpu.roll(x[:, cut:], 1, 1), x[:, :cut]], axis=1)
    right = jnp.concatenate([x[:, LANES:], pltpu.roll(x[:, :LANES], LANES - 1, 1)], axis=1)
    return left, right


def shuffle(x, matrix):
    high = x.astype(jnp.bfloat16)
    rest = x - high.astype(F32)
    mid = rest.astype(jnp.bfloat16)
    low = (rest - mid.astype(F32)).astype(jnp.bfloat16)
    out = [jnp.dot(part, matrix, preferred_element_type=F32) for part in (high, mid, low)]
    return out[0] + (out[1] + out[2])


def rows_sums(x):
    count = x.shape[0]
    return pltpu.roll(x, 1, 0), pltpu.roll(x, count - 1, 0)


def kernel(
    u_in, f_in, st_in, ap_hbm, ct_hbm, p_hbm, inj_hbm,
    u_out, p_out,
    xb, gb, st, outb, us, fs, into, back, row, rs, rn, sn, rc, sc, pk, gath, plw, qw, r4, r8, small, ct_v, tt, tx, corr, p1w, p2t, e4s, e4r,
    in_sem, out_sem, s_snd, s_rcv, n_snd, n_rcv, c_snd, c_rcv, g_snd, g_rcv,
    q_snd, q_rcv, w_snd, w_rcv, r4_snd, r4_rcv, r8_snd, r8_rcv, e4_snd, e4_rcv,
):
    s = lax.axis_index("strike")
    n = lax.axis_index("normal")
    is_a = n == NN // 2 - 1
    is_b = n == NN // 2
    is_i = jnp.logical_or(is_a, is_b)
    side = jnp.where(n >= NN // 2, 1, 0)
    has_s = {-1: s > 0, 1: s < NS - 1}
    has_n = {-1: n > 0, 1: n < NN - 1}
    lane = lax.broadcasted_iota(jnp.int32, (8, LANES), 1)
    sub = lax.broadcasted_iota(jnp.int32, (8, LANES), 0)
    sub5 = lax.broadcasted_iota(jnp.int32, (8, DIP), 0)

    order = (1, 0, 2)
    loads = {"st": pltpu.make_async_copy(st_in, st, in_sem.at[6])}
    for c in range(3):
        loads["u", c] = pltpu.make_async_copy(
            u_in.at[c], us.at[c], in_sem.at[c]
        )
        loads["f", c] = pltpu.make_async_copy(f_in.at[c], fs.at[c], in_sem.at[3 + c])
    for k, ref in enumerate((p_hbm, ap_hbm, inj_hbm)):
        loads["small", k] = pltpu.make_async_copy(ref, small.at[k], in_sem.at[7 + k])
        loads["small", k].start()
    loads["ct"] = pltpu.make_async_copy(ct_hbm, ct_v, in_sem.at[10])
    loads["ct"].start()
    loads["st"].start()
    for c in order:
        loads["f", c].start()
        loads["u", c].start()

    barrier = pltpu.get_barrier_semaphore()
    count = jnp.int32(0)

    def greet(cond, target):
        @pl.when(cond)
        def _():
            pl.semaphore_signal(barrier, inc=1, device_id=target, device_id_type=MESH)

        return jnp.where(cond, 1, 0)

    for a in WAYS:
        count += greet(has_s[a], (s + a, n))
        count += greet(has_n[a], (s, n + a))
        for b in WAYS:
            count += greet(jnp.logical_and(has_s[a], has_n[b]), (s + a, n + b))
    for mid in (NN // 2 - 1, NN // 2):
        count += greet(n != mid, (s, mid))
    for other in range(NN):
        count += greet(jnp.logical_and(is_i, n != other), (s, other))

    def in_range(j):
        return jnp.logical_and(s + (j - 2) >= 0, s + (j - 2) <= NS - 1)

    for j in range(5):
        ok = jnp.logical_and(is_i, in_range(j))
        if j != 2:
            count += greet(ok, (s + (j - 2), n))
        count += greet(ok, (s + (j - 2), NN - 1 - n))

    zrow = jnp.zeros((24, DIP), F32)

    def clear(i, carry):
        at = jnp.where(i < O, i, i + HS)
        for c in range(3):
            for rd in range(2):
                for pp in range(2):
                    xb[rd, c, pp, at] = zrow
            gb[c, at] = jnp.zeros((HN, DIP), F32)
        return carry

    lax.fori_loop(0, 10, clear, 0)

    def clear_own(i, carry):
        for c in range(3):
            for rd in range(2):
                xb[rd, c, 0, O + i, pl.ds(16, 8), :] = jnp.zeros((8, DIP), F32)
        return carry

    lax.fori_loop(0, HS, clear_own, 0)

    d0 = lax.broadcasted_iota(jnp.int32, (DIP, DIP), 0)
    d1 = lax.broadcasted_iota(jnp.int32, (DIP, DIP), 1)
    into[...] = jnp.where(d0 == 4 * (d1 % LANES) + d1 // LANES, 1.0, 0.0).astype(jnp.bfloat16)
    back[...] = jnp.where(d1 == 4 * (d0 % LANES) + d0 // LANES, 1.0, 0.0).astype(jnp.bfloat16)

    for a, w in ((-1, 0), (1, 1)):
        @pl.when(jnp.logical_not(has_s[a]))
        def _():
            rs[:, :, w] = jnp.zeros((2, 3, 4, HN, DIP), F32)

        @pl.when(jnp.logical_not(has_n[a]))
        def _():
            rn[:, :, w] = jnp.zeros((2, 3, 4, 8, DIP), F32)

        for b, v in ((-1, 0), (1, 1)):
            @pl.when(jnp.logical_not(jnp.logical_and(has_s[a], has_n[b])))
            def _():
                rc[:, :, w, v] = jnp.zeros((2, 3, 8, DIP), F32)

    @pl.when(is_i)
    def _():
        tx[...] = jnp.zeros_like(tx)
        for j in range(5):
            @pl.when(jnp.logical_not(in_range(j)))
            def _():
                plw[j] = jnp.zeros((4, 8, DIP), F32)
                qw[:, j] = jnp.zeros((2, 8, DIP), F32)
                r4[:, j] = jnp.zeros((2, 8, DIP), F32)
                if 1 <= j <= 3:
                    r8[:, j - 1] = jnp.zeros((2, 8, DIP), F32)

    for k in range(3):
        loads["small", k].wait()
    loads["ct"].wait()
    pk[...] = jnp.concatenate([small[0], small[1], ct_v[...].astype(F32), small[2]], axis=1)

    pl.semaphore_wait(barrier, count)

    gathers = []
    for k, mid in enumerate((NN // 2 - 1, NN // 2)):
        gathers.append(
            (
                n != mid,
                pltpu.make_async_remote_copy(
                    src_ref=pk, dst_ref=gath.at[n], send_sem=g_snd.at[k], recv_sem=g_rcv,
                    device_id=(s, mid), device_id_type=MESH,
                ),
            )
        )
    for cond, copy in gathers:
        pl.when(cond)(copy.start)

    loads["st"].wait()

    def recip(i, carry):
        st[i] = 0.1 / st[i]
        return carry

    lax.fori_loop(0, HS, recip, 0)

    @pl.when(is_a)
    def _():
        for i in range(HS):
            row[i : i + 1, :] = 0.5 * st[i, HN - 1 : HN, :]

    @pl.when(is_b)
    def _():
        for i in range(HS):
            row[i : i + 1, :] = 0.5 * st[i, 0:1, :]

    @pl.when(is_i)
    def _():
        qw[0, 2] = shuffle(row[...], into[...])

    def row_copies(buf, snd, rcv, first, last, src):
        out = []
        for rel in range(2):
            for j in range(first, last):
                if rel == 0 and j == 2:
                    continue
                target_n = n if rel == 0 else NN - 1 - n
                snd_copy = pltpu.make_async_remote_copy(
                    src_ref=src, dst_ref=buf.at[rel, 4 - j - first], send_sem=snd.at[rel, j - first],
                    recv_sem=rcv.at[rel, 4 - j - first], device_id=(s + (j - 2), target_n), device_id_type=MESH,
                )
                rcv_copy = pltpu.make_async_remote_copy(
                    src_ref=src, dst_ref=buf.at[rel, j - first], send_sem=snd.at[rel, j - first],
                    recv_sem=rcv.at[rel, j - first], device_id=(s + (j - 2), target_n), device_id_type=MESH,
                )
                out.append((in_range(j), snd_copy, rcv_copy))
        return out

    q_copies = row_copies(qw, q_snd, q_rcv, 0, 5, qw.at[0, 2])
    r4_copies = row_copies(r4, r4_snd, r4_rcv, 0, 5, r4.at[0, 2])
    r8_copies = row_copies(r8, r8_snd, r8_rcv, 1, 4, r8.at[0, 1])
    w_copies = []
    for j in (0, 1, 3, 4):
        w_copies.append(
            (
                in_range(j),
                pltpu.make_async_remote_copy(
                    src_ref=plw.at[2], dst_ref=plw.at[4 - j], send_sem=w_snd.at[j], recv_sem=w_rcv.at[4 - j],
                    device_id=(s + (j - 2), n), device_id_type=MESH,
                ),
                pltpu.make_async_remote_copy(
                    src_ref=plw.at[2], dst_ref=plw.at[j], send_sem=w_snd.at[j], recv_sem=w_rcv.at[j],
                    device_id=(s + (j - 2), n), device_id_type=MESH,
                ),
            )
        )

    def send_rows(copies):
        for cond, snd, _ in copies:
            pl.when(cond)(snd.start)

    def get_rows(copies):
        for cond, _, rcv in copies:
            pl.when(cond)(rcv.wait_recv)

    def end_rows(copies):
        for cond, snd, _ in copies:
            pl.when(cond)(snd.wait_send)

    @pl.when(is_i)
    def _():
        send_rows(q_copies)

    keep_hi = jnp.logical_or(has_n[1], sub >= 4)
    keep_lo = jnp.logical_or(has_n[-1], sub < 4)
    keep = jnp.logical_and(keep_hi, keep_lo)

    def sweeps(rd, c):
        def sweep(k, carry):
            src = lax.rem(k - 1, 2)
            dst = lax.rem(k, 2)

            def get(i):
                return [[xb[rd, c, src, i, t * 8 : t * 8 + 8, cols(j)] for j in range(NJ)] for t in range(3)]

            def pair(m, inner):
                base = O - k - lax.rem(k, 2) + 4 * m
                rows = [get(base - 1 + r) for r in range(4 + 2)]
                vals = {}
                for r in range(4):
                    i = base + r
                    xm, x, xp = rows[r : r + 3]
                    ok = jnp.logical_and(
                        jnp.logical_or(has_s[-1], i >= O), jnp.logical_or(has_s[1], i < O + HS)
                    )
                    one, two = jnp.where(ok, 0.1, 0.0), jnp.where(ok, 0.2, 0.0)
                    up = [[pltpu.roll(v, 1, 0) for v in q] for q in x]
                    dn = [[pltpu.roll(v, 7, 0) for v in q] for q in x]
                    for t in range(3):
                        left, right = lane_pair(x[t], lane)
                        for j in range(NJ):
                            sy = jnp.where(sub == 0, up[(t + 2) % 3][j], up[t][j]) + jnp.where(
                                sub == 7, dn[(t + 1) % 3][j], dn[t][j]
                            )
                            sx = xm[t][j] + xp[t][j]
                            sz = left[j] + right[j]
                            if c == 0:
                                val = two * (x[t][j] + sx) + one * (sy + sz)
                            elif c == 1:
                                val = two * (x[t][j] + sy) + one * (sx + sz)
                            else:
                                val = two * (x[t][j] + sz) + one * (sx + sy)
                            if t < 2:
                                val = val + gb[c, i, t * 8 : t * 8 + 8, cols(j)]
                            else:
                                val = jnp.where(keep, val, 0.0)
                            vals[r, t, j] = val
                for (r, t, j), val in vals.items():
                    xb[rd, c, dst, base + r, t * 8 : t * 8 + 8, cols(j)] = val
                return inner

            lax.fori_loop(0, (HS + 2 * k + 3) // 4, pair, 0)
            return carry

        lax.fori_loop(1, SW + 1, sweep, 0)

    def messages(rd, c):
        out = []
        for a, w in ((-1, 0), (1, 1)):
            first = 1 if a < 0 else O + HS
            out.append(
                (
                    has_s[a],
                    pltpu.make_async_remote_copy(
                        src_ref=xb.at[rd, c, 0, pl.ds(first, 4), pl.ds(0, HN)], dst_ref=rs.at[rd, c, 1 - w],
                        send_sem=s_snd.at[rd, c, w], recv_sem=s_rcv.at[rd, c, 1 - w],
                        device_id=(s + a, n), device_id_type=MESH,
                    ),
                    pltpu.make_async_remote_copy(
                        src_ref=rs.at[rd, c, w], dst_ref=rs.at[rd, c, w],
                        send_sem=s_snd.at[rd, c, w], recv_sem=s_rcv.at[rd, c, w],
                        device_id=(s + a, n), device_id_type=MESH,
                    ),
                )
            )
        for b, v in ((-1, 0), (1, 1)):
            out.append(
                (
                    has_n[b],
                    pltpu.make_async_remote_copy(
                        src_ref=sn.at[rd, c, v], dst_ref=rn.at[rd, c, 1 - v],
                        send_sem=n_snd.at[rd, c, v], recv_sem=n_rcv.at[rd, c, 1 - v],
                        device_id=(s, n + b), device_id_type=MESH,
                    ),
                    pltpu.make_async_remote_copy(
                        src_ref=sn.at[rd, c, v], dst_ref=rn.at[rd, c, v],
                        send_sem=n_snd.at[rd, c, v], recv_sem=n_rcv.at[rd, c, v],
                        device_id=(s, n + b), device_id_type=MESH,
                    ),
                )
            )
        for a, w in ((-1, 0), (1, 1)):
            for b, v in ((-1, 0), (1, 1)):
                out.append(
                    (
                        jnp.logical_and(has_s[a], has_n[b]),
                        pltpu.make_async_remote_copy(
                            src_ref=sc.at[rd, c, w, v], dst_ref=rc.at[rd, c, 1 - w, 1 - v],
                            send_sem=c_snd.at[rd, c, w, v], recv_sem=c_rcv.at[rd, c, 1 - w, 1 - v],
                            device_id=(s + a, n + b), device_id_type=MESH,
                        ),
                        pltpu.make_async_remote_copy(
                            src_ref=sc.at[rd, c, w, v], dst_ref=rc.at[rd, c, w, v],
                            send_sem=c_snd.at[rd, c, w, v], recv_sem=c_rcv.at[rd, c, w, v],
                            device_id=(s + a, n + b), device_id_type=MESH,
                        ),
                    )
                )
        return out

    msgs = {(rd, c): messages(rd, c) for rd in range(2) for c in range(3)}
    r4sub = sub5 < 4

    def ghost(rd, c, i):
        return xb[rd, c, 0, i, 16:24, :]

    def send(rd, c):
        group = msgs[rd, c]
        for cond, snd, _ in group[:2]:
            pl.when(cond)(snd.start)
        for w in range(2):
            g = [ghost(rd, c, O - d if w == 0 else O + HS - 1 + d) for d in (1, 2, 3)]
            sc[rd, c, w, 1] = jnp.where(
                r4sub, g[0], jnp.where(sub5 < 6, pltpu.roll(g[1], 4, 0), pltpu.roll(g[2], 6, 0))
            )
            sc[rd, c, w, 0] = jnp.where(
                r4sub, jnp.where(sub5 >= 2, pltpu.roll(g[1], 4, 0), pltpu.roll(g[2], 2, 0)), g[0]
            )
        for cond, snd, _ in group[4:]:
            pl.when(cond)(snd.start)
        for t in range(4):
            first, second = ghost(rd, c, O + t), ghost(rd, c, O + t + 4)
            sn[rd, c, 1, t] = jnp.where(r4sub, first, pltpu.roll(second, 4, 0))
            sn[rd, c, 0, t] = jnp.where(r4sub, pltpu.roll(first, 4, 0), second)
        for cond, snd, _ in group[2:4]:
            pl.when(cond)(snd.start)

    def merge(rd, c, store):
        for cond, _, rcv in msgs[rd, c]:
            pl.when(cond)(rcv.wait_recv)
        for i in range(HS):
            t = i % 4
            low = xb[rd, c, 0, O + i, 0:8, :]
            high = xb[rd, c, 0, O + i, 8:16, :]
            way = 0 if i < 4 else 1
            low = low + rs[rd, c, way, t, 0:8, :]
            high = high + rs[rd, c, way, t, 8:16, :]
            from_lo, from_hi = rn[rd, c, 0, t], rn[rd, c, 1, t]
            if i < 4:
                from_hi = pltpu.roll(from_hi, 4, 0)
            else:
                from_lo = pltpu.roll(from_lo, 4, 0)
            low = low + jnp.where(r4sub, from_lo, 0.0)
            high = high + jnp.where(r4sub, 0.0, from_hi)
            d = i + 1 if i < 4 else HS - i
            if d <= 3:
                corner_lo, corner_hi = rc[rd, c, way, 0], rc[rd, c, way, 1]
                if d == 1:
                    low = low + jnp.where(r4sub, corner_lo, 0.0)
                    high = high + jnp.where(r4sub, 0.0, corner_hi)
                elif d == 2:
                    low = low + jnp.where(sub5 < 2, pltpu.roll(corner_lo, 4, 0), 0.0)
                    high = high + jnp.where(sub5 >= 6, pltpu.roll(corner_hi, 4, 0), 0.0)
                else:
                    low = low + jnp.where(sub5 < 2, pltpu.roll(corner_lo, 2, 0), 0.0)
                    high = high + jnp.where(sub5 >= 6, pltpu.roll(corner_hi, 6, 0), 0.0)
            store(i, low, high)

    def traction(p_of, q_of):
        for r in range(-3, HS + 3):
            p_row = p_of(r)
            own = p_row * q_of(0, r)
            far = p_row * q_of(1, r)
            below = jnp.where(is_b, far, own)
            above = jnp.where(is_b, own, far)
            tt[r + 3] = jnp.where(sub5 == 3, -below, jnp.where(sub5 == 4, above, 0.0))

        def tile_sweep(src, dst, lo, hi, shift):
            def one(i, carry):
                x = [src[i, :, cols(j)] for j in range(NJ)]
                left, right = lane_pair(x, lane)
                for j in range(NJ):
                    sy = pltpu.roll(x[j], 1, 0) + pltpu.roll(x[j], 7, 0)
                    sx = src[i - 1, :, cols(j)] + src[i + 1, :, cols(j)]
                    dst[i - shift, :, cols(j)] = (
                        0.2 * (x[j] + sy) + 0.1 * (sx + left[j] + right[j]) + tt[i, :, cols(j)]
                    )
                return carry

            lax.fori_loop(jnp.where(has_s[-1], lo, 3), jnp.where(has_s[1], hi, 11), one, 0)

        tile_sweep(tt, tx.at[0], 1, 13, 0)
        tile_sweep(tx.at[0], tx.at[1], 2, 12, 0)
        tile_sweep(tx.at[1], corr, 3, 11, 3)

    def win_row(ref, r):
        j, i = divmod(r + 16, 8)
        return ref(j)[i : i + 1, :]

    def lubricate(opening, p, ap, ct, inj, first_row):
        rows = opening.shape[0]
        lanes = lax.broadcasted_iota(jnp.int32, (rows, DIP), 1)
        first, last = lanes == 0, lanes == DIP - 1
        strike = lax.broadcasted_iota(jnp.int32, (rows, DIP), 0) + (s * HS + first_row)
        valid = jnp.logical_and(strike >= 0, strike < NS * HS)
        soft = jnp.maximum(opening, 0.0) + jnp.log1p(jnp.exp(-jnp.abs(opening)))
        width = ap + soft
        k = ct * (width * width * width) / 12.0
        base = 0.5 * p - opening + inj
        k_up, k_dn = rows_sums(k)
        k_l, k_r = lane_shifts(k)
        k_l, k_r = jnp.where(first, 0.0, k_l), jnp.where(last, 0.0, k_r)
        f_up, f_dn, f_l, f_r = [0.5 * (k + v) for v in (k_up, k_dn, k_l, k_r)]
        rden = jnp.where(valid, 1.0 / (0.5 + (f_up + f_dn + f_l + f_r)), 0.0)
        base = base * rden
        f_up, f_dn = f_up * rden, f_dn * rden
        f_l = jnp.where(first, 0.0, f_l * rden)
        f_r = jnp.where(last, 0.0, f_r * rden)
        for _ in range(SW_L):
            p_up, p_dn = rows_sums(p)
            p_l, p_r = lane_shifts(p)
            p = (base + (f_up * p_up + f_dn * p_dn)) + (f_l * p_l + f_r * p_r)
        return p

    sign = jnp.where(is_b, 1.0, -1.0)

    for c in order:
        loads["f", c].wait()

        gb[c, pl.ds(O, HS)] = shuffle((fs[c] * st[...]).reshape(HS * HN, DIP), into[...]).reshape(HS, HN, DIP)
        loads["u", c].wait()
        xb[0, c, 0, pl.ds(O, HS), pl.ds(0, HN)] = shuffle(us[c].reshape(HS * HN, DIP), into[...]).reshape(HS, HN, DIP)
        sweeps(0, c)
        send(0, c)

    @pl.when(is_i)
    def _():
        gath[n] = pk[...]
        pltpu.make_async_copy(gath.at[pl.ds(0, NN - 1)], gath.at[pl.ds(0, NN - 1)], g_rcv).wait()
        for big in range(NJ):
            tiles = [gath[big * 4 + m] for m in range(4)]
            for kind in range(4):
                val = None
                for m in range(4):
                    shift = (m - kind) % 4 * 32
                    piece = pltpu.roll(tiles[m], shift, 1) if shift else tiles[m]
                    val = piece if val is None else jnp.where(lane >= 32 * m, piece, val)
                plw[2, kind, :, cols(big)] = val
        plw[2] = shuffle(plw[2].reshape(32, DIP), into[...]).reshape(4, 8, DIP)
        send_rows(w_copies)
        get_rows(q_copies)
        get_rows(w_copies)
        traction(
            lambda r: win_row(lambda j: plw[j, 0], r), lambda rel, r: win_row(lambda j: qw[rel, j], r)
        )

    def to_second(c):
        def store(i, low, high):
            xb[1, c, 0, O + i, 0:8, :] = low
            xb[1, c, 0, O + i, 8:16, :] = high

        return store

    def to_out(c):
        def store(i, low, high):
            outb[c, i, 0:8, :] = low
            outb[c, i, 8:16, :] = high

        return store

    def own_tile(get, put):
        @pl.when(is_a)
        def _():
            for i in range(HS):
                put(i, 8, get(i, 8) + jnp.where(r4sub, 0.0, pltpu.roll(corr[i], 4, 0)))

        @pl.when(is_b)
        def _():
            for i in range(HS):
                put(i, 0, get(i, 0) + jnp.where(r4sub, pltpu.roll(corr[i], 4, 0), 0.0))

    def put_rows(get, put):
        @pl.when(is_a)
        def _():
            for i in range(HS):
                put(i, get(i, HN - 1))

        @pl.when(is_b)
        def _():
            for i in range(HS):
                put(i, get(i, 0))

    def put_second(i, r, v):
        xb[1, 1, 0, O + i, r : r + 8, :] = v

    def put_out(i, r, v):
        outb[1, i, r : r + 8, :] = v

    def put_r4(i, v):
        r4[0, 2, i : i + 1, :] = v

    def put_r8(i, v):
        r8[0, 1, i : i + 1, :] = v

    for c in order:
        merge(0, c, to_second(c))
        if c == 1:
            own_tile(lambda i, r: xb[1, 1, 0, O + i, r : r + 8, :], put_second)
            put_rows(lambda i, r: xb[1, 1, 0, O + i, r : r + 1, :], put_r4)
            pl.when(is_i)(lambda: send_rows(r4_copies))
        sweeps(1, c)
        send(1, c)

    def flat(x):
        return x.reshape(x.shape[0] * 8, DIP)

    @pl.when(is_i)
    def _():
        get_rows(r4_copies)
        opening = sign * (flat(r4[0]) - flat(r4[1]))
        p1 = lubricate(opening, *[flat(plw[:, kind]) for kind in range(4)], -16)
        p1w[...] = p1.reshape(5, 8, DIP)
        traction(
            lambda r: win_row(lambda j: p1w[j], r), lambda rel, r: win_row(lambda j: qw[rel, j], r)
        )

    copies_out = [pltpu.make_async_copy(outb.at[c], u_out.at[c], out_sem.at[c]) for c in range(3)]
    for c in order:
        merge(1, c, to_out(c))
        if c == 1:
            put_rows(lambda i, r: outb[1, i, r : r + 1, :], put_r8)
            pl.when(is_i)(lambda: send_rows(r8_copies))
            own_tile(lambda i, r: outb[1, i, r : r + 8, :], put_out)
        outb[c] = shuffle(outb[c].reshape(HS * HN, DIP), back[...]).reshape(HS, HN, DIP)
        copies_out[c].start()

    e4_copies = []
    for i in range(NN // 2):
        e4_copies.append(
            (
                jnp.logical_and(is_i, n != side * 8 + i),
                pltpu.make_async_remote_copy(
                    src_ref=e4s.at[i], dst_ref=e4r, send_sem=e4_snd.at[i], recv_sem=e4_rcv,
                    device_id=(s, side * 8 + i), device_id_type=MESH,
                ),
            )
        )

    @pl.when(is_i)
    def _():
        lanes = lax.broadcasted_iota(jnp.int32, (40, DIP), 1)
        first, last = lanes == 0, lanes == DIP - 1
        strike = lax.broadcasted_iota(jnp.int32, (40, DIP), 0) + (s * HS - 16)
        valid = jnp.logical_and(strike >= 0, strike < NS * HS)

        def across(x):
            up, dn = rows_sums(x)
            left, right = lane_shifts(x)
            left, right = jnp.where(first, 0.0, left), jnp.where(last, 0.0, right)
            return 0.1 * ((up + dn) + (left + right))

        force = flat(p1w[...]) * (flat(qw[0]) + flat(qw[1]))
        d0 = jnp.where(valid, across(force) + force, 0.0)
        d1 = 0.2 * force
        e0 = jnp.where(valid, 0.2 * d1 + across(d0) + force, 0.0)
        e1 = jnp.where(valid, 0.2 * d1 + across(d1) + 0.2 * d0, 0.0)
        extra = (0.2 * e1 + across(e0) + force)[8:32]
        get_rows(r8_copies)
        opening = sign * (flat(r8[0]) - flat(r8[1])) + extra
        p2 = lubricate(
            opening, flat(p1w[1:4]), flat(plw[1:4, 1]), flat(plw[1:4, 2]), flat(plw[1:4, 3]), -8
        )
        p2 = shuffle(p2[8:16], back[...])
        for j in range(NJ):
            p2t[j] = p2[:, cols(j)]
        for i in range(NN // 2):
            shift = -(i % 4) * 32 % LANES
            tile = p2t[side * 2 + i // 4]
            e4s[i] = pltpu.roll(tile, shift, 1) if shift else tile
        for cond, copy in e4_copies:
            pl.when(cond)(copy.start)
        e4r[...] = e4s[jnp.where(is_b, 0, 7)]

    @pl.when(jnp.logical_not(is_i))
    def _():
        pltpu.make_async_remote_copy(
            src_ref=e4s.at[0], dst_ref=e4r, send_sem=e4_snd.at[0], recv_sem=e4_rcv,
            device_id=(s, NN - 1 - n), device_id_type=MESH,
        ).wait_recv()

    p_out[...] = e4r[...]

    for copy in copies_out:
        copy.wait()
    for group in msgs.values():
        for cond, snd, _ in group:
            pl.when(cond)(snd.wait_send)
    for cond, copy in gathers:
        pl.when(cond)(copy.wait_send)
    for cond, copy in e4_copies:
        pl.when(cond)(copy.wait_send)

    @pl.when(is_i)
    def _():
        for copies in (q_copies, w_copies, r4_copies, r8_copies):
            end_rows(copies)


def body(displacement, body_force, stiffness, aperture_base, contact_open, pressure_init, injection):
    vm = pl.BlockSpec(memory_space=pltpu.VMEM)
    hbm = pl.BlockSpec(memory_space=pl.ANY)
    dma = pltpu.SemaphoreType.DMA

    def buf(*shape):
        return pltpu.VMEM(shape, F32)

    scratch = [
        buf(2, 3, 2, 18, 24, DIP),
        buf(3, 18, HN, DIP),
        buf(HS, HN, DIP),
        buf(3, HS, HN, DIP),
        buf(3, HS, HN, DIP),
        buf(3, HS, HN, DIP),
        pltpu.VMEM((DIP, DIP), jnp.bfloat16),
        pltpu.VMEM((DIP, DIP), jnp.bfloat16),
        buf(8, DIP),
        buf(2, 3, 2, 4, HN, DIP),
        buf(2, 3, 2, 4, 8, DIP),
        buf(2, 3, 2, 4, 8, DIP),
        buf(2, 3, 2, 2, 8, DIP),
        buf(2, 3, 2, 2, 8, DIP),
        buf(8, LANES),
        buf(NN, 8, LANES),
        buf(5, 4, 8, DIP),
        buf(2, 5, 8, DIP),
        buf(2, 5, 8, DIP),
        buf(2, 3, 8, DIP),
        buf(3, 8, 32),
        pltpu.VMEM((8, 32), jnp.int32),
        buf(14, 8, DIP),
        buf(2, 14, 8, DIP),
        buf(HS, 8, DIP),
        buf(5, 8, DIP),
        buf(NJ, 8, LANES),
        buf(NN // 2, 8, LANES),
        buf(8, LANES),
        dma((11,)), dma((3,)),
        dma((2, 3, 2)), dma((2, 3, 2)), dma((2, 3, 2)), dma((2, 3, 2)),
        dma((2, 3, 2, 2)), dma((2, 3, 2, 2)),
        dma((2,)), dma,
        dma((2, 5)), dma((2, 5)), dma((5,)), dma((5,)), dma((2, 5)), dma((2, 5)), dma((2, 3)), dma((2, 3)),
        dma((NN // 2,)), dma,
    ]
    u, tile = pl.pallas_call(
        kernel,
        out_shape=(
            jax.ShapeDtypeStruct((3, HS, HN, DIP), F32),
            jax.ShapeDtypeStruct((8, LANES), F32),
        ),
        in_specs=[hbm] * 7,
        out_specs=(hbm, vm),
        scratch_shapes=scratch,
        compiler_params=pltpu.CompilerParams(
            collective_id=0, has_side_effects=True, vmem_limit_bytes=60 * 2**20
        ),
        cost_estimate=pl.CostEstimate(flops=60_000_000, bytes_accessed=2_700_000, transcendentals=40_000),
    )(displacement, body_force, stiffness, aperture_base, contact_open, pressure_init, injection)
    return u, tile[:, : HN * 2]


def solution(mesh):
    in_specs = (
        P(None, "strike", "normal", None),
        P(None, "strike", "normal", None),
        P("strike", "normal", None),
        P("strike", "normal"),
        P("strike", "normal"),
        P("strike", "normal"),
        P("strike", "normal"),
    )
    out_specs = (P(None, "strike", "normal", None), P("strike", "normal"))
    return jax.shard_map(body, mesh=mesh, in_specs=in_specs, out_specs=out_specs, check_vma=False)
```

```python
import jax
import jax.numpy as jnp
from jax import lax
from jax.experimental import pallas as pl
from jax.experimental.pallas import tpu as pltpu
from jax.sharding import PartitionSpec as P

MESH = pl.DeviceIdType.MESH
F32 = jnp.float32
NS, NN = 8, 16
HS, HN, DIP = 8, 16, 512
SW = 4
SW_L = 6
O = 5
LANES = 128
NJ = DIP // LANES
WAYS = (-1, 1)


def lane_pair(x, lane):
    left = [jnp.where(lane == 0, 0.0, pltpu.roll(x[-1], 1, 1))] + x[:-1]
    right = x[1:] + [jnp.where(lane == LANES - 1, 0.0, pltpu.roll(x[0], LANES - 1, 1))]
    return left, right


def cols(j):
    return slice(j * LANES, (j + 1) * LANES)


def lane_shifts(x):
    cut = DIP - LANES
    left = jnp.concatenate([pltpu.roll(x[:, cut:], 1, 1), x[:, :cut]], axis=1)
    right = jnp.concatenate([x[:, LANES:], pltpu.roll(x[:, :LANES], LANES - 1, 1)], axis=1)
    return left, right


def shuffle(x, matrix):
    high = x.astype(jnp.bfloat16)
    rest = x - high.astype(F32)
    mid = rest.astype(jnp.bfloat16)
    low = (rest - mid.astype(F32)).astype(jnp.bfloat16)
    out = [jnp.dot(part, matrix, preferred_element_type=F32) for part in (high, mid, low)]
    return out[0] + (out[1] + out[2])


def rows_sums(x):
    count = x.shape[0]
    return pltpu.roll(x, 1, 0), pltpu.roll(x, count - 1, 0)


def kernel(
    u_in, f_in, st_in, ap_hbm, ct_hbm, p_hbm, inj_hbm,
    u_out, p_out,
    xb, gb, st, outb, us, fs, into, back, row, rs, rn, sn, rc, sc, pk, gath, plw, qx, eb, eg, ea, ra, sw, c4w, c8w, small, ct_v, tt, tx, corr, p1w, p2t, e4s, e4r,
    in_sem, out_sem, s_snd, s_rcv, n_snd, n_rcv, c_snd, c_rcv, g_snd, g_rcv,
    q_snd, q_rcv, w_snd, w_rcv, a_snd, a_rcv, b_snd, b_rcv, e4_snd, e4_rcv,
):
    s = lax.axis_index("strike")
    n = lax.axis_index("normal")
    is_a = n == NN // 2 - 1
    is_b = n == NN // 2
    is_i = jnp.logical_or(is_a, is_b)
    side = jnp.where(n >= NN // 2, 1, 0)
    has_s = {-1: s > 0, 1: s < NS - 1}
    has_n = {-1: n > 0, 1: n < NN - 1}
    lane = lax.broadcasted_iota(jnp.int32, (8, LANES), 1)
    sub = lax.broadcasted_iota(jnp.int32, (8, LANES), 0)
    sub5 = lax.broadcasted_iota(jnp.int32, (8, DIP), 0)

    order = (1, 0, 2)
    loads = {"st": pltpu.make_async_copy(st_in, st, in_sem.at[6])}
    for c in range(3):
        loads["u", c] = pltpu.make_async_copy(
            u_in.at[c], us.at[c], in_sem.at[c]
        )
        loads["f", c] = pltpu.make_async_copy(f_in.at[c], fs.at[c], in_sem.at[3 + c])
    for k, ref in enumerate((p_hbm, ap_hbm, inj_hbm)):
        loads["small", k] = pltpu.make_async_copy(ref, small.at[k], in_sem.at[7 + k])
        loads["small", k].start()
    loads["ct"] = pltpu.make_async_copy(ct_hbm, ct_v, in_sem.at[10])
    loads["ct"].start()
    loads["st"].start()
    for c in order:
        loads["f", c].start()
        loads["u", c].start()

    barrier = pltpu.get_barrier_semaphore()
    count = jnp.int32(0)

    def greet(cond, target):
        @pl.when(cond)
        def _():
            pl.semaphore_signal(barrier, inc=1, device_id=target, device_id_type=MESH)

        return jnp.where(cond, 1, 0)

    for a in WAYS:
        count += greet(has_s[a], (s + a, n))
        count += greet(has_n[a], (s, n + a))
        for b in WAYS:
            count += greet(jnp.logical_and(has_s[a], has_n[b]), (s + a, n + b))
    for mid in (NN // 2 - 1, NN // 2):
        count += greet(n != mid, (s, mid))
    for other in range(NN):
        count += greet(jnp.logical_and(is_i, n != other), (s, other))

    def near(d):
        return jnp.logical_and(s + d >= 0, s + d <= NS - 1)

    for d in (-3, -2, 2, 3):
        count += greet(jnp.logical_and(is_i, near(d)), (s + d, n))

    zrow = jnp.zeros((24, DIP), F32)

    def clear(i, carry):
        at = jnp.where(i < O, i, i + HS)
        for c in range(3):
            for rd in range(2):
                for pp in range(2):
                    xb[rd, c, pp, at] = zrow
            gb[c, at] = jnp.zeros((HN, DIP), F32)
        return carry

    lax.fori_loop(0, 10, clear, 0)

    def clear_own(i, carry):
        for c in range(3):
            for rd in range(2):
                xb[rd, c, 0, O + i, pl.ds(16, 8), :] = jnp.zeros((8, DIP), F32)
        return carry

    lax.fori_loop(0, HS, clear_own, 0)

    d0 = lax.broadcasted_iota(jnp.int32, (DIP, DIP), 0)
    d1 = lax.broadcasted_iota(jnp.int32, (DIP, DIP), 1)
    into[...] = jnp.where(d0 == 4 * (d1 % LANES) + d1 // LANES, 1.0, 0.0).astype(jnp.bfloat16)
    back[...] = jnp.where(d1 == 4 * (d0 % LANES) + d0 // LANES, 1.0, 0.0).astype(jnp.bfloat16)

    for a, w in ((-1, 0), (1, 1)):
        @pl.when(jnp.logical_not(has_s[a]))
        def _():
            rs[:, :, w] = jnp.zeros((2, 3, 4, HN, DIP), F32)

        @pl.when(jnp.logical_not(has_n[a]))
        def _():
            rn[:, :, w] = jnp.zeros((2, 3, 4, 8, DIP), F32)

        for b, v in ((-1, 0), (1, 1)):
            @pl.when(jnp.logical_not(jnp.logical_and(has_s[a], has_n[b])))
            def _():
                rc[:, :, w, v] = jnp.zeros((2, 3, 8, DIP), F32)

    @pl.when(is_i)
    def _():
        tx[...] = jnp.zeros_like(tx)
        eb[...] = jnp.zeros_like(eb)
        eg[...] = jnp.zeros_like(eg)
        for d in range(-3, 4):
            @pl.when(jnp.logical_not(near(d)))
            def _():
                plw[d + 3] = jnp.zeros((6, 8, DIP), F32)
                if -2 <= d <= 2:
                    sw[d + 2] = jnp.zeros((2, 8, DIP), F32)
                if -1 <= d <= 1:
                    ra[:, d + 1] = jnp.zeros((2, 2, 8, DIP), F32)

    loads["st"].wait()

    def recip(i, carry):
        st[i] = 0.1 / st[i]
        return carry

    lax.fori_loop(0, HS, recip, 0)

    @pl.when(is_a)
    def _():
        for i in range(HS):
            row[i : i + 1, :] = 0.5 * st[i, HN - 1 : HN, :]

    @pl.when(is_b)
    def _():
        for i in range(HS):
            row[i : i + 1, :] = 0.5 * st[i, 0:1, :]

    @pl.when(is_i)
    def _():
        qx[0] = shuffle(row[...], into[...])


    gathers = []
    for k, mid in enumerate((NN // 2 - 1, NN // 2)):
        gathers.append(
            (
                n != mid,
                pltpu.make_async_remote_copy(
                    src_ref=pk, dst_ref=gath.at[n], send_sem=g_snd.at[k], recv_sem=g_rcv,
                    device_id=(s, mid), device_id_type=MESH,
                ),
            )
        )

    q_copy = pltpu.make_async_remote_copy(
        src_ref=qx.at[0], dst_ref=qx.at[1], send_sem=q_snd, recv_sem=q_rcv,
        device_id=(s, NN - 1 - n), device_id_type=MESH,
    )

    def pair_of(src, dst_there, dst_here, snd, rcv_there, rcv_here, target):
        return [
            pltpu.make_async_remote_copy(
                src_ref=src, dst_ref=dst, send_sem=snd, recv_sem=rcv, device_id=target, device_id_type=MESH
            )
            for dst, rcv in ((dst_there, rcv_there), (dst_here, rcv_here))
        ]

    a_copies, b_copies, w_copies = [], [], []
    for d in (-1, 1, 0):
        for rel in range(2):
            if d == 0 and rel == 0:
                continue
            a_copies.append(
                [near(d)] + pair_of(
                    ea.at[1 + d], ra.at[rel, 1 - d], ra.at[rel, 1 + d], a_snd.at[rel, 1 + d],
                    a_rcv.at[rel, 1 - d], a_rcv.at[rel, 1 + d], (s + d, n if rel == 0 else NN - 1 - n),
                )
            )
    for d in (-2, 2, -1, 1):
        b_copies.append(
            [near(d)] + pair_of(
                sw.at[2], sw.at[2 - d], sw.at[2 + d], b_snd.at[2 + d], b_rcv.at[2 - d], b_rcv.at[2 + d], (s + d, n)
            )
        )
    for d, kinds in ((-3, 2), (3, 2), (-2, 5), (2, 5), (-1, 6), (1, 6)):
        part = pl.ds(0, kinds)
        w_copies.append(
            [near(d)] + pair_of(
                plw.at[3, part], plw.at[3 - d, part], plw.at[3 + d, part], w_snd.at[3 + d],
                w_rcv.at[3 - d], w_rcv.at[3 + d], (s + d, n),
            )
        )

    def send_all(copies):
        for cond, snd, _ in copies:
            pl.when(cond)(snd.start)

    def get_all(copies):
        for cond, _, rcv in copies:
            pl.when(cond)(rcv.wait_recv)

    def end_all(copies):
        for cond, snd, _ in copies:
            pl.when(cond)(snd.wait_send)

    keep_hi = jnp.logical_or(has_n[1], sub >= 4)
    keep_lo = jnp.logical_or(has_n[-1], sub < 4)
    keep = jnp.logical_and(keep_hi, keep_lo)

    def sweeps(rd, c):
        def sweep(k, carry):
            src = lax.rem(k - 1, 2)
            dst = lax.rem(k, 2)

            def get(i):
                return [[xb[rd, c, src, i, t * 8 : t * 8 + 8, cols(j)] for j in range(NJ)] for t in range(3)]

            def pair(m, inner):
                base = O - k - lax.rem(k, 2) + 4 * m
                rows = [get(base - 1 + r) for r in range(4 + 2)]
                vals = {}
                for r in range(4):
                    i = base + r
                    xm, x, xp = rows[r : r + 3]
                    ok = jnp.logical_and(
                        jnp.logical_or(has_s[-1], i >= O), jnp.logical_or(has_s[1], i < O + HS)
                    )
                    one, two = jnp.where(ok, 0.1, 0.0), jnp.where(ok, 0.2, 0.0)
                    up = [[pltpu.roll(v, 1, 0) for v in q] for q in x]
                    dn = [[pltpu.roll(v, 7, 0) for v in q] for q in x]
                    for t in range(3):
                        left, right = lane_pair(x[t], lane)
                        for j in range(NJ):
                            sy = jnp.where(sub == 0, up[(t + 2) % 3][j], up[t][j]) + jnp.where(
                                sub == 7, dn[(t + 1) % 3][j], dn[t][j]
                            )
                            sx = xm[t][j] + xp[t][j]
                            sz = left[j] + right[j]
                            if c == 0:
                                val = two * (x[t][j] + sx) + one * (sy + sz)
                            elif c == 1:
                                val = two * (x[t][j] + sy) + one * (sx + sz)
                            else:
                                val = two * (x[t][j] + sz) + one * (sx + sy)
                            if t < 2:
                                val = val + gb[c, i, t * 8 : t * 8 + 8, cols(j)]
                            else:
                                val = jnp.where(keep, val, 0.0)
                            vals[r, t, j] = val
                for (r, t, j), val in vals.items():
                    xb[rd, c, dst, base + r, t * 8 : t * 8 + 8, cols(j)] = val
                return inner

            lax.fori_loop(0, (HS + 2 * k + 3) // 4, pair, 0)
            return carry

        lax.fori_loop(1, SW + 1, sweep, 0)

    def messages(rd, c):
        out = []
        for a, w in ((-1, 0), (1, 1)):
            first = 1 if a < 0 else O + HS
            out.append(
                (
                    has_s[a],
                    pltpu.make_async_remote_copy(
                        src_ref=xb.at[rd, c, 0, pl.ds(first, 4), pl.ds(0, HN)], dst_ref=rs.at[rd, c, 1 - w],
                        send_sem=s_snd.at[rd, c, w], recv_sem=s_rcv.at[rd, c, 1 - w],
                        device_id=(s + a, n), device_id_type=MESH,
                    ),
                    pltpu.make_async_remote_copy(
                        src_ref=rs.at[rd, c, w], dst_ref=rs.at[rd, c, w],
                        send_sem=s_snd.at[rd, c, w], recv_sem=s_rcv.at[rd, c, w],
                        device_id=(s + a, n), device_id_type=MESH,
                    ),
                )
            )
        for b, v in ((-1, 0), (1, 1)):
            out.append(
                (
                    has_n[b],
                    pltpu.make_async_remote_copy(
                        src_ref=sn.at[rd, c, v], dst_ref=rn.at[rd, c, 1 - v],
                        send_sem=n_snd.at[rd, c, v], recv_sem=n_rcv.at[rd, c, 1 - v],
                        device_id=(s, n + b), device_id_type=MESH,
                    ),
                    pltpu.make_async_remote_copy(
                        src_ref=sn.at[rd, c, v], dst_ref=rn.at[rd, c, v],
                        send_sem=n_snd.at[rd, c, v], recv_sem=n_rcv.at[rd, c, v],
                        device_id=(s, n + b), device_id_type=MESH,
                    ),
                )
            )
        for a, w in ((-1, 0), (1, 1)):
            for b, v in ((-1, 0), (1, 1)):
                out.append(
                    (
                        jnp.logical_and(has_s[a], has_n[b]),
                        pltpu.make_async_remote_copy(
                            src_ref=sc.at[rd, c, w, v], dst_ref=rc.at[rd, c, 1 - w, 1 - v],
                            send_sem=c_snd.at[rd, c, w, v], recv_sem=c_rcv.at[rd, c, 1 - w, 1 - v],
                            device_id=(s + a, n + b), device_id_type=MESH,
                        ),
                        pltpu.make_async_remote_copy(
                            src_ref=sc.at[rd, c, w, v], dst_ref=rc.at[rd, c, w, v],
                            send_sem=c_snd.at[rd, c, w, v], recv_sem=c_rcv.at[rd, c, w, v],
                            device_id=(s + a, n + b), device_id_type=MESH,
                        ),
                    )
                )
        return out

    msgs = {(rd, c): messages(rd, c) for rd in range(2) for c in range(3)}
    r4sub = sub5 < 4

    def ghost(rd, c, i):
        return xb[rd, c, 0, i, 16:24, :]

    def send(rd, c):
        group = msgs[rd, c]
        for cond, snd, _ in group[:2]:
            pl.when(cond)(snd.start)
        for w in range(2):
            g = [ghost(rd, c, O - d if w == 0 else O + HS - 1 + d) for d in (1, 2, 3)]
            sc[rd, c, w, 1] = jnp.where(
                r4sub, g[0], jnp.where(sub5 < 6, pltpu.roll(g[1], 4, 0), pltpu.roll(g[2], 6, 0))
            )
            sc[rd, c, w, 0] = jnp.where(
                r4sub, jnp.where(sub5 >= 2, pltpu.roll(g[1], 4, 0), pltpu.roll(g[2], 2, 0)), g[0]
            )
        for cond, snd, _ in group[4:]:
            pl.when(cond)(snd.start)
        for t in range(4):
            first, second = ghost(rd, c, O + t), ghost(rd, c, O + t + 4)
            sn[rd, c, 1, t] = jnp.where(r4sub, first, pltpu.roll(second, 4, 0))
            sn[rd, c, 0, t] = jnp.where(r4sub, pltpu.roll(first, 4, 0), second)
        for cond, snd, _ in group[2:4]:
            pl.when(cond)(snd.start)

    def merge(rd, c, store):
        for cond, _, rcv in msgs[rd, c]:
            pl.when(cond)(rcv.wait_recv)
        for i in range(HS):
            t = i % 4
            low = xb[rd, c, 0, O + i, 0:8, :]
            high = xb[rd, c, 0, O + i, 8:16, :]
            way = 0 if i < 4 else 1
            low = low + rs[rd, c, way, t, 0:8, :]
            high = high + rs[rd, c, way, t, 8:16, :]
            from_lo, from_hi = rn[rd, c, 0, t], rn[rd, c, 1, t]
            if i < 4:
                from_hi = pltpu.roll(from_hi, 4, 0)
            else:
                from_lo = pltpu.roll(from_lo, 4, 0)
            low = low + jnp.where(r4sub, from_lo, 0.0)
            high = high + jnp.where(r4sub, 0.0, from_hi)
            d = i + 1 if i < 4 else HS - i
            if d <= 3:
                corner_lo, corner_hi = rc[rd, c, way, 0], rc[rd, c, way, 1]
                if d == 1:
                    low = low + jnp.where(r4sub, corner_lo, 0.0)
                    high = high + jnp.where(r4sub, 0.0, corner_hi)
                elif d == 2:
                    low = low + jnp.where(sub5 < 2, pltpu.roll(corner_lo, 4, 0), 0.0)
                    high = high + jnp.where(sub5 >= 6, pltpu.roll(corner_hi, 4, 0), 0.0)
                else:
                    low = low + jnp.where(sub5 < 2, pltpu.roll(corner_lo, 2, 0), 0.0)
                    high = high + jnp.where(sub5 >= 6, pltpu.roll(corner_hi, 6, 0), 0.0)
            store(i, low, high)

    def traction(p_of, q_of):
        for r in range(-3, HS + 3):
            p_row = p_of(r)
            own = p_row * q_of(0, r)
            far = p_row * q_of(1, r)
            below = jnp.where(is_b, far, own)
            above = jnp.where(is_b, own, far)
            tt[r + 3] = jnp.where(sub5 == 3, -below, jnp.where(sub5 == 4, above, 0.0))

        def tile_sweep(src, dst, first, trips, shift):
            def four(m, carry):
                base = first + 4 * m
                rows = [[src[base - 1 + r, :, cols(j)] for j in range(NJ)] for r in range(6)]
                vals = {}
                for r in range(4):
                    i = base + r
                    xm, x, xp = rows[r : r + 3]
                    ok = jnp.logical_and(
                        jnp.logical_or(has_s[-1], i >= 3), jnp.logical_or(has_s[1], i < 3 + HS)
                    )
                    one, two = jnp.where(ok, 0.1, 0.0), jnp.where(ok, 0.2, 0.0)
                    left, right = lane_pair(x, lane)
                    for j in range(NJ):
                        sy = pltpu.roll(x[j], 1, 0) + pltpu.roll(x[j], 7, 0)
                        vals[r, j] = (
                            two * (x[j] + sy) + one * ((xm[j] + xp[j]) + (left[j] + right[j]))
                            + tt[i, :, cols(j)]
                        )
                for (r, j), val in vals.items():
                    dst[base + r - shift, :, cols(j)] = val
                return carry

            lax.fori_loop(0, trips, four, 0)

        tile_sweep(tt, tx.at[0], 1, 3, 0)
        tile_sweep(tx.at[0], tx.at[1], 1, 3, 0)
        tile_sweep(tx.at[1], corr, 3, 2, 3)

    def win_row(ref, r, half):
        j, i = divmod(r + 8 * half, 8)
        return ref(j)[i : i + 1, :]

    def q_row(rel, r):
        own = win_row(lambda j: plw[j, 5], r, 3)
        return own if rel == 0 else win_row(lambda j: plw[j, 1], r, 3) - own

    def lubricate(opening, p, ap, ct, inj, first_row):
        rows = opening.shape[0]
        lanes = lax.broadcasted_iota(jnp.int32, (rows, DIP), 1)
        first, last = lanes == 0, lanes == DIP - 1
        strike = lax.broadcasted_iota(jnp.int32, (rows, DIP), 0) + (s * HS + first_row)
        valid = jnp.logical_and(strike >= 0, strike < NS * HS)
        soft = jnp.maximum(opening, 0.0) + jnp.log1p(jnp.exp(-jnp.abs(opening)))
        width = ap + soft
        k = ct * (width * width * width) / 12.0
        base = 0.5 * p - opening + inj
        k_up, k_dn = rows_sums(k)
        k_l, k_r = lane_shifts(k)
        k_l, k_r = jnp.where(first, 0.0, k_l), jnp.where(last, 0.0, k_r)
        f_up, f_dn, f_l, f_r = [0.5 * (k + v) for v in (k_up, k_dn, k_l, k_r)]
        rden = jnp.where(valid, 1.0 / (0.5 + (f_up + f_dn + f_l + f_r)), 0.0)
        base = base * rden
        f_up, f_dn = f_up * rden, f_dn * rden
        f_l = jnp.where(first, 0.0, f_l * rden)
        f_r = jnp.where(last, 0.0, f_r * rden)
        for _ in range(SW_L):
            p_up, p_dn = rows_sums(p)
            p_l, p_r = lane_shifts(p)
            p = (base + (f_up * p_up + f_dn * p_dn)) + (f_l * p_l + f_r * p_r)
        return p

    sign = jnp.where(is_b, 1.0, -1.0)

    def antisymmetric():
        near_row = pl.multiple_of(jnp.where(is_b, 0, 8), 8)
        far_row = pl.multiple_of(jnp.where(is_b, 8, 0), 8)
        c_up, c_dn = jnp.where(is_b, -1.0, 0.0), jnp.where(is_b, 0.0, -1.0)
        for i in range(HS):
            eb[0, 9 + i] = xb[0, 1, 0, O + i, pl.ds(near_row, 8), :]
            eg[9 + i] = gb[1, O + i, pl.ds(near_row, 8), :]

        def sweep(k, carry):
            src, dst = lax.rem(k - 1, 2), lax.rem(k, 2)

            def four(m, inner):
                base = jnp.where(k <= 4, 5, 1) + 8 * m
                rows = [[eb[src, base - 1 + r, :, cols(j)] for j in range(NJ)] for r in range(10)]
                vals = {}
                for r in range(8):
                    i = base + r
                    xm, x, xp = rows[r : r + 3]
                    ok = jnp.logical_and(
                        jnp.logical_or(has_s[-1], i >= 9), jnp.logical_or(has_s[1], i < 9 + HS)
                    )
                    one, two = jnp.where(ok, 0.1, 0.0), jnp.where(ok, 0.2, 0.0)
                    left, right = lane_pair(x, lane)
                    for j in range(NJ):
                        up = jnp.where(sub == 0, c_up * x[j], pltpu.roll(x[j], 1, 0))
                        dn = jnp.where(sub == 7, c_dn * x[j], pltpu.roll(x[j], 7, 0))
                        vals[r, j] = (
                            two * (x[j] + (up + dn)) + one * ((xm[j] + xp[j]) + (left[j] + right[j]))
                            + eg[i, :, cols(j)]
                        )
                for (r, j), val in vals.items():
                    eb[dst, base + r, :, cols(j)] = val
                return inner

            lax.fori_loop(0, jnp.where(k <= 4, 2, 3), four, 0)
            return carry

        def take(e):
            for cond, row_at in ((is_a, 7), (is_b, 0)):
                @pl.when(cond)
                def _():
                    for i in range(24):
                        ea[i // 8, e, i % 8 : i % 8 + 1, :] = eb[0, 1 + i, row_at : row_at + 1, :]

        lax.fori_loop(1, 2, sweep, 0)
        for i in range(HS):
            far = xb[0, 1, 0, O + i, pl.ds(far_row, 8), :]
            from_far = jnp.where(is_b, pltpu.roll(far, 7, 0), pltpu.roll(far, 1, 0))
            eb[1, 9 + i] = eb[1, 9 + i] + jnp.where(sub5 == jnp.where(is_b, 7, 0), 0.2 * from_far, 0.0)
        lax.fori_loop(2, 5, sweep, 0)
        take(0)
        lax.fori_loop(5, 9, sweep, 0)
        take(1)
        ra[0, 1] = ea[1]

    def flat(x):
        return x.reshape(x.shape[0] * 8, DIP)

    def spread(rows, first_row):
        lanes = lax.broadcasted_iota(jnp.int32, (rows, DIP), 1)
        first, last = lanes == 0, lanes == DIP - 1
        strike = lax.broadcasted_iota(jnp.int32, (rows, DIP), 0) + (s * HS + first_row)
        valid = jnp.logical_and(strike >= 0, strike < NS * HS)

        def across(x):
            up, dn = rows_sums(x)
            left, right = lane_shifts(x)
            left, right = jnp.where(first, 0.0, left), jnp.where(last, 0.0, right)
            return 0.1 * ((up + dn) + (left + right))

        return across, valid

    def layers(d, force, k, across, valid):
        out = []
        for m in range(min(k, 9 - k)):
            here = d[m] if m < len(d) else None
            val = None
            if here is not None:
                val = across(here)
                if m > 0:
                    val = val + 0.2 * here
            if m + 1 < len(d):
                val = val + 0.2 * d[m + 1]
            if m > 0:
                below = 0.2 * d[m - 1]
                val = below if val is None else val + below
            if m == 0 and force is not None:
                val = force if val is None else val + force
            out.append(jnp.where(valid, val, 0.0))
        return out

    def early():
        across, valid = spread(56, -24)
        force = flat(plw[:, 0]) * flat(plw[:, 1])
        d = [force]
        for k in range(2, 5):
            d = layers(d, force, k, across, valid)
        d = [x[8:48] for x in d]
        c4w[...] = d[0].reshape(5, 8, DIP)
        across, valid = spread(40, -16)
        for k in range(5, 9):
            d = layers(d, None, k, across, valid)
        c8w[...] = d[0][8:32].reshape(3, 8, DIP)

    def ready(c):
        loads["f", c].wait()
        gb[c, pl.ds(O, HS)] = shuffle((fs[c] * st[...]).reshape(HS * HN, DIP), into[...]).reshape(HS, HN, DIP)
        loads["u", c].wait()
        xb[0, c, 0, pl.ds(O, HS), pl.ds(0, HN)] = shuffle(us[c].reshape(HS * HN, DIP), into[...]).reshape(HS, HN, DIP)

    for k in range(3):
        loads["small", k].wait()
    loads["ct"].wait()
    pk[...] = jnp.concatenate([small[0], small[1], ct_v[...].astype(F32), small[2]], axis=1)

    def unpack():
        @pl.when(is_i)
        def _():
            gath[n] = pk[...]
            pltpu.make_async_copy(gath.at[pl.ds(0, NN - 1)], gath.at[pl.ds(0, NN - 1)], g_rcv).wait()
            for big in range(NJ):
                tiles = [gath[big * 4 + m] for m in range(4)]
                for kind, place in enumerate((0, 2, 3, 4)):
                    val = None
                    for m in range(4):
                        shift = (m - kind) % 4 * 32
                        piece = pltpu.roll(tiles[m], shift, 1) if shift else tiles[m]
                        val = piece if val is None else jnp.where(lane >= 32 * m, piece, val)
                    plw[3, place, :, cols(big)] = val
            both = shuffle(jnp.concatenate([plw[3, 0], plw[3, 2], plw[3, 3], plw[3, 4]], axis=0), into[...])
            for m, place in enumerate((0, 2, 3, 4)):
                plw[3, place] = both[8 * m : 8 * m + 8]
            q_copy.wait_recv()
            plw[3, 1] = qx[0] + qx[1]
            plw[3, 5] = qx[0]
            send_all(w_copies)

    def total():
        @pl.when(is_i)
        def _():
            get_all(a_copies)
            for e in range(2):
                own = ra[0, 0, e] + ra[0, 1, e] + ra[0, 2, e]
                sw[2, e] = sign * (own - (ra[1, 0, e] + ra[1, 1, e] + ra[1, 2, e]))
            send_all(b_copies)

    def pressed():
        @pl.when(is_i)
        def _():
            get_all(w_copies)
            traction(lambda r: win_row(lambda j: plw[j, 0], r, 3), q_row)
            early()

    sign = jnp.where(is_b, 1.0, -1.0)

    def to_second(c):
        def store(i, low, high):
            xb[1, c, 0, O + i, 0:8, :] = low
            xb[1, c, 0, O + i, 8:16, :] = high

        return store

    def to_out(c):
        def store(i, low, high):
            outb[c, i, 0:8, :] = low
            outb[c, i, 8:16, :] = high

        return store

    def own_tile(get, put):
        @pl.when(is_a)
        def _():
            for i in range(HS):
                put(i, 8, get(i, 8) + jnp.where(r4sub, 0.0, pltpu.roll(corr[i], 4, 0)))

        @pl.when(is_b)
        def _():
            for i in range(HS):
                put(i, 0, get(i, 0) + jnp.where(r4sub, pltpu.roll(corr[i], 4, 0), 0.0))

    def put_second(i, r, v):
        xb[1, 1, 0, O + i, r : r + 8, :] = v

    def put_out(i, r, v):
        outb[1, i, r : r + 8, :] = v

    e4_copies = []
    for i in range(NN // 2):
        e4_copies.append(
            (
                jnp.logical_and(is_i, n != side * 8 + i),
                pltpu.make_async_remote_copy(
                    src_ref=e4s.at[i], dst_ref=e4r, send_sem=e4_snd.at[i], recv_sem=e4_rcv,
                    device_id=(s, side * 8 + i), device_id_type=MESH,
                ),
            )
        )

    def plane():
        @pl.when(is_i)
        def _():
            get_all(b_copies)
            p1 = lubricate(
                flat(sw[:, 0]) + flat(c4w[...]), *[flat(plw[1:6, kind]) for kind in (0, 2, 3, 4)], -16
            )
            p1w[...] = p1.reshape(5, 8, DIP)
            across, valid = spread(40, -16)
            force = p1 * flat(plw[1:6, 1])
            d = layers([force], force, 2, across, valid)
            d = layers(d, force, 6 + 1, across, valid)
            d = layers(d, force, 8, across, valid)
            opening = (flat(sw[1:4, 1]) + flat(c8w[...])) + d[0][8:32]
            p2 = lubricate(opening, p1[8:32], *[flat(plw[2:5, kind]) for kind in (2, 3, 4)], -8)
            p2 = shuffle(p2[8:16], back[...])
            for j in range(NJ):
                p2t[j] = p2[:, cols(j)]
            for i in range(NN // 2):
                shift = -(i % 4) * 32 % LANES
                tile = p2t[side * 2 + i // 4]
                e4s[i] = pltpu.roll(tile, shift, 1) if shift else tile
            for cond, copy in e4_copies:
                pl.when(cond)(copy.start)
            e4r[...] = e4s[jnp.where(is_b, 0, 7)]
            traction(lambda r: win_row(lambda j: p1w[j], r, 2), q_row)

    def start():
        ready(1)
        pl.semaphore_wait(barrier, count)
        for cond, copy in gathers:
            pl.when(cond)(copy.start)
        pl.when(is_i)(q_copy.start)

    def ahead():
        @pl.when(is_i)
        def _():
            antisymmetric()
            send_all(a_copies)

    def one(c):
        if c != 1:
            ready(c)
        sweeps(0, c)
        send(0, c)

    def two(c):
        merge(0, c, to_second(c))
        if c == 1:
            own_tile(lambda i, r: xb[1, 1, 0, O + i, r : r + 8, :], put_second)
        sweeps(1, c)
        send(1, c)

    copies_out = [pltpu.make_async_copy(outb.at[c], u_out.at[c], out_sem.at[c]) for c in range(3)]
    def last(c):
        merge(1, c, to_out(c))
        if c == 1:
            own_tile(lambda i, r: outb[1, i, r : r + 8, :], put_out)
        outb[c] = shuffle(outb[c].reshape(HS * HN, DIP), back[...]).reshape(HS, HN, DIP)
        copies_out[c].start()

    start()
    ahead()
    one(0)
    one(2)
    unpack()
    one(1)
    total()
    two(0)
    two(2)
    pressed()
    two(1)
    plane()
    last(0)
    last(2)
    last(1)

    @pl.when(jnp.logical_not(is_i))
    def _():
        pltpu.make_async_remote_copy(
            src_ref=e4s.at[0], dst_ref=e4r, send_sem=e4_snd.at[0], recv_sem=e4_rcv,
            device_id=(s, NN - 1 - n), device_id_type=MESH,
        ).wait_recv()

    p_out[...] = e4r[...]

    for copy in copies_out:
        copy.wait()
    for group in msgs.values():
        for cond, snd, _ in group:
            pl.when(cond)(snd.wait_send)
    for cond, copy in gathers:
        pl.when(cond)(copy.wait_send)
    for cond, copy in e4_copies:
        pl.when(cond)(copy.wait_send)

    @pl.when(is_i)
    def _():
        q_copy.wait_send()
        for copies in (a_copies, b_copies, w_copies):
            end_all(copies)


def body(displacement, body_force, stiffness, aperture_base, contact_open, pressure_init, injection):
    vm = pl.BlockSpec(memory_space=pltpu.VMEM)
    hbm = pl.BlockSpec(memory_space=pl.ANY)
    dma = pltpu.SemaphoreType.DMA

    def buf(*shape):
        return pltpu.VMEM(shape, F32)

    scratch = [
        buf(2, 3, 2, 18, 24, DIP),
        buf(3, 18, HN, DIP),
        buf(HS, HN, DIP),
        buf(3, HS, HN, DIP),
        buf(3, HS, HN, DIP),
        buf(3, HS, HN, DIP),
        pltpu.VMEM((DIP, DIP), jnp.bfloat16),
        pltpu.VMEM((DIP, DIP), jnp.bfloat16),
        buf(8, DIP),
        buf(2, 3, 2, 4, HN, DIP),
        buf(2, 3, 2, 4, 8, DIP),
        buf(2, 3, 2, 4, 8, DIP),
        buf(2, 3, 2, 2, 8, DIP),
        buf(2, 3, 2, 2, 8, DIP),
        buf(8, LANES),
        buf(NN, 8, LANES),
        buf(7, 6, 8, DIP),
        buf(2, 8, DIP),
        buf(2, 26, 8, DIP),
        buf(26, 8, DIP),
        buf(3, 2, 8, DIP),
        buf(2, 3, 2, 8, DIP),
        buf(5, 2, 8, DIP),
        buf(5, 8, DIP),
        buf(3, 8, DIP),
        buf(3, 8, 32),
        pltpu.VMEM((8, 32), jnp.int32),
        buf(14, 8, DIP),
        buf(2, 14, 8, DIP),
        buf(HS, 8, DIP),
        buf(5, 8, DIP),
        buf(NJ, 8, LANES),
        buf(NN // 2, 8, LANES),
        buf(8, LANES),
        dma((11,)), dma((3,)),
        dma((2, 3, 2)), dma((2, 3, 2)), dma((2, 3, 2)), dma((2, 3, 2)),
        dma((2, 3, 2, 2)), dma((2, 3, 2, 2)),
        dma((2,)), dma,
        dma, dma, dma((7,)), dma((7,)), dma((2, 3)), dma((2, 3)), dma((5,)), dma((5,)),
        dma((NN // 2,)), dma,
    ]
    u, tile = pl.pallas_call(
        kernel,
        out_shape=(
            jax.ShapeDtypeStruct((3, HS, HN, DIP), F32),
            jax.ShapeDtypeStruct((8, LANES), F32),
        ),
        in_specs=[hbm] * 7,
        out_specs=(hbm, vm),
        scratch_shapes=scratch,
        compiler_params=pltpu.CompilerParams(
            collective_id=0, has_side_effects=True, vmem_limit_bytes=60 * 2**20
        ),
        cost_estimate=pl.CostEstimate(flops=60_000_000, bytes_accessed=2_700_000, transcendentals=40_000),
    )(displacement, body_force, stiffness, aperture_base, contact_open, pressure_init, injection)
    return u, tile[:, : HN * 2]


def solution(mesh):
    in_specs = (
        P(None, "strike", "normal", None),
        P(None, "strike", "normal", None),
        P("strike", "normal", None),
        P("strike", "normal"),
        P("strike", "normal"),
        P("strike", "normal"),
        P("strike", "normal"),
    )
    out_specs = (P(None, "strike", "normal", None), P("strike", "normal"))
    return jax.shard_map(body, mesh=mesh, in_specs=in_specs, out_specs=out_specs, check_vma=False)
```

```python
import jax
import jax.numpy as jnp
from jax import lax
from jax.experimental import pallas as pl
from jax.experimental.pallas import tpu as pltpu
from jax.sharding import PartitionSpec as P

MESH = pl.DeviceIdType.MESH
F32 = jnp.float32
NS, NN = 8, 16
HS, HN, DIP = 8, 16, 512
SW = 4
SW_L = 6
O = 5
LANES = 128
NJ = DIP // LANES
WAYS = (-1, 1)


def lane_pair(x, lane):
    left = [jnp.where(lane == 0, 0.0, pltpu.roll(x[-1], 1, 1))] + x[:-1]
    right = x[1:] + [jnp.where(lane == LANES - 1, 0.0, pltpu.roll(x[0], LANES - 1, 1))]
    return left, right


def cols(j):
    return slice(j * LANES, (j + 1) * LANES)


def lane_shifts(x):
    cut = DIP - LANES
    left = jnp.concatenate([pltpu.roll(x[:, cut:], 1, 1), x[:, :cut]], axis=1)
    right = jnp.concatenate([x[:, LANES:], pltpu.roll(x[:, :LANES], LANES - 1, 1)], axis=1)
    return left, right


def shuffle(x, matrix):
    high = x.astype(jnp.bfloat16)
    rest = x - high.astype(F32)
    mid = rest.astype(jnp.bfloat16)
    low = (rest - mid.astype(F32)).astype(jnp.bfloat16)
    out = [jnp.dot(part, matrix, preferred_element_type=F32) for part in (high, mid, low)]
    return out[0] + (out[1] + out[2])


def rows_sums(x):
    count = x.shape[0]
    return pltpu.roll(x, 1, 0), pltpu.roll(x, count - 1, 0)


def kernel(
    u_in, f_in, st_in, ap_hbm, ct_hbm, p_hbm, inj_hbm,
    u_out, p_out,
    xb, gb, st, outb, us, fs, into, back, row, rs, rn, sn, rc, sc, pk, gath, plw, qx, eb, eg, ea, ra, sw, c4w, c8w, small, ct_v, tt, tx, corr, p1w, p2t, e4s, e4r,
    in_sem, s_snd, s_rcv, n_snd, n_rcv, c_snd, c_rcv, g_snd, g_rcv,
    q_snd, q_rcv, w_snd, w_rcv, a_snd, a_rcv, b_snd, b_rcv, e4_snd, e4_rcv,
):
    s = lax.axis_index("strike")
    n = lax.axis_index("normal")
    is_a = n == NN // 2 - 1
    is_b = n == NN // 2
    is_i = jnp.logical_or(is_a, is_b)
    side = jnp.where(n >= NN // 2, 1, 0)
    has_s = {-1: s > 0, 1: s < NS - 1}
    has_n = {-1: n > 0, 1: n < NN - 1}
    lane = lax.broadcasted_iota(jnp.int32, (8, LANES), 1)
    sub = lax.broadcasted_iota(jnp.int32, (8, LANES), 0)
    sub5 = lax.broadcasted_iota(jnp.int32, (8, DIP), 0)

    order = (1, 0, 2)
    loads = {"st": pltpu.make_async_copy(st_in, st, in_sem.at[6])}
    for c in range(3):
        loads["u", c] = pltpu.make_async_copy(
            u_in.at[c], us.at[c], in_sem.at[c]
        )
        loads["f", c] = pltpu.make_async_copy(f_in.at[c], fs.at[c], in_sem.at[3 + c])
    for k, ref in enumerate((p_hbm, ap_hbm, inj_hbm)):
        loads["small", k] = pltpu.make_async_copy(ref, small.at[k], in_sem.at[7 + k])
        loads["small", k].start()
    loads["ct"] = pltpu.make_async_copy(ct_hbm, ct_v, in_sem.at[10])
    loads["ct"].start()
    loads["st"].start()
    for c in order:
        loads["f", c].start()
        loads["u", c].start()

    barrier = pltpu.get_barrier_semaphore()
    count = jnp.int32(0)

    def greet(cond, target):
        @pl.when(cond)
        def _():
            pl.semaphore_signal(barrier, inc=1, device_id=target, device_id_type=MESH)

        return jnp.where(cond, 1, 0)

    for a in WAYS:
        count += greet(has_s[a], (s + a, n))
        count += greet(has_n[a], (s, n + a))
        for b in WAYS:
            count += greet(jnp.logical_and(has_s[a], has_n[b]), (s + a, n + b))
    for mid in (NN // 2 - 1, NN // 2):
        count += greet(n != mid, (s, mid))
    for other in range(NN):
        count += greet(jnp.logical_and(is_i, n != other), (s, other))

    def near(d):
        return jnp.logical_and(s + d >= 0, s + d <= NS - 1)

    for d in (-3, -2, 2, 3):
        count += greet(jnp.logical_and(is_i, near(d)), (s + d, n))

    zrow = jnp.zeros((24, DIP), F32)

    def clear(i, carry):
        at = jnp.where(i < O, i, i + HS)
        for c in range(3):
            for rd in range(2):
                for pp in range(2):
                    xb[rd, c, pp, at] = zrow
            gb[c, at] = jnp.zeros((HN, DIP), F32)
        return carry

    lax.fori_loop(0, 10, clear, 0)

    def clear_own(i, carry):
        for c in range(3):
            for rd in range(2):
                xb[rd, c, 0, O + i, pl.ds(16, 8), :] = jnp.zeros((8, DIP), F32)
        return carry

    lax.fori_loop(0, HS, clear_own, 0)

    d0 = lax.broadcasted_iota(jnp.int32, (DIP, DIP), 0)
    d1 = lax.broadcasted_iota(jnp.int32, (DIP, DIP), 1)
    into[...] = jnp.where(d0 == 4 * (d1 % LANES) + d1 // LANES, 1.0, 0.0).astype(jnp.bfloat16)
    back[...] = jnp.where(d1 == 4 * (d0 % LANES) + d0 // LANES, 1.0, 0.0).astype(jnp.bfloat16)

    for a, w in ((-1, 0), (1, 1)):
        @pl.when(jnp.logical_not(has_s[a]))
        def _():
            rs[:, :, w] = jnp.zeros((2, 3, 4, HN, DIP), F32)

        @pl.when(jnp.logical_not(has_n[a]))
        def _():
            rn[:, :, w] = jnp.zeros((2, 3, 4, 8, DIP), F32)

        for b, v in ((-1, 0), (1, 1)):
            @pl.when(jnp.logical_not(jnp.logical_and(has_s[a], has_n[b])))
            def _():
                rc[:, :, w, v] = jnp.zeros((2, 3, 8, DIP), F32)

    @pl.when(is_i)
    def _():
        tx[...] = jnp.zeros_like(tx)
        eb[...] = jnp.zeros_like(eb)
        eg[...] = jnp.zeros_like(eg)
        for d in range(-3, 4):
            @pl.when(jnp.logical_not(near(d)))
            def _():
                plw[d + 3] = jnp.zeros((6, 8, DIP), F32)
                if -2 <= d <= 2:
                    sw[d + 2] = jnp.zeros((2, 8, DIP), F32)
                if -1 <= d <= 1:
                    ra[:, d + 1] = jnp.zeros((2, 2, 8, DIP), F32)

    loads["st"].wait()

    def recip(i, carry):
        st[i] = 0.1 / st[i]
        return carry

    lax.fori_loop(0, HS, recip, 0)

    @pl.when(is_a)
    def _():
        for i in range(HS):
            row[i : i + 1, :] = 0.5 * st[i, HN - 1 : HN, :]

    @pl.when(is_b)
    def _():
        for i in range(HS):
            row[i : i + 1, :] = 0.5 * st[i, 0:1, :]

    @pl.when(is_i)
    def _():
        qx[0] = shuffle(row[...], into[...])


    gathers = []
    for k, mid in enumerate((NN // 2 - 1, NN // 2)):
        gathers.append(
            (
                n != mid,
                pltpu.make_async_remote_copy(
                    src_ref=pk, dst_ref=gath.at[n], send_sem=g_snd.at[k], recv_sem=g_rcv,
                    device_id=(s, mid), device_id_type=MESH,
                ),
            )
        )

    q_copy = pltpu.make_async_remote_copy(
        src_ref=qx.at[0], dst_ref=qx.at[1], send_sem=q_snd, recv_sem=q_rcv,
        device_id=(s, NN - 1 - n), device_id_type=MESH,
    )

    def pair_of(src, dst_there, dst_here, snd, rcv_there, rcv_here, target):
        return [
            pltpu.make_async_remote_copy(
                src_ref=src, dst_ref=dst, send_sem=snd, recv_sem=rcv, device_id=target, device_id_type=MESH
            )
            for dst, rcv in ((dst_there, rcv_there), (dst_here, rcv_here))
        ]

    a_copies, b_copies, w_copies = [], [], []
    for d in (-1, 1, 0):
        for rel in range(2):
            if d == 0 and rel == 0:
                continue
            a_copies.append(
                [near(d)] + pair_of(
                    ea.at[1 + d], ra.at[rel, 1 - d], ra.at[rel, 1 + d], a_snd.at[rel, 1 + d],
                    a_rcv.at[rel, 1 - d], a_rcv.at[rel, 1 + d], (s + d, n if rel == 0 else NN - 1 - n),
                )
            )
    for d in (-2, 2, -1, 1):
        b_copies.append(
            [near(d)] + pair_of(
                sw.at[2], sw.at[2 - d], sw.at[2 + d], b_snd.at[2 + d], b_rcv.at[2 - d], b_rcv.at[2 + d], (s + d, n)
            )
        )
    for d, kinds in ((-3, 2), (3, 2), (-2, 5), (2, 5), (-1, 6), (1, 6)):
        part = pl.ds(0, kinds)
        w_copies.append(
            [near(d)] + pair_of(
                plw.at[3, part], plw.at[3 - d, part], plw.at[3 + d, part], w_snd.at[3 + d],
                w_rcv.at[3 - d], w_rcv.at[3 + d], (s + d, n),
            )
        )

    def send_all(copies):
        for cond, snd, _ in copies:
            pl.when(cond)(snd.start)

    def get_all(copies):
        for cond, _, rcv in copies:
            pl.when(cond)(rcv.wait_recv)

    def end_all(copies):
        for cond, snd, _ in copies:
            pl.when(cond)(snd.wait_send)

    keep_hi = jnp.logical_or(has_n[1], sub >= 4)
    keep_lo = jnp.logical_or(has_n[-1], sub < 4)
    keep = jnp.logical_and(keep_hi, keep_lo)

    def sweeps(rd, c):
        def sweep(k, carry):
            src = lax.rem(k - 1, 2)
            dst = lax.rem(k, 2)

            def get(i):
                return [[xb[rd, c, src, i, t * 8 : t * 8 + 8, cols(j)] for j in range(NJ)] for t in range(3)]

            def pair(m, inner):
                base = O - k - lax.rem(k, 2) + 4 * m
                rows = [get(base - 1 + r) for r in range(4 + 2)]
                vals = {}
                for r in range(4):
                    i = base + r
                    xm, x, xp = rows[r : r + 3]
                    ok = jnp.logical_and(
                        jnp.logical_or(has_s[-1], i >= O), jnp.logical_or(has_s[1], i < O + HS)
                    )
                    one, two = jnp.where(ok, 0.1, 0.0), jnp.where(ok, 0.2, 0.0)
                    up = [[pltpu.roll(v, 1, 0) for v in q] for q in x]
                    dn = [[pltpu.roll(v, 7, 0) for v in q] for q in x]
                    for t in range(3):
                        left, right = lane_pair(x[t], lane)
                        for j in range(NJ):
                            sy = jnp.where(sub == 0, up[(t + 2) % 3][j], up[t][j]) + jnp.where(
                                sub == 7, dn[(t + 1) % 3][j], dn[t][j]
                            )
                            sx = xm[t][j] + xp[t][j]
                            sz = left[j] + right[j]
                            if c == 0:
                                val = two * (x[t][j] + sx) + one * (sy + sz)
                            elif c == 1:
                                val = two * (x[t][j] + sy) + one * (sx + sz)
                            else:
                                val = two * (x[t][j] + sz) + one * (sx + sy)
                            if t < 2:
                                val = val + gb[c, i, t * 8 : t * 8 + 8, cols(j)]
                            else:
                                val = jnp.where(keep, val, 0.0)
                            vals[r, t, j] = val
                for (r, t, j), val in vals.items():
                    xb[rd, c, dst, base + r, t * 8 : t * 8 + 8, cols(j)] = val
                return inner

            lax.fori_loop(0, (HS + 2 * k + 3) // 4, pair, 0)
            return carry

        lax.fori_loop(1, SW + 1, sweep, 0)

    def messages(rd, c):
        out = []
        for a, w in ((-1, 0), (1, 1)):
            first = 1 if a < 0 else O + HS
            out.append(
                (
                    has_s[a],
                    pltpu.make_async_remote_copy(
                        src_ref=xb.at[rd, c, 0, pl.ds(first, 4), pl.ds(0, HN)], dst_ref=rs.at[rd, c, 1 - w],
                        send_sem=s_snd.at[rd, c, w], recv_sem=s_rcv.at[rd, c, 1 - w],
                        device_id=(s + a, n), device_id_type=MESH,
                    ),
                    pltpu.make_async_remote_copy(
                        src_ref=rs.at[rd, c, w], dst_ref=rs.at[rd, c, w],
                        send_sem=s_snd.at[rd, c, w], recv_sem=s_rcv.at[rd, c, w],
                        device_id=(s + a, n), device_id_type=MESH,
                    ),
                )
            )
        for b, v in ((-1, 0), (1, 1)):
            out.append(
                (
                    has_n[b],
                    pltpu.make_async_remote_copy(
                        src_ref=sn.at[rd, c, v], dst_ref=rn.at[rd, c, 1 - v],
                        send_sem=n_snd.at[rd, c, v], recv_sem=n_rcv.at[rd, c, 1 - v],
                        device_id=(s, n + b), device_id_type=MESH,
                    ),
                    pltpu.make_async_remote_copy(
                        src_ref=sn.at[rd, c, v], dst_ref=rn.at[rd, c, v],
                        send_sem=n_snd.at[rd, c, v], recv_sem=n_rcv.at[rd, c, v],
                        device_id=(s, n + b), device_id_type=MESH,
                    ),
                )
            )
        for a, w in ((-1, 0), (1, 1)):
            for b, v in ((-1, 0), (1, 1)):
                out.append(
                    (
                        jnp.logical_and(has_s[a], has_n[b]),
                        pltpu.make_async_remote_copy(
                            src_ref=sc.at[rd, c, w, v], dst_ref=rc.at[rd, c, 1 - w, 1 - v],
                            send_sem=c_snd.at[rd, c, w, v], recv_sem=c_rcv.at[rd, c, 1 - w, 1 - v],
                            device_id=(s + a, n + b), device_id_type=MESH,
                        ),
                        pltpu.make_async_remote_copy(
                            src_ref=sc.at[rd, c, w, v], dst_ref=rc.at[rd, c, w, v],
                            send_sem=c_snd.at[rd, c, w, v], recv_sem=c_rcv.at[rd, c, w, v],
                            device_id=(s + a, n + b), device_id_type=MESH,
                        ),
                    )
                )
        return out

    msgs = {(rd, c): messages(rd, c) for rd in range(2) for c in range(3)}
    r4sub = sub5 < 4

    def ghost(rd, c, i):
        return xb[rd, c, 0, i, 16:24, :]

    def send(rd, c):
        group = msgs[rd, c]
        for cond, snd, _ in group[:2]:
            pl.when(cond)(snd.start)
        for w in range(2):
            g = [ghost(rd, c, O - d if w == 0 else O + HS - 1 + d) for d in (1, 2, 3)]
            sc[rd, c, w, 1] = jnp.where(
                r4sub, g[0], jnp.where(sub5 < 6, pltpu.roll(g[1], 4, 0), pltpu.roll(g[2], 6, 0))
            )
            sc[rd, c, w, 0] = jnp.where(
                r4sub, jnp.where(sub5 >= 2, pltpu.roll(g[1], 4, 0), pltpu.roll(g[2], 2, 0)), g[0]
            )
        for cond, snd, _ in group[4:]:
            pl.when(cond)(snd.start)
        for t in range(4):
            first, second = ghost(rd, c, O + t), ghost(rd, c, O + t + 4)
            sn[rd, c, 1, t] = jnp.where(r4sub, first, pltpu.roll(second, 4, 0))
            sn[rd, c, 0, t] = jnp.where(r4sub, pltpu.roll(first, 4, 0), second)
        for cond, snd, _ in group[2:4]:
            pl.when(cond)(snd.start)

    def merge(rd, c, store):
        for cond, _, rcv in msgs[rd, c]:
            pl.when(cond)(rcv.wait_recv)
        for i in range(HS):
            t = i % 4
            low = xb[rd, c, 0, O + i, 0:8, :]
            high = xb[rd, c, 0, O + i, 8:16, :]
            way = 0 if i < 4 else 1
            low = low + rs[rd, c, way, t, 0:8, :]
            high = high + rs[rd, c, way, t, 8:16, :]
            from_lo, from_hi = rn[rd, c, 0, t], rn[rd, c, 1, t]
            if i < 4:
                from_hi = pltpu.roll(from_hi, 4, 0)
            else:
                from_lo = pltpu.roll(from_lo, 4, 0)
            low = low + jnp.where(r4sub, from_lo, 0.0)
            high = high + jnp.where(r4sub, 0.0, from_hi)
            d = i + 1 if i < 4 else HS - i
            if d <= 3:
                corner_lo, corner_hi = rc[rd, c, way, 0], rc[rd, c, way, 1]
                if d == 1:
                    low = low + jnp.where(r4sub, corner_lo, 0.0)
                    high = high + jnp.where(r4sub, 0.0, corner_hi)
                elif d == 2:
                    low = low + jnp.where(sub5 < 2, pltpu.roll(corner_lo, 4, 0), 0.0)
                    high = high + jnp.where(sub5 >= 6, pltpu.roll(corner_hi, 4, 0), 0.0)
                else:
                    low = low + jnp.where(sub5 < 2, pltpu.roll(corner_lo, 2, 0), 0.0)
                    high = high + jnp.where(sub5 >= 6, pltpu.roll(corner_hi, 6, 0), 0.0)
            store(i, low, high)

    def traction(p_of, q_of):
        for r in range(-3, HS + 3):
            p_row = p_of(r)
            own = p_row * q_of(0, r)
            far = p_row * q_of(1, r)
            below = jnp.where(is_b, far, own)
            above = jnp.where(is_b, own, far)
            tt[r + 3] = jnp.where(sub5 == 3, -below, jnp.where(sub5 == 4, above, 0.0))

        def tile_sweep(src, dst, first, trips, shift):
            def four(m, carry):
                base = first + 4 * m
                rows = [[src[base - 1 + r, :, cols(j)] for j in range(NJ)] for r in range(6)]
                vals = {}
                for r in range(4):
                    i = base + r
                    xm, x, xp = rows[r : r + 3]
                    ok = jnp.logical_and(
                        jnp.logical_or(has_s[-1], i >= 3), jnp.logical_or(has_s[1], i < 3 + HS)
                    )
                    one, two = jnp.where(ok, 0.1, 0.0), jnp.where(ok, 0.2, 0.0)
                    left, right = lane_pair(x, lane)
                    for j in range(NJ):
                        sy = pltpu.roll(x[j], 1, 0) + pltpu.roll(x[j], 7, 0)
                        vals[r, j] = (
                            two * (x[j] + sy) + one * ((xm[j] + xp[j]) + (left[j] + right[j]))
                            + tt[i, :, cols(j)]
                        )
                for (r, j), val in vals.items():
                    dst[base + r - shift, :, cols(j)] = val
                return carry

            lax.fori_loop(0, trips, four, 0)

        tile_sweep(tt, tx.at[0], 1, 3, 0)
        tile_sweep(tx.at[0], tx.at[1], 1, 3, 0)
        tile_sweep(tx.at[1], corr, 3, 2, 3)

    def win_row(ref, r, half):
        j, i = divmod(r + 8 * half, 8)
        return ref(j)[i : i + 1, :]

    def q_row(rel, r):
        own = win_row(lambda j: plw[j, 5], r, 3)
        return own if rel == 0 else win_row(lambda j: plw[j, 1], r, 3) - own

    def lubricate(opening, p, ap, ct, inj, first_row):
        rows = opening.shape[0]
        lanes = lax.broadcasted_iota(jnp.int32, (rows, DIP), 1)
        first, last = lanes == 0, lanes == DIP - 1
        strike = lax.broadcasted_iota(jnp.int32, (rows, DIP), 0) + (s * HS + first_row)
        valid = jnp.logical_and(strike >= 0, strike < NS * HS)
        soft = jnp.maximum(opening, 0.0) + jnp.log1p(jnp.exp(-jnp.abs(opening)))
        width = ap + soft
        k = ct * (width * width * width) / 12.0
        base = 0.5 * p - opening + inj
        k_up, k_dn = rows_sums(k)
        k_l, k_r = lane_shifts(k)
        k_l, k_r = jnp.where(first, 0.0, k_l), jnp.where(last, 0.0, k_r)
        f_up, f_dn, f_l, f_r = [0.5 * (k + v) for v in (k_up, k_dn, k_l, k_r)]
        rden = jnp.where(valid, 1.0 / (0.5 + (f_up + f_dn + f_l + f_r)), 0.0)
        base = base * rden
        f_up, f_dn = f_up * rden, f_dn * rden
        f_l = jnp.where(first, 0.0, f_l * rden)
        f_r = jnp.where(last, 0.0, f_r * rden)
        for _ in range(SW_L):
            p_up, p_dn = rows_sums(p)
            p_l, p_r = lane_shifts(p)
            p = (base + (f_up * p_up + f_dn * p_dn)) + (f_l * p_l + f_r * p_r)
        return p

    sign = jnp.where(is_b, 1.0, -1.0)

    def antisymmetric():
        near_row = pl.multiple_of(jnp.where(is_b, 0, 8), 8)
        far_row = pl.multiple_of(jnp.where(is_b, 8, 0), 8)
        c_up, c_dn = jnp.where(is_b, -1.0, 0.0), jnp.where(is_b, 0.0, -1.0)
        for i in range(HS):
            eb[0, 9 + i] = xb[0, 1, 0, O + i, pl.ds(near_row, 8), :]
            eg[9 + i] = gb[1, O + i, pl.ds(near_row, 8), :]

        def sweep(k, carry):
            src, dst = lax.rem(k - 1, 2), lax.rem(k, 2)

            def four(m, inner):
                base = jnp.where(k <= 4, 5, 1) + 8 * m
                rows = [[eb[src, base - 1 + r, :, cols(j)] for j in range(NJ)] for r in range(10)]
                vals = {}
                for r in range(8):
                    i = base + r
                    xm, x, xp = rows[r : r + 3]
                    ok = jnp.logical_and(
                        jnp.logical_or(has_s[-1], i >= 9), jnp.logical_or(has_s[1], i < 9 + HS)
                    )
                    one, two = jnp.where(ok, 0.1, 0.0), jnp.where(ok, 0.2, 0.0)
                    left, right = lane_pair(x, lane)
                    for j in range(NJ):
                        up = jnp.where(sub == 0, c_up * x[j], pltpu.roll(x[j], 1, 0))
                        dn = jnp.where(sub == 7, c_dn * x[j], pltpu.roll(x[j], 7, 0))
                        vals[r, j] = (
                            two * (x[j] + (up + dn)) + one * ((xm[j] + xp[j]) + (left[j] + right[j]))
                            + eg[i, :, cols(j)]
                        )
                for (r, j), val in vals.items():
                    eb[dst, base + r, :, cols(j)] = val
                return inner

            lax.fori_loop(0, jnp.where(k <= 4, 2, 3), four, 0)
            return carry

        def take(e):
            for cond, row_at in ((is_a, 7), (is_b, 0)):
                @pl.when(cond)
                def _():
                    for i in range(24):
                        ea[i // 8, e, i % 8 : i % 8 + 1, :] = eb[0, 1 + i, row_at : row_at + 1, :]

        lax.fori_loop(1, 2, sweep, 0)
        for i in range(HS):
            far = xb[0, 1, 0, O + i, pl.ds(far_row, 8), :]
            from_far = jnp.where(is_b, pltpu.roll(far, 7, 0), pltpu.roll(far, 1, 0))
            eb[1, 9 + i] = eb[1, 9 + i] + jnp.where(sub5 == jnp.where(is_b, 7, 0), 0.2 * from_far, 0.0)
        lax.fori_loop(2, 5, sweep, 0)
        take(0)
        lax.fori_loop(5, 9, sweep, 0)
        take(1)
        ra[0, 1] = ea[1]

    def flat(x):
        return x.reshape(x.shape[0] * 8, DIP)

    def spread(rows, first_row):
        lanes = lax.broadcasted_iota(jnp.int32, (rows, DIP), 1)
        first, last = lanes == 0, lanes == DIP - 1
        strike = lax.broadcasted_iota(jnp.int32, (rows, DIP), 0) + (s * HS + first_row)
        valid = jnp.logical_and(strike >= 0, strike < NS * HS)

        def across(x):
            up, dn = rows_sums(x)
            left, right = lane_shifts(x)
            left, right = jnp.where(first, 0.0, left), jnp.where(last, 0.0, right)
            return 0.1 * ((up + dn) + (left + right))

        return across, valid

    def layers(d, force, k, across, valid):
        out = []
        for m in range(min(k, 9 - k)):
            here = d[m] if m < len(d) else None
            val = None
            if here is not None:
                val = across(here)
                if m > 0:
                    val = val + 0.2 * here
            if m + 1 < len(d):
                val = val + 0.2 * d[m + 1]
            if m > 0:
                below = 0.2 * d[m - 1]
                val = below if val is None else val + below
            if m == 0 and force is not None:
                val = force if val is None else val + force
            out.append(jnp.where(valid, val, 0.0))
        return out

    def early():
        across, valid = spread(56, -24)
        force = flat(plw[:, 0]) * flat(plw[:, 1])
        d = [force]
        for k in range(2, 5):
            d = layers(d, force, k, across, valid)
        d = [x[8:48] for x in d]
        c4w[...] = d[0].reshape(5, 8, DIP)
        across, valid = spread(40, -16)
        for k in range(5, 9):
            d = layers(d, None, k, across, valid)
        c8w[...] = d[0][8:32].reshape(3, 8, DIP)

    def ready(c):
        loads["f", c].wait()
        gb[c, pl.ds(O, HS)] = shuffle((fs[c] * st[...]).reshape(HS * HN, DIP), into[...]).reshape(HS, HN, DIP)
        loads["u", c].wait()
        xb[0, c, 0, pl.ds(O, HS), pl.ds(0, HN)] = shuffle(us[c].reshape(HS * HN, DIP), into[...]).reshape(HS, HN, DIP)

    for k in range(3):
        loads["small", k].wait()
    loads["ct"].wait()
    pk[...] = jnp.concatenate([small[0], small[1], ct_v[...].astype(F32), small[2]], axis=1)

    def unpack():
        @pl.when(is_i)
        def _():
            gath[n] = pk[...]
            pltpu.make_async_copy(gath.at[pl.ds(0, NN - 1)], gath.at[pl.ds(0, NN - 1)], g_rcv).wait()
            for big in range(NJ):
                tiles = [gath[big * 4 + m] for m in range(4)]
                for kind, place in enumerate((0, 2, 3, 4)):
                    val = None
                    for m in range(4):
                        shift = (m - kind) % 4 * 32
                        piece = pltpu.roll(tiles[m], shift, 1) if shift else tiles[m]
                        val = piece if val is None else jnp.where(lane >= 32 * m, piece, val)
                    plw[3, place, :, cols(big)] = val
            both = shuffle(jnp.concatenate([plw[3, 0], plw[3, 2], plw[3, 3], plw[3, 4]], axis=0), into[...])
            for m, place in enumerate((0, 2, 3, 4)):
                plw[3, place] = both[8 * m : 8 * m + 8]
            q_copy.wait_recv()
            plw[3, 1] = qx[0] + qx[1]
            plw[3, 5] = qx[0]
            send_all(w_copies)

    def total():
        @pl.when(is_i)
        def _():
            get_all(a_copies)
            for e in range(2):
                own = ra[0, 0, e] + ra[0, 1, e] + ra[0, 2, e]
                sw[2, e] = sign * (own - (ra[1, 0, e] + ra[1, 1, e] + ra[1, 2, e]))
            send_all(b_copies)

    def pressed():
        @pl.when(is_i)
        def _():
            get_all(w_copies)
            traction(lambda r: win_row(lambda j: plw[j, 0], r, 3), q_row)
            early()

    sign = jnp.where(is_b, 1.0, -1.0)

    def to_second(c):
        def store(i, low, high):
            xb[1, c, 0, O + i, 0:8, :] = low
            xb[1, c, 0, O + i, 8:16, :] = high

        return store

    def to_out(c):
        def store(i, low, high):
            outb[c, i, 0:8, :] = low
            outb[c, i, 8:16, :] = high

        return store

    def own_tile(get, put):
        @pl.when(is_a)
        def _():
            for i in range(HS):
                put(i, 8, get(i, 8) + jnp.where(r4sub, 0.0, pltpu.roll(corr[i], 4, 0)))

        @pl.when(is_b)
        def _():
            for i in range(HS):
                put(i, 0, get(i, 0) + jnp.where(r4sub, pltpu.roll(corr[i], 4, 0), 0.0))

    def put_second(i, r, v):
        xb[1, 1, 0, O + i, r : r + 8, :] = v

    def put_out(i, r, v):
        outb[1, i, r : r + 8, :] = v

    e4_copies = []
    for i in range(NN // 2):
        e4_copies.append(
            (
                jnp.logical_and(is_i, n != side * 8 + i),
                pltpu.make_async_remote_copy(
                    src_ref=e4s.at[i], dst_ref=e4r, send_sem=e4_snd.at[i], recv_sem=e4_rcv,
                    device_id=(s, side * 8 + i), device_id_type=MESH,
                ),
            )
        )

    def plane():
        @pl.when(is_i)
        def _():
            get_all(b_copies)
            p1 = lubricate(
                flat(sw[:, 0]) + flat(c4w[...]), *[flat(plw[1:6, kind]) for kind in (0, 2, 3, 4)], -16
            )
            p1w[...] = p1.reshape(5, 8, DIP)
            across, valid = spread(40, -16)
            force = p1 * flat(plw[1:6, 1])
            d = layers([force], force, 2, across, valid)
            d = layers(d, force, 6 + 1, across, valid)
            d = layers(d, force, 8, across, valid)
            opening = (flat(sw[1:4, 1]) + flat(c8w[...])) + d[0][8:32]
            p2 = lubricate(opening, p1[8:32], *[flat(plw[2:5, kind]) for kind in (2, 3, 4)], -8)
            p2 = shuffle(p2[8:16], back[...])
            for j in range(NJ):
                p2t[j] = p2[:, cols(j)]
            for i in range(NN // 2):
                shift = -(i % 4) * 32 % LANES
                tile = p2t[side * 2 + i // 4]
                e4s[i] = pltpu.roll(tile, shift, 1) if shift else tile
            for cond, copy in e4_copies:
                pl.when(cond)(copy.start)
            e4r[...] = e4s[jnp.where(is_b, 0, 7)]
            traction(lambda r: win_row(lambda j: p1w[j], r, 2), q_row)

    def start():
        ready(1)
        pl.semaphore_wait(barrier, count)
        for cond, copy in gathers:
            pl.when(cond)(copy.start)
        pl.when(is_i)(q_copy.start)

    def ahead():
        @pl.when(is_i)
        def _():
            antisymmetric()
            send_all(a_copies)

    def one(c):
        if c != 1:
            ready(c)
        sweeps(0, c)
        send(0, c)

    def two(c):
        merge(0, c, to_second(c))
        if c == 1:
            own_tile(lambda i, r: xb[1, 1, 0, O + i, r : r + 8, :], put_second)
        sweeps(1, c)
        send(1, c)

    def last(c):
        merge(1, c, to_out(c))
        if c == 1:
            own_tile(lambda i, r: outb[1, i, r : r + 8, :], put_out)
        u_out[c] = shuffle(outb[c].reshape(HS * HN, DIP), back[...]).reshape(HS, HN, DIP)

    start()
    ahead()
    one(0)
    one(2)
    unpack()
    one(1)
    total()
    two(0)
    two(2)
    pressed()
    two(1)
    plane()
    last(0)
    last(2)
    last(1)

    @pl.when(jnp.logical_not(is_i))
    def _():
        pltpu.make_async_remote_copy(
            src_ref=e4s.at[0], dst_ref=e4r, send_sem=e4_snd.at[0], recv_sem=e4_rcv,
            device_id=(s, NN - 1 - n), device_id_type=MESH,
        ).wait_recv()

    p_out[...] = e4r[...]

    for group in msgs.values():
        for cond, snd, _ in group:
            pl.when(cond)(snd.wait_send)
    for cond, copy in gathers:
        pl.when(cond)(copy.wait_send)
    for cond, copy in e4_copies:
        pl.when(cond)(copy.wait_send)

    @pl.when(is_i)
    def _():
        q_copy.wait_send()
        for copies in (a_copies, b_copies, w_copies):
            end_all(copies)


def body(displacement, body_force, stiffness, aperture_base, contact_open, pressure_init, injection):
    vm = pl.BlockSpec(memory_space=pltpu.VMEM)
    hbm = pl.BlockSpec(memory_space=pl.ANY)
    dma = pltpu.SemaphoreType.DMA

    def buf(*shape):
        return pltpu.VMEM(shape, F32)

    scratch = [
        buf(2, 3, 2, 18, 24, DIP),
        buf(3, 18, HN, DIP),
        buf(HS, HN, DIP),
        buf(3, HS, HN, DIP),
        buf(3, HS, HN, DIP),
        buf(3, HS, HN, DIP),
        pltpu.VMEM((DIP, DIP), jnp.bfloat16),
        pltpu.VMEM((DIP, DIP), jnp.bfloat16),
        buf(8, DIP),
        buf(2, 3, 2, 4, HN, DIP),
        buf(2, 3, 2, 4, 8, DIP),
        buf(2, 3, 2, 4, 8, DIP),
        buf(2, 3, 2, 2, 8, DIP),
        buf(2, 3, 2, 2, 8, DIP),
        buf(8, LANES),
        buf(NN, 8, LANES),
        buf(7, 6, 8, DIP),
        buf(2, 8, DIP),
        buf(2, 26, 8, DIP),
        buf(26, 8, DIP),
        buf(3, 2, 8, DIP),
        buf(2, 3, 2, 8, DIP),
        buf(5, 2, 8, DIP),
        buf(5, 8, DIP),
        buf(3, 8, DIP),
        buf(3, 8, 32),
        pltpu.VMEM((8, 32), jnp.int32),
        buf(14, 8, DIP),
        buf(2, 14, 8, DIP),
        buf(HS, 8, DIP),
        buf(5, 8, DIP),
        buf(NJ, 8, LANES),
        buf(NN // 2, 8, LANES),
        buf(8, LANES),
        dma((11,)),
        dma((2, 3, 2)), dma((2, 3, 2)), dma((2, 3, 2)), dma((2, 3, 2)),
        dma((2, 3, 2, 2)), dma((2, 3, 2, 2)),
        dma((2,)), dma,
        dma, dma, dma((7,)), dma((7,)), dma((2, 3)), dma((2, 3)), dma((5,)), dma((5,)),
        dma((NN // 2,)), dma,
    ]
    u, tile = pl.pallas_call(
        kernel,
        out_shape=(
            pltpu.VMEM((3, HS, HN, DIP), F32),
            pltpu.VMEM((8, LANES), F32),
        ),
        in_specs=[hbm] * 7,
        out_specs=(vm, vm),
        scratch_shapes=scratch,
        compiler_params=pltpu.CompilerParams(
            collective_id=0, has_side_effects=True, vmem_limit_bytes=60 * 2**20
        ),
        cost_estimate=pl.CostEstimate(flops=60_000_000, bytes_accessed=2_700_000, transcendentals=40_000),
    )(displacement, body_force, stiffness, aperture_base, contact_open, pressure_init, injection)
    return u, tile[:, : HN * 2]


def solution(mesh):
    in_specs = (
        P(None, "strike", "normal", None),
        P(None, "strike", "normal", None),
        P("strike", "normal", None),
        P("strike", "normal"),
        P("strike", "normal"),
        P("strike", "normal"),
        P("strike", "normal"),
    )
    out_specs = (P(None, "strike", "normal", None), P("strike", "normal"))
    return jax.shard_map(body, mesh=mesh, in_specs=in_specs, out_specs=out_specs, check_vma=False)
```

```python
import jax
import jax.numpy as jnp
from jax import lax
from jax.experimental import pallas as pl
from jax.experimental.pallas import tpu as pltpu
from jax.sharding import PartitionSpec as P

MESH = pl.DeviceIdType.MESH
F32 = jnp.float32
NS, NN = 8, 16
HS, HN, DIP = 8, 16, 512
SW = 4
SW_L = 6
O = 5
LANES = 128
NJ = DIP // LANES
WAYS = (-1, 1)


def lane_pair(x, lane):
    left = [jnp.where(lane == 0, 0.0, pltpu.roll(x[-1], 1, 1))] + x[:-1]
    right = x[1:] + [jnp.where(lane == LANES - 1, 0.0, pltpu.roll(x[0], LANES - 1, 1))]
    return left, right


def cols(j):
    return slice(j * LANES, (j + 1) * LANES)


def lane_shifts(x):
    cut = DIP - LANES
    left = jnp.concatenate([pltpu.roll(x[:, cut:], 1, 1), x[:, :cut]], axis=1)
    right = jnp.concatenate([x[:, LANES:], pltpu.roll(x[:, :LANES], LANES - 1, 1)], axis=1)
    return left, right


def shuffle(x, matrix):
    high = x.astype(jnp.bfloat16)
    rest = x - high.astype(F32)
    mid = rest.astype(jnp.bfloat16)
    low = (rest - mid.astype(F32)).astype(jnp.bfloat16)
    return jnp.dot(jnp.concatenate([high, mid, low], axis=1), matrix, preferred_element_type=F32)


def rows_sums(x):
    count = x.shape[0]
    return pltpu.roll(x, 1, 0), pltpu.roll(x, count - 1, 0)


def kernel(
    u_in, f_in, st_in, ap_hbm, ct_hbm, p_hbm, inj_hbm,
    u_out, p_out,
    xb, gb, st, outb, us, fs, into, back, row, rs, rn, sn, rc, sc, pk, gath, plw, qx, eb, eg, ea, ra, sw, c4w, c8w, small, ct_v, tt, tx, corr, p1w, p2t, e4s, e4r,
    in_sem, s_snd, s_rcv, n_snd, n_rcv, c_snd, c_rcv, g_snd, g_rcv,
    q_snd, q_rcv, w_snd, w_rcv, a_snd, a_rcv, b_snd, b_rcv, e4_snd, e4_rcv,
):
    s = lax.axis_index("strike")
    n = lax.axis_index("normal")
    is_a = n == NN // 2 - 1
    is_b = n == NN // 2
    is_i = jnp.logical_or(is_a, is_b)
    side = jnp.where(n >= NN // 2, 1, 0)
    has_s = {-1: s > 0, 1: s < NS - 1}
    has_n = {-1: n > 0, 1: n < NN - 1}
    lane = lax.broadcasted_iota(jnp.int32, (8, LANES), 1)
    sub = lax.broadcasted_iota(jnp.int32, (8, LANES), 0)
    sub5 = lax.broadcasted_iota(jnp.int32, (8, DIP), 0)

    order = (1, 0, 2)
    loads = {"st": pltpu.make_async_copy(st_in, st, in_sem.at[6])}
    for c in range(3):
        loads["u", c] = pltpu.make_async_copy(
            u_in.at[c], us.at[c], in_sem.at[c]
        )
        loads["f", c] = pltpu.make_async_copy(f_in.at[c], fs.at[c], in_sem.at[3 + c])
    for k, ref in enumerate((p_hbm, ap_hbm, inj_hbm)):
        loads["small", k] = pltpu.make_async_copy(ref, small.at[k], in_sem.at[7 + k])
        loads["small", k].start()
    loads["ct"] = pltpu.make_async_copy(ct_hbm, ct_v, in_sem.at[10])
    loads["ct"].start()
    loads["st"].start()
    for c in order:
        loads["f", c].start()
        loads["u", c].start()

    barrier = pltpu.get_barrier_semaphore()
    count = jnp.int32(0)

    def greet(cond, target):
        @pl.when(cond)
        def _():
            pl.semaphore_signal(barrier, inc=1, device_id=target, device_id_type=MESH)

        return jnp.where(cond, 1, 0)

    for a in WAYS:
        count += greet(has_s[a], (s + a, n))
        count += greet(has_n[a], (s, n + a))
        for b in WAYS:
            count += greet(jnp.logical_and(has_s[a], has_n[b]), (s + a, n + b))
    for mid in (NN // 2 - 1, NN // 2):
        count += greet(n != mid, (s, mid))
    for other in range(NN):
        count += greet(jnp.logical_and(is_i, n != other), (s, other))

    def near(d):
        return jnp.logical_and(s + d >= 0, s + d <= NS - 1)

    for d in (-3, -2, 2, 3):
        count += greet(jnp.logical_and(is_i, near(d)), (s + d, n))

    zrow = jnp.zeros((24, DIP), F32)

    def clear(i, carry):
        at = jnp.where(i < O, i, i + HS)
        for c in range(3):
            for rd in range(2):
                for pp in range(2):
                    xb[rd, c, pp, at] = zrow
            gb[c, at] = jnp.zeros((HN, DIP), F32)
        return carry

    lax.fori_loop(0, 10, clear, 0)

    def clear_own(i, carry):
        for c in range(3):
            for rd in range(2):
                xb[rd, c, 0, O + i, pl.ds(16, 8), :] = jnp.zeros((8, DIP), F32)
        return carry

    lax.fori_loop(0, HS, clear_own, 0)

    d0 = lax.broadcasted_iota(jnp.int32, (DIP, DIP), 0)
    d1 = lax.broadcasted_iota(jnp.int32, (DIP, DIP), 1)
    one_in = jnp.where(d0 == 4 * (d1 & (LANES - 1)) + jnp.right_shift(d1, 7), 1.0, 0.0).astype(jnp.bfloat16)
    one_back = jnp.where(d1 == 4 * (d0 & (LANES - 1)) + jnp.right_shift(d0, 7), 1.0, 0.0).astype(jnp.bfloat16)
    for part in range(3):
        into[pl.ds(part * DIP, DIP)] = one_in
        back[pl.ds(part * DIP, DIP)] = one_back

    for a, w in ((-1, 0), (1, 1)):
        @pl.when(jnp.logical_not(has_s[a]))
        def _():
            rs[:, :, w] = jnp.zeros((2, 3, 4, HN, DIP), F32)

        @pl.when(jnp.logical_not(has_n[a]))
        def _():
            rn[:, :, w] = jnp.zeros((2, 3, 4, 8, DIP), F32)

        for b, v in ((-1, 0), (1, 1)):
            @pl.when(jnp.logical_not(jnp.logical_and(has_s[a], has_n[b])))
            def _():
                rc[:, :, w, v] = jnp.zeros((2, 3, 8, DIP), F32)

    @pl.when(is_i)
    def _():
        tx[...] = jnp.zeros_like(tx)
        eb[...] = jnp.zeros_like(eb)
        eg[...] = jnp.zeros_like(eg)
        for d in range(-3, 4):
            @pl.when(jnp.logical_not(near(d)))
            def _():
                plw[d + 3] = jnp.zeros((6, 8, DIP), F32)
                if -2 <= d <= 2:
                    sw[d + 2] = jnp.zeros((2, 8, DIP), F32)
                if -1 <= d <= 1:
                    ra[:, d + 1] = jnp.zeros((2, 2, 8, DIP), F32)

    loads["st"].wait()

    def recip(i, carry):
        st[i] = 0.1 / st[i]
        return carry

    lax.fori_loop(0, HS, recip, 0)

    @pl.when(is_a)
    def _():
        for i in range(HS):
            row[i : i + 1, :] = 0.5 * st[i, HN - 1 : HN, :]

    @pl.when(is_b)
    def _():
        for i in range(HS):
            row[i : i + 1, :] = 0.5 * st[i, 0:1, :]

    @pl.when(is_i)
    def _():
        qx[0] = shuffle(row[...], into[...])


    gathers = []
    for k, mid in enumerate((NN // 2 - 1, NN // 2)):
        gathers.append(
            (
                n != mid,
                pltpu.make_async_remote_copy(
                    src_ref=pk, dst_ref=gath.at[n], send_sem=g_snd.at[k], recv_sem=g_rcv,
                    device_id=(s, mid), device_id_type=MESH,
                ),
            )
        )

    q_copy = pltpu.make_async_remote_copy(
        src_ref=qx.at[0], dst_ref=qx.at[1], send_sem=q_snd, recv_sem=q_rcv,
        device_id=(s, NN - 1 - n), device_id_type=MESH,
    )

    def pair_of(src, dst_there, dst_here, snd, rcv_there, rcv_here, target):
        return [
            pltpu.make_async_remote_copy(
                src_ref=src, dst_ref=dst, send_sem=snd, recv_sem=rcv, device_id=target, device_id_type=MESH
            )
            for dst, rcv in ((dst_there, rcv_there), (dst_here, rcv_here))
        ]

    a_copies, b_copies, w_copies = [], [], []
    for d in (-1, 1, 0):
        for rel in range(2):
            if d == 0 and rel == 0:
                continue
            a_copies.append(
                [near(d)] + pair_of(
                    ea.at[1 + d], ra.at[rel, 1 - d], ra.at[rel, 1 + d], a_snd.at[rel, 1 + d],
                    a_rcv.at[rel, 1 - d], a_rcv.at[rel, 1 + d], (s + d, n if rel == 0 else NN - 1 - n),
                )
            )
    for d in (-2, 2, -1, 1):
        b_copies.append(
            [near(d)] + pair_of(
                sw.at[2], sw.at[2 - d], sw.at[2 + d], b_snd.at[2 + d], b_rcv.at[2 - d], b_rcv.at[2 + d], (s + d, n)
            )
        )
    for d, kinds in ((-3, 2), (3, 2), (-2, 5), (2, 5), (-1, 6), (1, 6)):
        part = pl.ds(0, kinds)
        w_copies.append(
            [near(d)] + pair_of(
                plw.at[3, part], plw.at[3 - d, part], plw.at[3 + d, part], w_snd.at[3 + d],
                w_rcv.at[3 - d], w_rcv.at[3 + d], (s + d, n),
            )
        )

    def send_all(copies):
        for cond, snd, _ in copies:
            pl.when(cond)(snd.start)

    def get_all(copies):
        for cond, _, rcv in copies:
            pl.when(cond)(rcv.wait_recv)

    def end_all(copies):
        for cond, snd, _ in copies:
            pl.when(cond)(snd.wait_send)

    keep_hi = jnp.logical_or(has_n[1], sub >= 4)
    keep_lo = jnp.logical_or(has_n[-1], sub < 4)
    keep = jnp.logical_and(keep_hi, keep_lo)

    def sweeps(rd, c):
        def sweep(k, carry):
            src = lax.rem(k - 1, 2)
            dst = lax.rem(k, 2)

            def get(i):
                return [[xb[rd, c, src, i, t * 8 : t * 8 + 8, cols(j)] for j in range(NJ)] for t in range(3)]

            def pair(m, inner):
                base = O - k - lax.rem(k, 2) + 4 * m
                rows = [get(base - 1 + r) for r in range(4 + 2)]
                vals = {}
                for r in range(4):
                    i = base + r
                    xm, x, xp = rows[r : r + 3]
                    ok = jnp.logical_and(
                        jnp.logical_or(has_s[-1], i >= O), jnp.logical_or(has_s[1], i < O + HS)
                    )
                    one, two = jnp.where(ok, 0.1, 0.0), jnp.where(ok, 0.2, 0.0)
                    up = [[pltpu.roll(v, 1, 0) for v in q] for q in x]
                    dn = [[pltpu.roll(v, 7, 0) for v in q] for q in x]
                    for t in range(3):
                        left, right = lane_pair(x[t], lane)
                        for j in range(NJ):
                            sy = jnp.where(sub == 0, up[(t + 2) % 3][j], up[t][j]) + jnp.where(
                                sub == 7, dn[(t + 1) % 3][j], dn[t][j]
                            )
                            sx = xm[t][j] + xp[t][j]
                            sz = left[j] + right[j]
                            if c == 0:
                                val = two * (x[t][j] + sx) + one * (sy + sz)
                            elif c == 1:
                                val = two * (x[t][j] + sy) + one * (sx + sz)
                            else:
                                val = two * (x[t][j] + sz) + one * (sx + sy)
                            if t < 2:
                                val = val + gb[c, i, t * 8 : t * 8 + 8, cols(j)]
                            else:
                                val = jnp.where(keep, val, 0.0)
                            vals[r, t, j] = val
                for (r, t, j), val in vals.items():
                    xb[rd, c, dst, base + r, t * 8 : t * 8 + 8, cols(j)] = val
                return inner

            lax.fori_loop(0, (HS + 2 * k + 3) // 4, pair, 0)
            return carry

        lax.fori_loop(1, SW + 1, sweep, 0)

    def messages(rd, c):
        out = []
        for a, w in ((-1, 0), (1, 1)):
            first = 1 if a < 0 else O + HS
            out.append(
                (
                    has_s[a],
                    pltpu.make_async_remote_copy(
                        src_ref=xb.at[rd, c, 0, pl.ds(first, 4), pl.ds(0, HN)], dst_ref=rs.at[rd, c, 1 - w],
                        send_sem=s_snd.at[rd, c, w], recv_sem=s_rcv.at[rd, c, 1 - w],
                        device_id=(s + a, n), device_id_type=MESH,
                    ),
                    pltpu.make_async_remote_copy(
                        src_ref=rs.at[rd, c, w], dst_ref=rs.at[rd, c, w],
                        send_sem=s_snd.at[rd, c, w], recv_sem=s_rcv.at[rd, c, w],
                        device_id=(s + a, n), device_id_type=MESH,
                    ),
                )
            )
        for b, v in ((-1, 0), (1, 1)):
            out.append(
                (
                    has_n[b],
                    pltpu.make_async_remote_copy(
                        src_ref=sn.at[rd, c, v], dst_ref=rn.at[rd, c, 1 - v],
                        send_sem=n_snd.at[rd, c, v], recv_sem=n_rcv.at[rd, c, 1 - v],
                        device_id=(s, n + b), device_id_type=MESH,
                    ),
                    pltpu.make_async_remote_copy(
                        src_ref=sn.at[rd, c, v], dst_ref=rn.at[rd, c, v],
                        send_sem=n_snd.at[rd, c, v], recv_sem=n_rcv.at[rd, c, v],
                        device_id=(s, n + b), device_id_type=MESH,
                    ),
                )
            )
        for a, w in ((-1, 0), (1, 1)):
            for b, v in ((-1, 0), (1, 1)):
                out.append(
                    (
                        jnp.logical_and(has_s[a], has_n[b]),
                        pltpu.make_async_remote_copy(
                            src_ref=sc.at[rd, c, w, v], dst_ref=rc.at[rd, c, 1 - w, 1 - v],
                            send_sem=c_snd.at[rd, c, w, v], recv_sem=c_rcv.at[rd, c, 1 - w, 1 - v],
                            device_id=(s + a, n + b), device_id_type=MESH,
                        ),
                        pltpu.make_async_remote_copy(
                            src_ref=sc.at[rd, c, w, v], dst_ref=rc.at[rd, c, w, v],
                            send_sem=c_snd.at[rd, c, w, v], recv_sem=c_rcv.at[rd, c, w, v],
                            device_id=(s + a, n + b), device_id_type=MESH,
                        ),
                    )
                )
        return out

    msgs = {(rd, c): messages(rd, c) for rd in range(2) for c in range(3)}
    r4sub = sub5 < 4

    def ghost(rd, c, i):
        return xb[rd, c, 0, i, 16:24, :]

    def send(rd, c):
        group = msgs[rd, c]
        for cond, snd, _ in group[:2]:
            pl.when(cond)(snd.start)
        for w in range(2):
            g = [ghost(rd, c, O - d if w == 0 else O + HS - 1 + d) for d in (1, 2, 3)]
            sc[rd, c, w, 1] = jnp.where(
                r4sub, g[0], jnp.where(sub5 < 6, pltpu.roll(g[1], 4, 0), pltpu.roll(g[2], 6, 0))
            )
            sc[rd, c, w, 0] = jnp.where(
                r4sub, jnp.where(sub5 >= 2, pltpu.roll(g[1], 4, 0), pltpu.roll(g[2], 2, 0)), g[0]
            )
        for cond, snd, _ in group[4:]:
            pl.when(cond)(snd.start)
        for t in range(4):
            first, second = ghost(rd, c, O + t), ghost(rd, c, O + t + 4)
            sn[rd, c, 1, t] = jnp.where(r4sub, first, pltpu.roll(second, 4, 0))
            sn[rd, c, 0, t] = jnp.where(r4sub, pltpu.roll(first, 4, 0), second)
        for cond, snd, _ in group[2:4]:
            pl.when(cond)(snd.start)

    def merge(rd, c, store):
        for cond, _, rcv in msgs[rd, c]:
            pl.when(cond)(rcv.wait_recv)
        for i in range(HS):
            t = i % 4
            low = xb[rd, c, 0, O + i, 0:8, :]
            high = xb[rd, c, 0, O + i, 8:16, :]
            way = 0 if i < 4 else 1
            low = low + rs[rd, c, way, t, 0:8, :]
            high = high + rs[rd, c, way, t, 8:16, :]
            from_lo, from_hi = rn[rd, c, 0, t], rn[rd, c, 1, t]
            if i < 4:
                from_hi = pltpu.roll(from_hi, 4, 0)
            else:
                from_lo = pltpu.roll(from_lo, 4, 0)
            low = low + jnp.where(r4sub, from_lo, 0.0)
            high = high + jnp.where(r4sub, 0.0, from_hi)
            d = i + 1 if i < 4 else HS - i
            if d <= 3:
                corner_lo, corner_hi = rc[rd, c, way, 0], rc[rd, c, way, 1]
                if d == 1:
                    low = low + jnp.where(r4sub, corner_lo, 0.0)
                    high = high + jnp.where(r4sub, 0.0, corner_hi)
                elif d == 2:
                    low = low + jnp.where(sub5 < 2, pltpu.roll(corner_lo, 4, 0), 0.0)
                    high = high + jnp.where(sub5 >= 6, pltpu.roll(corner_hi, 4, 0), 0.0)
                else:
                    low = low + jnp.where(sub5 < 2, pltpu.roll(corner_lo, 2, 0), 0.0)
                    high = high + jnp.where(sub5 >= 6, pltpu.roll(corner_hi, 6, 0), 0.0)
            store(i, low, high)

    def traction(p_of, q_of):
        for r in range(-3, HS + 3):
            p_row = p_of(r)
            own = p_row * q_of(0, r)
            far = p_row * q_of(1, r)
            below = jnp.where(is_b, far, own)
            above = jnp.where(is_b, own, far)
            tt[r + 3] = jnp.where(sub5 == 3, -below, jnp.where(sub5 == 4, above, 0.0))

        def tile_sweep(src, dst, first, trips, shift):
            def four(m, carry):
                base = first + 4 * m
                rows = [[src[base - 1 + r, :, cols(j)] for j in range(NJ)] for r in range(6)]
                vals = {}
                for r in range(4):
                    i = base + r
                    xm, x, xp = rows[r : r + 3]
                    ok = jnp.logical_and(
                        jnp.logical_or(has_s[-1], i >= 3), jnp.logical_or(has_s[1], i < 3 + HS)
                    )
                    one, two = jnp.where(ok, 0.1, 0.0), jnp.where(ok, 0.2, 0.0)
                    left, right = lane_pair(x, lane)
                    for j in range(NJ):
                        sy = pltpu.roll(x[j], 1, 0) + pltpu.roll(x[j], 7, 0)
                        vals[r, j] = (
                            two * (x[j] + sy) + one * ((xm[j] + xp[j]) + (left[j] + right[j]))
                            + tt[i, :, cols(j)]
                        )
                for (r, j), val in vals.items():
                    dst[base + r - shift, :, cols(j)] = val
                return carry

            lax.fori_loop(0, trips, four, 0)

        tile_sweep(tt, tx.at[0], 1, 3, 0)
        tile_sweep(tx.at[0], tx.at[1], 1, 3, 0)
        tile_sweep(tx.at[1], corr, 3, 2, 3)

    def win_row(ref, r, half):
        j, i = divmod(r + 8 * half, 8)
        return ref(j)[i : i + 1, :]

    def q_row(rel, r):
        own = win_row(lambda j: plw[j, 5], r, 3)
        return own if rel == 0 else win_row(lambda j: plw[j, 1], r, 3) - own

    def lubricate(opening, p, ap, ct, inj, first_row):
        rows = opening.shape[0]
        lanes = lax.broadcasted_iota(jnp.int32, (rows, DIP), 1)
        first, last = lanes == 0, lanes == DIP - 1
        strike = lax.broadcasted_iota(jnp.int32, (rows, DIP), 0) + (s * HS + first_row)
        valid = jnp.logical_and(strike >= 0, strike < NS * HS)
        soft = jnp.maximum(opening, 0.0) + jnp.log1p(jnp.exp(-jnp.abs(opening)))
        width = ap + soft
        k = ct * (width * width * width) / 12.0
        base = 0.5 * p - opening + inj
        k_up, k_dn = rows_sums(k)
        k_l, k_r = lane_shifts(k)
        k_l, k_r = jnp.where(first, 0.0, k_l), jnp.where(last, 0.0, k_r)
        f_up, f_dn, f_l, f_r = [0.5 * (k + v) for v in (k_up, k_dn, k_l, k_r)]
        rden = jnp.where(valid, 1.0 / (0.5 + (f_up + f_dn + f_l + f_r)), 0.0)
        base = base * rden
        f_up, f_dn = f_up * rden, f_dn * rden
        f_l = jnp.where(first, 0.0, f_l * rden)
        f_r = jnp.where(last, 0.0, f_r * rden)
        for _ in range(SW_L):
            p_up, p_dn = rows_sums(p)
            p_l, p_r = lane_shifts(p)
            p = (base + (f_up * p_up + f_dn * p_dn)) + (f_l * p_l + f_r * p_r)
        return p

    sign = jnp.where(is_b, 1.0, -1.0)

    def antisymmetric():
        near_row = pl.multiple_of(jnp.where(is_b, 0, 8), 8)
        far_row = pl.multiple_of(jnp.where(is_b, 8, 0), 8)
        c_up, c_dn = jnp.where(is_b, -1.0, 0.0), jnp.where(is_b, 0.0, -1.0)
        for i in range(HS):
            eb[0, 9 + i] = xb[0, 1, 0, O + i, pl.ds(near_row, 8), :]
            eg[9 + i] = gb[1, O + i, pl.ds(near_row, 8), :]

        def sweep(k, carry):
            src, dst = lax.rem(k - 1, 2), lax.rem(k, 2)

            def four(m, inner):
                base = jnp.where(k <= 4, 5, 1) + 8 * m
                rows = [[eb[src, base - 1 + r, :, cols(j)] for j in range(NJ)] for r in range(10)]
                vals = {}
                for r in range(8):
                    i = base + r
                    xm, x, xp = rows[r : r + 3]
                    ok = jnp.logical_and(
                        jnp.logical_or(has_s[-1], i >= 9), jnp.logical_or(has_s[1], i < 9 + HS)
                    )
                    one, two = jnp.where(ok, 0.1, 0.0), jnp.where(ok, 0.2, 0.0)
                    left, right = lane_pair(x, lane)
                    for j in range(NJ):
                        up = jnp.where(sub == 0, c_up * x[j], pltpu.roll(x[j], 1, 0))
                        dn = jnp.where(sub == 7, c_dn * x[j], pltpu.roll(x[j], 7, 0))
                        vals[r, j] = (
                            two * (x[j] + (up + dn)) + one * ((xm[j] + xp[j]) + (left[j] + right[j]))
                            + eg[i, :, cols(j)]
                        )
                for (r, j), val in vals.items():
                    eb[dst, base + r, :, cols(j)] = val
                return inner

            lax.fori_loop(0, jnp.where(k <= 4, 2, 3), four, 0)
            return carry

        def take(e):
            for cond, row_at in ((is_a, 7), (is_b, 0)):
                @pl.when(cond)
                def _():
                    for i in range(24):
                        ea[i // 8, e, i % 8 : i % 8 + 1, :] = eb[0, 1 + i, row_at : row_at + 1, :]

        lax.fori_loop(1, 2, sweep, 0)
        for i in range(HS):
            far = xb[0, 1, 0, O + i, pl.ds(far_row, 8), :]
            from_far = jnp.where(is_b, pltpu.roll(far, 7, 0), pltpu.roll(far, 1, 0))
            eb[1, 9 + i] = eb[1, 9 + i] + jnp.where(sub5 == jnp.where(is_b, 7, 0), 0.2 * from_far, 0.0)
        lax.fori_loop(2, 5, sweep, 0)
        take(0)
        lax.fori_loop(5, 9, sweep, 0)
        take(1)
        ra[0, 1] = ea[1]

    def flat(x):
        return x.reshape(x.shape[0] * 8, DIP)

    def spread(rows, first_row):
        lanes = lax.broadcasted_iota(jnp.int32, (rows, DIP), 1)
        first, last = lanes == 0, lanes == DIP - 1
        strike = lax.broadcasted_iota(jnp.int32, (rows, DIP), 0) + (s * HS + first_row)
        valid = jnp.logical_and(strike >= 0, strike < NS * HS)

        def across(x):
            up, dn = rows_sums(x)
            left, right = lane_shifts(x)
            left, right = jnp.where(first, 0.0, left), jnp.where(last, 0.0, right)
            return 0.1 * ((up + dn) + (left + right))

        return across, valid

    def layers(d, force, k, across, valid):
        out = []
        for m in range(min(k, 9 - k)):
            here = d[m] if m < len(d) else None
            val = None
            if here is not None:
                val = across(here)
                if m > 0:
                    val = val + 0.2 * here
            if m + 1 < len(d):
                val = val + 0.2 * d[m + 1]
            if m > 0:
                below = 0.2 * d[m - 1]
                val = below if val is None else val + below
            if m == 0 and force is not None:
                val = force if val is None else val + force
            out.append(jnp.where(valid, val, 0.0))
        return out

    def early():
        across, valid = spread(56, -24)
        force = flat(plw[:, 0]) * flat(plw[:, 1])
        d = [force]
        for k in range(2, 5):
            d = layers(d, force, k, across, valid)
        d = [x[8:48] for x in d]
        c4w[...] = d[0].reshape(5, 8, DIP)
        across, valid = spread(40, -16)
        for k in range(5, 9):
            d = layers(d, None, k, across, valid)
        c8w[...] = d[0][8:32].reshape(3, 8, DIP)

    def ready(c):
        loads["f", c].wait()
        gb[c, pl.ds(O, HS)] = shuffle((fs[c] * st[...]).reshape(HS * HN, DIP), into[...]).reshape(HS, HN, DIP)
        loads["u", c].wait()
        xb[0, c, 0, pl.ds(O, HS), pl.ds(0, HN)] = shuffle(us[c].reshape(HS * HN, DIP), into[...]).reshape(HS, HN, DIP)

    for k in range(3):
        loads["small", k].wait()
    loads["ct"].wait()
    pk[...] = jnp.concatenate([small[0], small[1], ct_v[...].astype(F32), small[2]], axis=1)

    def unpack():
        @pl.when(is_i)
        def _():
            gath[n] = pk[...]
            pltpu.make_async_copy(gath.at[pl.ds(0, NN - 1)], gath.at[pl.ds(0, NN - 1)], g_rcv).wait()
            for big in range(NJ):
                tiles = [gath[big * 4 + m] for m in range(4)]
                for kind, place in enumerate((0, 2, 3, 4)):
                    val = None
                    for m in range(4):
                        shift = (m - kind) % 4 * 32
                        piece = pltpu.roll(tiles[m], shift, 1) if shift else tiles[m]
                        val = piece if val is None else jnp.where(lane >= 32 * m, piece, val)
                    plw[3, place, :, cols(big)] = val
            both = shuffle(jnp.concatenate([plw[3, 0], plw[3, 2], plw[3, 3], plw[3, 4]], axis=0), into[...])
            for m, place in enumerate((0, 2, 3, 4)):
                plw[3, place] = both[8 * m : 8 * m + 8]
            q_copy.wait_recv()
            plw[3, 1] = qx[0] + qx[1]
            plw[3, 5] = qx[0]
            send_all(w_copies)

    def total():
        @pl.when(is_i)
        def _():
            get_all(a_copies)
            for e in range(2):
                own = ra[0, 0, e] + ra[0, 1, e] + ra[0, 2, e]
                sw[2, e] = sign * (own - (ra[1, 0, e] + ra[1, 1, e] + ra[1, 2, e]))
            send_all(b_copies)

    def pressed():
        @pl.when(is_i)
        def _():
            get_all(w_copies)
            traction(lambda r: win_row(lambda j: plw[j, 0], r, 3), q_row)
            early()

    sign = jnp.where(is_b, 1.0, -1.0)

    def to_second(c):
        def store(i, low, high):
            xb[1, c, 0, O + i, 0:8, :] = low
            xb[1, c, 0, O + i, 8:16, :] = high

        return store

    def to_out(c):
        def store(i, low, high):
            outb[c, i, 0:8, :] = low
            outb[c, i, 8:16, :] = high

        return store

    def own_tile(get, put):
        @pl.when(is_a)
        def _():
            for i in range(HS):
                put(i, 8, get(i, 8) + jnp.where(r4sub, 0.0, pltpu.roll(corr[i], 4, 0)))

        @pl.when(is_b)
        def _():
            for i in range(HS):
                put(i, 0, get(i, 0) + jnp.where(r4sub, pltpu.roll(corr[i], 4, 0), 0.0))

    def put_second(i, r, v):
        xb[1, 1, 0, O + i, r : r + 8, :] = v

    def put_out(i, r, v):
        outb[1, i, r : r + 8, :] = v

    e4_copies = []
    for i in range(NN // 2):
        e4_copies.append(
            (
                jnp.logical_and(is_i, n != side * 8 + i),
                pltpu.make_async_remote_copy(
                    src_ref=e4s.at[i], dst_ref=e4r, send_sem=e4_snd.at[i], recv_sem=e4_rcv,
                    device_id=(s, side * 8 + i), device_id_type=MESH,
                ),
            )
        )

    def plane():
        @pl.when(is_i)
        def _():
            get_all(b_copies)
            p1 = lubricate(
                flat(sw[:, 0]) + flat(c4w[...]), *[flat(plw[1:6, kind]) for kind in (0, 2, 3, 4)], -16
            )
            p1w[...] = p1.reshape(5, 8, DIP)
            across, valid = spread(40, -16)
            force = p1 * flat(plw[1:6, 1])
            d = layers([force], force, 2, across, valid)
            d = layers(d, force, 6 + 1, across, valid)
            d = layers(d, force, 8, across, valid)
            opening = (flat(sw[1:4, 1]) + flat(c8w[...])) + d[0][8:32]
            p2 = lubricate(opening, p1[8:32], *[flat(plw[2:5, kind]) for kind in (2, 3, 4)], -8)
            p2 = shuffle(p2[8:16], back[...])
            for j in range(NJ):
                p2t[j] = p2[:, cols(j)]
            for i in range(NN // 2):
                shift = -(i % 4) * 32 % LANES
                tile = p2t[side * 2 + i // 4]
                e4s[i] = pltpu.roll(tile, shift, 1) if shift else tile
            for cond, copy in e4_copies:
                pl.when(cond)(copy.start)
            e4r[...] = e4s[jnp.where(is_b, 0, 7)]
            traction(lambda r: win_row(lambda j: p1w[j], r, 2), q_row)

    def start():
        ready(1)
        pl.semaphore_wait(barrier, count)
        for cond, copy in gathers:
            pl.when(cond)(copy.start)
        pl.when(is_i)(q_copy.start)

    def ahead():
        @pl.when(is_i)
        def _():
            antisymmetric()
            send_all(a_copies)

    def one(c):
        if c != 1:
            ready(c)
        sweeps(0, c)
        send(0, c)

    def two(c):
        merge(0, c, to_second(c))
        if c == 1:
            own_tile(lambda i, r: xb[1, 1, 0, O + i, r : r + 8, :], put_second)
        sweeps(1, c)
        send(1, c)

    def last(c):
        merge(1, c, to_out(c))
        if c == 1:
            own_tile(lambda i, r: outb[1, i, r : r + 8, :], put_out)
        u_out[c] = shuffle(outb[c].reshape(HS * HN, DIP), back[...]).reshape(HS, HN, DIP)

    start()
    ahead()
    one(0)
    one(2)
    unpack()
    one(1)
    total()
    two(0)
    two(2)
    pressed()
    two(1)
    plane()
    last(0)
    last(2)
    last(1)

    @pl.when(jnp.logical_not(is_i))
    def _():
        pltpu.make_async_remote_copy(
            src_ref=e4s.at[0], dst_ref=e4r, send_sem=e4_snd.at[0], recv_sem=e4_rcv,
            device_id=(s, NN - 1 - n), device_id_type=MESH,
        ).wait_recv()

    p_out[...] = e4r[...]

    for group in msgs.values():
        for cond, snd, _ in group:
            pl.when(cond)(snd.wait_send)
    for cond, copy in gathers:
        pl.when(cond)(copy.wait_send)
    for cond, copy in e4_copies:
        pl.when(cond)(copy.wait_send)

    @pl.when(is_i)
    def _():
        q_copy.wait_send()
        for copies in (a_copies, b_copies, w_copies):
            end_all(copies)


def body(displacement, body_force, stiffness, aperture_base, contact_open, pressure_init, injection):
    vm = pl.BlockSpec(memory_space=pltpu.VMEM)
    hbm = pl.BlockSpec(memory_space=pl.ANY)
    dma = pltpu.SemaphoreType.DMA

    def buf(*shape):
        return pltpu.VMEM(shape, F32)

    scratch = [
        buf(2, 3, 2, 18, 24, DIP),
        buf(3, 18, HN, DIP),
        buf(HS, HN, DIP),
        buf(3, HS, HN, DIP),
        buf(3, HS, HN, DIP),
        buf(3, HS, HN, DIP),
        pltpu.VMEM((3 * DIP, DIP), jnp.bfloat16),
        pltpu.VMEM((3 * DIP, DIP), jnp.bfloat16),
        buf(8, DIP),
        buf(2, 3, 2, 4, HN, DIP),
        buf(2, 3, 2, 4, 8, DIP),
        buf(2, 3, 2, 4, 8, DIP),
        buf(2, 3, 2, 2, 8, DIP),
        buf(2, 3, 2, 2, 8, DIP),
        buf(8, LANES),
        buf(NN, 8, LANES),
        buf(7, 6, 8, DIP),
        buf(2, 8, DIP),
        buf(2, 26, 8, DIP),
        buf(26, 8, DIP),
        buf(3, 2, 8, DIP),
        buf(2, 3, 2, 8, DIP),
        buf(5, 2, 8, DIP),
        buf(5, 8, DIP),
        buf(3, 8, DIP),
        buf(3, 8, 32),
        pltpu.VMEM((8, 32), jnp.int32),
        buf(14, 8, DIP),
        buf(2, 14, 8, DIP),
        buf(HS, 8, DIP),
        buf(5, 8, DIP),
        buf(NJ, 8, LANES),
        buf(NN // 2, 8, LANES),
        buf(8, LANES),
        dma((11,)),
        dma((2, 3, 2)), dma((2, 3, 2)), dma((2, 3, 2)), dma((2, 3, 2)),
        dma((2, 3, 2, 2)), dma((2, 3, 2, 2)),
        dma((2,)), dma,
        dma, dma, dma((7,)), dma((7,)), dma((2, 3)), dma((2, 3)), dma((5,)), dma((5,)),
        dma((NN // 2,)), dma,
    ]
    u, tile = pl.pallas_call(
        kernel,
        out_shape=(
            pltpu.VMEM((3, HS, HN, DIP), F32),
            pltpu.VMEM((8, LANES), F32),
        ),
        in_specs=[hbm] * 7,
        out_specs=(vm, vm),
        scratch_shapes=scratch,
        compiler_params=pltpu.CompilerParams(
            collective_id=0, has_side_effects=True, vmem_limit_bytes=60 * 2**20
        ),
        cost_estimate=pl.CostEstimate(flops=60_000_000, bytes_accessed=2_700_000, transcendentals=40_000),
    )(displacement, body_force, stiffness, aperture_base, contact_open, pressure_init, injection)
    return u, tile[:, : HN * 2]


def solution(mesh):
    in_specs = (
        P(None, "strike", "normal", None),
        P(None, "strike", "normal", None),
        P("strike", "normal", None),
        P("strike", "normal"),
        P("strike", "normal"),
        P("strike", "normal"),
        P("strike", "normal"),
    )
    out_specs = (P(None, "strike", "normal", None), P("strike", "normal"))
    return jax.shard_map(body, mesh=mesh, in_specs=in_specs, out_specs=out_specs, check_vma=False)
```
